128 devices in a mesh: tok: 16 (over y, x_lo, core), mdl: 8 (over x_hi, z).
Axes of the slice: x: 4 (x_hi: 2, x_lo: 2; x = x_hi * 2 + x_lo), y: 4, z: 4, core: 2. Of those that a mesh axis runs over, the one named last changes fastest.
Arguments:
- tokens: bfloat16 [12288, 2048], P('tok', 'mdl'), may hold values from -6 to 6
- segments: int32 [16, 768], P('tok'), may hold values from 0 to 5, never falling along the last dimension, each value on 1 to 576 neighbouring positions
- gain_attn: bfloat16 [2048], P('tok'), may hold values from 0.5 to 1.5
- w_query: bfloat16 [2048, 2048], P('tok', 'mdl'), may hold values from -2 to 2
- key_weight_matrix: bfloat16 [2048, 1024], P('tok', 'mdl'), may hold values from -2 to 2
- value_weight_matrix: bfloat16 [2048, 1024], P('tok', 'mdl'), may hold values from -0.125 to 0.125
- w_output: bfloat16 [2048, 2048], P('tok', 'mdl'), may hold values from -0.5 to 0.5
- gain_ffn: bfloat16 [2048], P('tok'), may hold values from 0.5 to 1.5
- w_gate: bfloat16 [2048, 8192], P('tok', 'mdl'), may hold values from -0.125 to 0.125
- w_up: bfloat16 [2048, 8192], P('tok', 'mdl'), may hold values from -0.125 to 0.125
- w_down: bfloat16 [2048, 8192], P('tok', 'mdl'), may hold values from -0.09375 to 0.09375
- cotangent: bfloat16 [12288, 2048], P('tok', 'mdl'), may hold values from -6 to 6
Outputs:
- output: bfloat16 [12288, 2048], P('tok', 'mdl')
- grad_input: float32 [12288, 2048], P('tok', 'mdl')
- grad_gain_attn: float32 [2048], P('tok')
- grad_w_query: float32 [2048, 2048], P('tok', 'mdl')
- grad_w_key: float32 [2048, 1024], P('tok', 'mdl')
- grad_w_value: float32 [2048, 1024], P('tok', 'mdl')
- grad_w_output: float32 [2048, 2048], P('tok', 'mdl')
- grad_gain_ffn: float32 [2048], P('tok')
- grad_w_gate: float32 [2048, 8192], P('tok', 'mdl')
- grad_w_up: float32 [2048, 8192], P('tok', 'mdl')
- grad_w_down: float32 [2048, 8192], P('tok', 'mdl')
- clipped_query: bfloat16 [2048, 2048], P('tok', 'mdl')
- clipped_key: bfloat16 [2048, 1024], P('tok', 'mdl')
The draws below stay inside these ranges and needn't reach their ends.
Inputs may be any that keep to these rules, and one draw needn't show every extreme that they name: `segments`: segment numbers never fall along a sequence; each of the 6 documents of a sequence has 1 to 576 tokens, and one has exactly that many.
All inputs are finite; a program needn't handle non-finite values.
Results may differ from the reference program's by a relative error of at most 0.025.
Values may be sent and summed in bfloat16 or wider, within the bound.
No kernel may reach another device: no remote copies, remote signals or barrier semaphores. Data moves between devices by JAX's collectives and lax.ppermute only.
A program may use at most 192 MiB of HBM per device.

```python
import math
import jax
import jax.numpy as jnp
import numpy as np
from jax import lax

MODEL_WIDTH = 2048
QUERY_HEADS = 8
KEY_VALUE_HEADS = 4
HEAD_WIDTH = 256
FF = 8192
LEN = 768
DOCS = 6
SEQS = 16
TOKENS = 12288


def head_levels(key, heads, upper):
    ranking = jax.random.permutation(key, heads)
    return jnp.where(ranking < heads // 2, 1.0, upper).astype(jnp.float32)


def draw_w_query(key, part):
    key = jax.random.fold_in(key, 11)
    levels = jnp.repeat(head_levels(jax.random.fold_in(key, 1), QUERY_HEADS, 1.3), HEAD_WIDTH)
    entry_key = jax.random.fold_in(key, 2)
    entries = jax.random.truncated_normal(entry_key, -6.0, 6.0, (MODEL_WIDTH, QUERY_HEADS * HEAD_WIDTH), jnp.float32)
    return (entries * levels[None, :] * MODEL_WIDTH ** (-0.5)).astype(jnp.bfloat16)


def draw_key_weight_matrix(key, part):
    key = jax.random.fold_in(key, 23)
    levels = jnp.repeat(head_levels(jax.random.fold_in(key, 1), KEY_VALUE_HEADS, 2.3), HEAD_WIDTH)
    entry_key = jax.random.fold_in(key, 2)
    entries = jax.random.truncated_normal(entry_key, -6.0, 6.0, (MODEL_WIDTH, KEY_VALUE_HEADS * HEAD_WIDTH), jnp.float32)
    return (entries * levels[None, :] * MODEL_WIDTH ** (-0.5)).astype(jnp.bfloat16)


def block_levels(key, dims, cuts, least, largest):
    factor_of, own = 1.0, jax.random.fold_in(key, 6)
    for axis_at, blocks in cuts:
        steps = jnp.exp(jax.random.uniform(jax.random.fold_in(own, axis_at), (blocks,), jnp.float32, least / len(cuts), largest / len(cuts)))
        factor_of = factor_of * jnp.repeat(steps, dims[axis_at] // blocks).reshape([-1 if axis == axis_at else 1 for axis in range(len(dims))])
    return factor_of


def length_profile(number_of, total, reach, lean):
    portions = [(1 << 20) // math.isqrt(standing ** lean) + 1 for standing in range(2, number_of + 1)]
    rest, given = total - reach - (number_of - 1), [1] * (number_of - 1)
    while rest > 0:
        candidates = [i for i in range(number_of - 1) if given[i] < reach]
        whole, left = sum([portions[i] for i in candidates]), rest
        for i in candidates:
            more = min(reach - given[i], max(1, left * portions[i] // whole), rest)
            given[i] = given[i] + more
            rest = rest - more
    return np.array([reach] + given)


def ragged(rng, number_of, total, limit, skew):
    if number_of == 2:
        one = jax.random.randint(rng, (), max(1, total - limit), min(limit, total - 1) + 1)
        return jnp.stack([one, total - one])
    tallies = jnp.asarray(length_profile(number_of, total, limit, skew), jnp.int32)
    couples = (number_of - 1) // 2
    source_of, taker = tallies[1:1 + 2 * couples:2], tallies[2:2 + 2 * couples:2]
    slack = jnp.minimum(source_of - 1, limit - taker)
    passed = jax.random.randint(jax.random.fold_in(rng, 1), (couples,), 0, 1 << 20) % (slack + 1)
    tallies = tallies.at[1:1 + 2 * couples:2].set(source_of - passed).at[2:2 + 2 * couples:2].set(taker + passed)
    return tallies[jax.random.permutation(jax.random.fold_in(rng, 2), number_of)]


def normal_values(rng, dims, deviation, bound, shards=(), held_as=jnp.bfloat16):
    level = block_levels(rng, dims, shards, -0.22, 0.18) if shards else 1.0
    result = jax.random.normal(rng, dims, jnp.float32) * deviation * level
    return jnp.minimum(jnp.maximum(result, -bound), bound).astype(held_as)


def setup_inputs(seed: int = 0) -> dict:
    arg_keys = jax.random.split(jax.random.key(seed), 13)
    tokens = normal_values(arg_keys[0], (TOKENS, MODEL_WIDTH), 1.0, 6.0, ((0, 16), (1, 8)))
    segments = jax.vmap(lambda own: jnp.searchsorted(jnp.cumsum(ragged(own, DOCS, LEN, LEN * 3 // 4, 1)), jnp.arange(LEN), side="right"))(jax.random.split(arg_keys[1], SEQS)).reshape((SEQS, LEN)).astype(jnp.int32)
    gain_attn = jnp.clip(1.0 + 0.1 * jax.random.normal(arg_keys[2], (MODEL_WIDTH,), jnp.float32), 0.5, 1.5).astype(jnp.bfloat16)
    w_query = draw_w_query(jax.random.fold_in(arg_keys[12], 71), 0)
    key_weight_matrix = draw_key_weight_matrix(jax.random.fold_in(arg_keys[12], 71), 0)
    value_weight_matrix = normal_values(arg_keys[5], (MODEL_WIDTH, KEY_VALUE_HEADS * HEAD_WIDTH), MODEL_WIDTH ** -0.5, 0.125, ((0, 16), (1, 8)))
    w_output = normal_values(arg_keys[6], (MODEL_WIDTH, QUERY_HEADS * HEAD_WIDTH), (QUERY_HEADS * HEAD_WIDTH // 16) ** -0.5, 0.5, ((0, 16), (1, 8)))
    gain_ffn = jnp.clip(1.0 + 0.1 * jax.random.normal(arg_keys[7], (MODEL_WIDTH,), jnp.float32), 0.5, 1.5).astype(jnp.bfloat16)
    w_gate = normal_values(arg_keys[8], (MODEL_WIDTH, FF), MODEL_WIDTH ** -0.5, 0.125, ((0, 16), (1, 8)))
    w_up = normal_values(arg_keys[9], (MODEL_WIDTH, FF), MODEL_WIDTH ** -0.5, 0.125, ((0, 16), (1, 8)))
    w_down = normal_values(arg_keys[10], (MODEL_WIDTH, FF), (FF // 2) ** -0.5, 0.09375, ((0, 16), (1, 8)))
    cotangent = normal_values(arg_keys[11], (TOKENS, MODEL_WIDTH), 1.0, 6.0, ((0, 16), (1, 8)))
    return {"tokens": tokens, "segments": segments, "gain_attn": gain_attn, "w_query": w_query, "key_weight_matrix": key_weight_matrix, "value_weight_matrix": value_weight_matrix, "w_output": w_output, "gain_ffn": gain_ffn, "w_gate": w_gate, "w_up": w_up, "w_down": w_down, "cotangent": cotangent}


norm_epsilon = 1e-06
rope_base = 1000042.0
logit_ceiling = 4.0
masked_value = -1e+30
peak_floor_epsilon = 1e-06

@jax.custom_vjp
def reduced_precision(v):
    return lax.optimization_barrier(v.astype(jnp.bfloat16)).astype(jnp.float32)

@jax.custom_vjp
def low_back(v):
    return v

def low_keep(v):
    return (reduced_precision(v), None)

def low_pass(kept, grad):
    return (grad,)

def back_keep(v):
    return (v, None)

def back_low(kept, grad):
    return (reduced_precision(grad),)
reduced_precision.defvjp(low_keep, low_pass)
low_back.defvjp(back_keep, back_low)

def rope_tables(segment_row, head_size):
    token_length = segment_row.shape[0]
    earlier = lax.optimization_barrier(jnp.sum((segment_row[None, :] < segment_row[:, None]).astype(jnp.int32), axis=1))
    places = jnp.arange(token_length, dtype=jnp.int32) - earlier
    half_size = head_size // 2
    inverse = jnp.exp(jnp.arange(half_size, dtype=jnp.float32) * (-2.0 * math.log(rope_base) / head_size))
    angles = places.astype(jnp.float32)[:, None] * inverse[None, :]
    return (jnp.cos(angles), jnp.sin(angles))

def apply_rotary_heads(values, cosine_lookup, sine_lookup, turn_sign):
    half_size = values.shape[-1] // 2
    shape_tail = (cosine_lookup.shape[0],) + (1,) * (values.ndim - 2) + (half_size,)
    cos_part = cosine_lookup.reshape(shape_tail)
    sin_part = sine_lookup.reshape(shape_tail) * turn_sign
    first_half = values[..., :half_size]
    second_half = values[..., half_size:]
    return jnp.concatenate([first_half * cos_part - second_half * sin_part, second_half * cos_part + first_half * sin_part], axis=-1)

def allowed_pairs(segment_row):
    index_row = jnp.arange(segment_row.shape[0], dtype=jnp.int32)
    return (segment_row[:, None] == segment_row[None, :]) & (index_row[:, None] >= index_row[None, :])

def forward_sequence(inputs, segment_row, gain_attn, w_query, key_weight_matrix, value_weight_matrix, w_output, gain_ffn, w_gate, w_up, w_down):
    token_length = inputs.shape[0]
    queries_per_group = QUERY_HEADS // KEY_VALUE_HEADS
    highest = lax.Precision.HIGHEST
    factor_attn = lax.rsqrt(lax.optimization_barrier(jnp.mean(inputs * inputs, axis=1, keepdims=True)) + norm_epsilon)
    normed_attn = reduced_precision(inputs * factor_attn * gain_attn)
    query_unrotated = low_back(jnp.dot(normed_attn, w_query, precision=highest))
    key_unrotated = low_back(jnp.dot(normed_attn, key_weight_matrix, precision=highest))
    value_reduced = reduced_precision(low_back(jnp.dot(normed_attn, value_weight_matrix, precision=highest)))
    cosine_lookup, sine_lookup = rope_tables(segment_row, HEAD_WIDTH)
    query_rotated = reduced_precision(apply_rotary_heads(query_unrotated.reshape(token_length, KEY_VALUE_HEADS, queries_per_group, HEAD_WIDTH), cosine_lookup, sine_lookup, 1.0))
    key_rotated = reduced_precision(apply_rotary_heads(key_unrotated.reshape(token_length, KEY_VALUE_HEADS, HEAD_WIDTH), cosine_lookup, sine_lookup, 1.0))
    value_head_rows = value_reduced.reshape(token_length, KEY_VALUE_HEADS, HEAD_WIDTH)
    allowed = allowed_pairs(segment_row)
    scores = low_back(jnp.einsum('qjgd,kjd->jgqk', query_rotated, key_rotated, precision=highest) * HEAD_WIDTH ** (-0.5))
    masked = jnp.where(allowed, scores, masked_value)
    probs = jax.nn.softmax(masked, axis=-1)
    attended = reduced_precision(low_back(jnp.einsum('jgqk,kjd->qjgd', reduced_precision(probs), value_head_rows, precision=highest)))
    peaks = lax.optimization_barrier(jnp.max(jnp.where(allowed, jnp.abs(scores), 0.0), axis=(2, 3))).reshape(QUERY_HEADS)
    attn_out = low_back(jnp.dot(attended.reshape(token_length, QUERY_HEADS * HEAD_WIDTH), w_output.T, precision=highest))
    hidden_res = inputs + attn_out
    factor_ffn = lax.rsqrt(lax.optimization_barrier(jnp.mean(hidden_res * hidden_res, axis=1, keepdims=True)) + norm_epsilon)
    normed_ffn = reduced_precision(hidden_res * factor_ffn * gain_ffn)
    gate_pre = low_back(jnp.dot(normed_ffn, w_gate, precision=highest))
    up_pre = low_back(jnp.dot(normed_ffn, w_up, precision=highest))
    hidden_units = reduced_precision(jax.nn.silu(gate_pre) * up_pre)
    output = hidden_res + jnp.dot(hidden_units, w_down.T, precision=highest)
    return (output, peaks)

def reference(tokens, segments, gain_attn, w_query, key_weight_matrix, value_weight_matrix, w_output, gain_ffn, w_gate, w_up, w_down, cotangent):
    weights = tuple((array_item.astype(jnp.float32) for array_item in (gain_attn, w_query, key_weight_matrix, value_weight_matrix, w_output, gain_ffn, w_gate, w_up, w_down)))
    inputs_all = tokens.astype(jnp.float32).reshape(SEQS, LEN, MODEL_WIDTH)
    upstream_all = cotangent.astype(jnp.float32).reshape(SEQS, LEN, MODEL_WIDTH)

    def per_sequence(totals, items):
        inputs, segment_row, upstream = items

        def apply(inputs_arg, *weight_args):
            return forward_sequence(inputs_arg, segment_row, *weight_args)
        output, pullback, peaks = jax.vjp(apply, inputs, *weights, has_aux=True)
        grads = pullback(upstream)
        totals = tuple((total_item + grad_item for total_item, grad_item in zip(totals, grads[1:])))
        return (totals, (output, grads[0], peaks))
    zero_grads = tuple((jnp.zeros(weight_item.shape, jnp.float32) for weight_item in weights))
    totals, (outputs, input_grads, peaks) = lax.scan(per_sequence, zero_grads, (inputs_all, segments, upstream_all))
    head_logit_peaks = lax.optimization_barrier(jnp.max(peaks, axis=0))
    scale_query = jnp.sqrt(logit_ceiling / (head_logit_peaks + peak_floor_epsilon))
    key_clip_scale = jnp.sqrt(logit_ceiling / (lax.optimization_barrier(jnp.max(head_logit_peaks.reshape(KEY_VALUE_HEADS, QUERY_HEADS // KEY_VALUE_HEADS), axis=1)) + peak_floor_epsilon))
    clipped_query = (weights[1] * jnp.repeat(scale_query, HEAD_WIDTH)[None, :]).astype(jnp.bfloat16)
    clipped_key = (weights[2] * jnp.repeat(key_clip_scale, HEAD_WIDTH)[None, :]).astype(jnp.bfloat16)
    return (outputs.reshape(TOKENS, MODEL_WIDTH).astype(jnp.bfloat16), input_grads.reshape(TOKENS, MODEL_WIDTH), totals[0], totals[1], totals[2], totals[3], totals[4], totals[5], totals[6], totals[7], totals[8], clipped_query, clipped_key)
```

```python
import functools
import math

import jax
import jax.numpy as jnp
from jax import lax
from jax.experimental import pallas as pl
from jax.experimental.pallas import tpu as pltpu
from jax.sharding import Mesh
from jax.sharding import PartitionSpec as P

QUERY_HEADS = 8
HEAD = 256
WIDTH = 2048
LEN = 768
OWN = 96
FF = 1024
Y, XLO, CORE, XHI, Z = "tok_0", "tok_1", "tok_2", "mdl_0", "mdl_1"
TOK = (Y, XLO, CORE)
MDL = (XHI, Z)

norm_epsilon = 1e-06
rope_base = 1000042.0
logit_ceiling = 4.0
masked_value = -1e30
peak_floor_epsilon = 1e-06
SCALE = HEAD ** (-0.5)
nt = (((1,), (1,)), ((), ()))
tn = (((0,), (0,)), ((), ()))
f32 = jnp.float32
bf16 = jnp.bfloat16


def dot(a, b, dims=(((1,), (0,)), ((), ()))):
    return lax.dot_general(a, b, dims, preferred_element_type=f32)


def swap(a):
    got = lax.ppermute(a, (CORE, XHI), [(1, 2), (2, 1)])
    return jnp.where(lax.axis_index(CORE) == lax.axis_index(XHI), a, got)


def other_core(a):
    return lax.ppermute(a, CORE, [(0, 1), (1, 0)])


def shift(a, axis, by):
    return lax.ppermute(a, axis, [(i, (i + by) % 4) for i in range(4)])


def z_other(a, mask):
    return lax.ppermute(a, Z, [(i, i ^ mask) for i in range(4)])


def y_other(a, mask):
    return lax.ppermute(a, Y, [(i, i ^ mask) for i in range(4)])


def kv_partner(a):
    return lax.ppermute(a, Z, [(0, 1), (1, 0), (2, 3), (3, 2)])


def plane_pairs(flip_lo, flip_core):
    pairs = []
    for lo in range(2):
        for core in range(2):
            for hi in range(2):
                pairs.append((lo * 4 + core * 2 + hi, (lo ^ flip_lo) * 4 + hi * 2 + (core ^ flip_core)))
    return pairs


def x_pairs(flip_lo, flip_core, back):
    pairs = plane_pairs(flip_lo, flip_core)
    return [(there, here) if back else (here, there) for here, there in pairs if here != there]


def x_in(a, flip_lo, flip_core):
    return lax.ppermute(a, (XLO, CORE, XHI), x_pairs(flip_lo, flip_core, False))


def x_out(a, flip_lo, flip_core):
    return lax.ppermute(a, (XLO, CORE, XHI), x_pairs(flip_lo, flip_core, True))


def own_or(got, own):
    return jnp.where(lax.axis_index(CORE) == lax.axis_index(XHI), own, got)


FLIPS = ((0, 0), (0, 1), (1, 0), (1, 1))


def from_y(a):
    return [a, shift(a, Y, -1), shift(a, Y, 2), shift(a, Y, 1)]


def from_z(a):
    return [a, shift(a, Z, -1), shift(a, Z, 2), shift(a, Z, 1)]


def x_ring(a, mask):
    return lax.ppermute(a, (XLO, XHI), [(i, i ^ mask) for i in range(4)])


def total(pieces, cols=slice(None)):
    return sum(piece[:, cols].astype(f32) for piece in pieces)


def team_gather(own):
    return lax.all_gather(own, (CORE, Z), axis=0, tiled=True)


def team_scatter(give, keep):
    both = (keep.astype(f32) + other_core(give).astype(f32)).astype(bf16)
    return lax.psum_scatter(both, Z, scatter_dimension=0, tiled=True).astype(f32)


def after(value, *others):
    return lax.optimization_barrier((value, *others))[0]


def rope_tables(segment_row):
    earlier = jnp.sum((segment_row[None, :] < segment_row[:, None]).astype(jnp.int32), axis=1)
    places = jnp.arange(LEN, dtype=jnp.int32) - earlier
    half = HEAD // 2
    inverse = jnp.exp(jnp.arange(half, dtype=f32) * (-2.0 * math.log(rope_base) / HEAD))
    angles = places.astype(f32)[:, None] * inverse[None, :]
    return jnp.cos(angles), jnp.sin(angles)


def position(r, at):
    return (((r >> 2) - at[0]) & 3) * 4 + (((r >> 1) & 1) ^ at[1]) * 2 + ((r & 1) ^ at[2])


def lanes(index, size):
    return pl.ds(pl.multiple_of(index * size, size), size)


def owner(at, there, dz):
    return (at[3] ^ there) * 4 + ((at[4] + dz) & 3)


def kdot(a, b, dims=(((1,), (0,)), ((), ()))):
    return lax.dot_general(a, b, dims, preferred_element_type=f32)


def in_vmem(n):
    return [pl.BlockSpec(memory_space=pltpu.VMEM)] * n


def call(body, name, inputs, outs, scratch, flops, megabytes=56, anywhere=0):
    moved = sum(v.size * v.dtype.itemsize for v in inputs[1:])
    moved += sum(math.prod(s) * jnp.dtype(d).itemsize for s, d in outs)
    specs = [pl.BlockSpec(memory_space=pltpu.SMEM)] + in_vmem(len(inputs) - 1 - anywhere)
    specs += [pl.BlockSpec(memory_space=pl.ANY)] * anywhere
    return list(pl.pallas_call(
        body,
        name=name,
        out_shape=[jax.ShapeDtypeStruct(s, d) for s, d in outs],
        in_specs=specs,
        out_specs=in_vmem(len(outs)),
        scratch_shapes=scratch,
        cost_estimate=pl.CostEstimate(flops=int(flops), bytes_accessed=int(moved), transcendentals=0),
        compiler_params=pltpu.CompilerParams(vmem_limit_bytes=megabytes * 2**20),
    )(*inputs))


def turn(values, cosine, sine):
    first, second = values[:, :128], values[:, 128:]
    return first * cosine - second * sine, second * cosine + first * sine


def attention_weights(a_refs, b_refs, w_qkv, w_o, sem):
    copies = []

    def move(source, to):
        copies.append(pltpu.make_async_copy(source, to, sem.at[len(copies)]))
        copies[-1].start()

    for i in range(4):
        for dy in range(4):
            rows = pl.ds((dy * 4 + i) * 128, 128)
            move(b_refs[i].at[pl.ds(dy * 144, 128), pl.ds(256, 256)], w_o.at[rows])
    for dy in range(4):
        for i in range(4):
            rows = pl.ds((dy * 4 + i) * 128, 128)
            move(b_refs[i].at[pl.ds(dy * 144, 128), pl.ds(0, 256)], w_qkv.at[rows, pl.ds(0, 256)])
            move(a_refs[dy].at[pl.ds(i * 128, 128)], w_qkv.at[rows, pl.ds(256, 512)])
    return copies


def pack_body(at, *refs):
    xs, ys, to_y, to_x, sem = refs[:4], refs[4:8], refs[8], refs[9], refs[10]
    pairs = [(ref.at[pl.ds(0, 128)], to_y.at[pl.ds(128 * i, 128)]) for i, ref in enumerate(xs)]
    pairs += [(ref.at[pl.ds(0, 144)], to_x.at[pl.ds(144 * i, 144)]) for i, ref in enumerate(ys)]
    copies = [pltpu.make_async_copy(a, b, sem.at[i]) for i, (a, b) in enumerate(pairs)]
    for copy in copies:
        copy.start()
    for copy in copies:
        copy.wait()


def riders_body(at, *refs):
    xs, ys = refs[:4], refs[4:8]
    a_wide, b_wide, a_down, b_down, sem = refs[8:]
    copies = []
    for ref, row, wide, down in [(xs, 128, a_wide, a_down), (ys, 144, b_wide, b_down)]:
        for i in range(4):
            for j in range(3):
                source = ref[i].at[pl.ds(row + j * 128, 128)]
                rows = pl.ds(i * 128, 128)
                to = down.at[rows] if j == 2 else wide.at[rows, pl.ds(j * 512, 512)]
                copies.append(pltpu.make_async_copy(source, to, sem.at[len(copies)]))
    for copy in copies:
        copy.start()
    for copy in copies:
        copy.wait()


def allowed_block(i, seg_col, seg_row):
    rows, cols = 256, (i + 1) * 256
    same = seg_col[i * 256 : (i + 1) * 256, :] == seg_row[:, :cols]
    row = i * 256 + lax.broadcasted_iota(jnp.int32, (rows, cols), 0)
    return same & (row >= lax.broadcasted_iota(jnp.int32, (rows, cols), 1))


def forward_body(at, *refs):
    x, cosine, sine, seg_row, seg_col = refs[:5]
    a_refs, b_refs = refs[5:9], refs[9:13]
    a1, r1, x_mine, qr, kr, v, o, lse, peak, gains, give, keep = refs[13:25]
    w_qkv, w_o, gain_rows, sem, gain_sem = refs[25:]
    gain_copies = []
    for dy in range(4):
        for i in range(4):
            source = b_refs[i].at[pl.ds(dy * 144 + 128, 16), pl.ds(0, 128)]
            to = gain_rows.at[:, pl.ds((dy * 4 + i) * 128, 128)]
            gain_copies.append(pltpu.make_async_copy(source, to, gain_sem.at[len(gain_copies)]))
            gain_copies[-1].start()
    copies = attention_weights(a_refs, b_refs, w_qkv, w_o, sem)
    for copy in gain_copies:
        copy.wait()
    gains[...] = gain_rows[...].astype(f32)[:8]
    own = at[3] * 4 + at[4]
    for r in range(16):
        rows = pl.ds(pl.multiple_of((r // 2) * LEN + own * OWN, OWN), OWN)
        x_mine[:, lanes(position(r, at), 128)] = x[rows, (r % 2) * 128 : (r % 2 + 1) * 128]

    def norm(step, carry):
        rows = pl.ds(pl.multiple_of(step * 128, 128), 128)
        total = jnp.zeros((128, 1), f32)
        for m in range(8):
            value = x[pl.ds(pl.multiple_of(m * LEN + step * 128, 128), 128), :].astype(f32)
            total = total + jnp.sum(value * value, axis=1, keepdims=True)
        factor = lax.rsqrt(total / WIDTH + norm_epsilon)
        r1[rows, :] = factor
        for r in range(16):
            at_lanes = lanes(position(r, at), 128)
            from_rows = pl.ds(pl.multiple_of((r // 2) * LEN + step * 128, 128), 128)
            value = x[from_rows, (r % 2) * 128 : (r % 2 + 1) * 128].astype(f32)
            a1[rows, at_lanes] = (value * factor * gains[0:1, at_lanes]).astype(bf16)
        return carry

    lax.fori_loop(0, 6, norm, 0)
    for copy in copies:
        copy.wait()
    for i in range(3):
        rows = slice(i * 256, (i + 1) * 256)
        qk = kdot(a1[rows, :], w_qkv[:, :512])
        cos_i, sin_i = cosine[rows, :], sine[rows, :]
        for ref, at_col in ((qr, 0), (kr, 256)):
            one, two = turn(qk[:, at_col : at_col + 256], cos_i, sin_i)
            ref[rows, :128] = one.astype(bf16)
            ref[rows, 128:] = two.astype(bf16)
        v[rows, :] = kdot(a1[rows, :], w_qkv[:, 512:]).astype(bf16)
    largest = jnp.zeros((1, 1), f32)
    for i in range(3):
        rows, cols = slice(i * 256, (i + 1) * 256), (i + 1) * 256
        allowed = allowed_block(i, seg_col, seg_row)
        scores = kdot(qr[rows, :], kr[:cols, :], nt) * SCALE
        masked = jnp.where(allowed, scores, masked_value)
        size = jnp.where(allowed, jnp.abs(scores), 0.0)
        largest = jnp.maximum(largest, jnp.max(jnp.max(size, axis=1, keepdims=True), axis=0, keepdims=True))
        top = jnp.max(masked, axis=1, keepdims=True)
        log_total = top + jnp.log(jnp.sum(jnp.exp(masked - top), axis=1, keepdims=True))
        lse[rows, :] = log_total
        probs = jnp.exp(masked - log_total).astype(bf16)
        o[rows, :] = kdot(probs, v[:cols, :]).astype(bf16)
    peak[...] = jnp.broadcast_to(largest, (8, 128))
    for ref, c in ((give, 1 - at[3]), (keep, at[3])):
        rows = pl.ds(pl.multiple_of(c * 384, 384), 384)
        for half in range(2):
            cols = slice(half * 1024, (half + 1) * 1024)
            ref[:, cols] = kdot(o[rows, :], w_o[cols, :], nt).astype(bf16)


def reorder_body(at, whole, out):
    for r in range(16):
        rows = slice((r // 2) * LEN, (r // 2 + 1) * LEN)
        out[:, lanes(position(r, at), 128)] = whole[rows, (r % 2) * 128 : (r % 2 + 1) * 128]


def start_either(at, own, got, to, sem):
    mine = at[2] == at[3]

    @pl.when(mine)
    def _():
        pltpu.make_async_copy(own, to, sem).start()

    @pl.when(jnp.logical_not(mine))
    def _():
        pltpu.make_async_copy(got, to, sem).start()

    return pltpu.make_async_copy(got, to, sem)


def rows_a(refs, to_ref, cols, sem, copies):
    for i, ref in enumerate(refs):
        to = to_ref.at[pl.ds(i * 512, 512), cols]
        copies.append(pltpu.make_async_copy(ref, to, sem.at[len(copies)]))
        copies[-1].start()


def rows_b(at, own, refs, to_ref, cols, sem, copies):
    for i, ref in enumerate(refs):
        for j in range(4):
            to = to_ref.at[pl.ds((j * 4 + i) * 128, 128), cols]
            rows = pl.ds(j * 128, 128)
            if i == 0:
                copies.append(start_either(at, own.at[rows], ref.at[rows], to, sem.at[len(copies)]))
            else:
                copies.append(pltpu.make_async_copy(ref.at[rows], to, sem.at[len(copies)]))
                copies[-1].start()


def ffn_body(at, *refs):
    h, gains, dy = refs[:3]
    wide_a, down_a, wide_b, down_b = [refs[3 + 4 * i : 7 + 4 * i] for i in range(4)]
    own_wide, own_down = refs[19:21]
    a2, hid, dgate, dup, h_cols, give, keep = refs[21:28]
    w_gate, w_up, w_down, sem = refs[28:]
    copies = []
    rows_a(wide_a, w_gate, pl.ds(0, FF), sem, copies)
    rows_b(at, own_wide, wide_b, w_up, pl.ds(0, FF), sem, copies)
    rows_a(down_a, w_down, pl.ds(0, 512), sem, copies)
    rows_b(at, own_down, down_b, w_down, pl.ds(512, 512), sem, copies)
    own = at[3] * 4 + at[4]
    for j in range(2):
        h_cols[:, j * 128 : (j + 1) * 128] = h[:, lanes(position(2 * own + j, at), 128)]
    for i in range(6):
        rows = slice(i * 128, (i + 1) * 128)
        value = h[rows, :].astype(f32)
        factor = lax.rsqrt(jnp.mean(value * value, axis=1, keepdims=True) + norm_epsilon)
        a2[rows, :] = (value * factor * gains[1:2, :]).astype(bf16)
    for copy in copies:
        copy.wait()
    for half in range(2):
        rows = slice(half * 384, (half + 1) * 384)
        for j in range(4):
            cols = slice(j * 256, (j + 1) * 256)
            gate = kdot(a2[rows, :], w_gate[:, cols])
            up = kdot(a2[rows, :], w_up[:, cols])
            grad = kdot(dy[rows, :], w_down[:, cols])
            sig = 1.0 / (1.0 + jnp.exp(-gate))
            act = gate * sig
            hid[rows, cols] = (act * up).astype(bf16)
            dgate[rows, cols] = (grad * up * sig * (1.0 + gate * (1.0 - sig))).astype(bf16)
            dup[rows, cols] = (grad * act).astype(bf16)
    for ref, c in ((give, 1 - at[3]), (keep, at[3])):
        rows = pl.ds(pl.multiple_of(c * 384, 384), 384)
        for j in range(4):
            cols = slice(j * 512, (j + 1) * 512)
            ref[:, cols] = (
                kdot(dgate[rows, :], w_gate[cols, :], nt) + kdot(dup[rows, :], w_up[cols, :], nt)
            ).astype(bf16)


def ffn_out_body(at, hid, *refs):
    down_a, down_b, own_down = refs[:4], refs[4:8], refs[8]
    give, keep, w_down, sem = refs[9:]
    copies = []
    rows_a(down_a, w_down, pl.ds(0, 512), sem, copies)
    rows_b(at, own_down, down_b, w_down, pl.ds(512, 512), sem, copies)
    for copy in copies:
        copy.wait()
    for ref, c in ((give, 1 - at[3]), (keep, at[3])):
        for dz in range(4):
            m = c * 4 + dz
            pair = pl.ds(pl.multiple_of((position(2 * m, at) >> 1) * 256, 256), 256)
            value = kdot(hid[...], w_down[pair, :], nt)
            rows = slice(dz * LEN, (dz + 1) * LEN)
            for j in range(2):
                ref[rows, lanes(at[2] ^ j, 128)] = value[:, j * 128 : (j + 1) * 128].astype(bf16)


def weight_gate_body(blocks, at, a2, dgate, *outs):
    for i, out in zip(blocks, outs):
        for j in range(2):
            n = slice(j * 512, (j + 1) * 512)
            out[:, n] = kdot(a2[:, i * 512 : (i + 1) * 512], dgate[:, n], tn).astype(bf16)


def weight_up_body(first, at, a2, dup, *outs):
    for i in range(4):
        cols = slice((i * 4 + first) * 128, (i * 4 + first + 2) * 128)
        for j in range(2):
            n = slice(j * 512, (j + 1) * 512)
            value = kdot(a2[:, cols], dup[:, n], tn).astype(bf16)
            for k in range(2):
                outs[k][i * 128 : (i + 1) * 128, n] = value[k * 128 : (k + 1) * 128]


def weight_rest_body(at, a2, dy, dgate, dup, hid, *outs):
    a_wide, b_wide, a_down, b_down = outs[:2], outs[2:4], outs[4:8], outs[8:]
    for i in range(4):
        cols, rows = slice(i * 512, (i + 1) * 512), slice(i * 128, (i + 1) * 128)
        for j in range(2):
            n = slice(j * 512, (j + 1) * 512)
            value = kdot(a2[:, i * 512 : i * 512 + 256], dup[:, n], tn).astype(bf16)
            for k in range(2):
                b_wide[k][rows, n] = value[k * 128 : (k + 1) * 128]
            if i % 2 == 0:
                a_wide[i // 2][:, n] = kdot(a2[:, cols], dgate[:, n], tn).astype(bf16)
        a_down[i][...] = kdot(dy[:, cols], hid[:, :512], tn).astype(bf16)
        value = kdot(dy[:, cols], hid[:, 512:], tn).astype(bf16)
        for k in range(4):
            b_down[k][rows, :] = value[k * 128 : (k + 1) * 128]


def backward_body(at, *refs):
    db, cosine, sine, seg_row, seg_col, qr, kr, v, lse, a1, gains = refs[:11]
    a_refs, b_refs = refs[11:15], refs[15:19]
    db_cols, dqkv, row_part, gain_part, give, keep = refs[19:25]
    w_qkv, w_o, d_o, dk_sum, dv_sum, sem = refs[25:]
    copies = attention_weights(a_refs, b_refs, w_qkv, w_o, sem)
    own = at[3] * 4 + at[4]
    for j in range(2):
        db_cols[:, j * 128 : (j + 1) * 128] = db[:, lanes(position(2 * own + j, at), 128)]
    for copy in copies:
        copy.wait()
    for i in range(3):
        rows = slice(i * 256, (i + 1) * 256)
        d_o[rows, :] = kdot(db[rows, :], w_o[...]).astype(bf16)
    for i in (2, 1, 0):
        rows, cols = slice(i * 256, (i + 1) * 256), (i + 1) * 256
        allowed = allowed_block(i, seg_col, seg_row)
        scores = kdot(qr[rows, :], kr[:cols, :], nt) * SCALE
        probs = jnp.exp(jnp.where(allowed, scores, masked_value) - lse[rows, :])
        low = probs.astype(bf16)
        dp = kdot(d_o[rows, :], v[:cols, :], nt)
        delta = jnp.sum(dp * probs, axis=1, keepdims=True)
        ds = (probs * (dp - delta)).astype(bf16)
        dq = kdot(ds, kr[:cols, :]) * SCALE
        row_part[rows, :] = jnp.sum(dq * qr[rows, :].astype(f32), axis=1, keepdims=True)
        one, two = turn(dq, cosine[rows, :], -sine[rows, :])
        dqkv[rows, :128] = one.astype(bf16)
        dqkv[rows, 128:256] = two.astype(bf16)
        dk_new = kdot(ds, qr[rows, :], tn)
        dv_new = kdot(low, d_o[rows, :], tn)
        if i == 2:
            dk_sum[...] = dk_new
            dv_sum[...] = dv_new
        else:
            dk_sum[:cols, :] = dk_sum[:cols, :] + dk_new
            dv_sum[:cols, :] = dv_sum[:cols, :] + dv_new
    for i in range(3):
        rows = slice(i * 256, (i + 1) * 256)
        dk = dk_sum[rows, :] * SCALE
        dv_i = dv_sum[rows, :]
        row_part[rows, :] = (
            row_part[rows, :]
            + jnp.sum(dk * kr[rows, :].astype(f32), axis=1, keepdims=True)
            + jnp.sum(dv_i * v[rows, :].astype(f32), axis=1, keepdims=True)
        )
        one, two = turn(dk, cosine[rows, :], -sine[rows, :])
        dqkv[rows, 256:384] = one.astype(bf16)
        dqkv[rows, 384:512] = two.astype(bf16)
        dqkv[rows, 512:] = dv_i.astype(bf16)
    for m, ref in [(j, give) for j in range(4)] + [(j, keep) for j in range(4)]:
        half = 1 - at[3] if ref is give else at[3]
        pair = lanes(position(2 * (half * 4 + m), at) >> 1, 256)
        value = kdot(dqkv[...], w_qkv[pair, :], nt)
        gain_part[:, pair] = jnp.sum(value * a1[:, pair].astype(f32), axis=0, keepdims=True) / gains[0:1, pair]
        rows = slice(m * LEN, (m + 1) * LEN)
        for j in range(2):
            ref[rows, lanes(at[2] ^ j, 128)] = value[:, j * 128 : (j + 1) * 128].astype(bf16)


def attention_weight_body(at, a1, dqkv, db, o, *outs):
    a_outs, b_outs = outs[:4], outs[4:]
    for i in range(4):
        cols, rows = slice(i * 512, (i + 1) * 512), slice(i * 128, (i + 1) * 128)
        a_outs[i][...] = kdot(a1[:, cols], dqkv[:, 256:], tn).astype(bf16)
        for n, left, right in ((slice(0, 256), a1, dqkv.at[:, :256]), (slice(256, 512), db, o)):
            value = kdot(left[:, cols], right[...], tn).astype(bf16)
            for k in range(4):
                b_outs[k][rows, n] = value[k * 128 : (k + 1) * 128]


def ffn_sum_body(at, *refs):
    wide_a, down_a, wide_b, down_b = [refs[4 * i : 4 * i + 4] for i in range(4)]
    own_wide, own_down, out_a, out_b = refs[16:]
    mine = at[2] == at[3]
    for cols, a, b, own in ((slice(0, FF), wide_a, wide_b, own_wide), (slice(FF, 1536), down_a, down_b, own_down)):
        value = a[0][...].astype(f32) + a[1][...].astype(f32) + a[2][...].astype(f32) + a[3][...].astype(f32)
        out_a[:, cols] = value.astype(bf16)
        value = jnp.where(mine, own[...], b[0][...]).astype(f32) + b[1][...].astype(f32)
        value = value + b[2][...].astype(f32) + b[3][...].astype(f32)
        out_b[:, cols] = value.astype(bf16)


def join_body(at, *refs):
    ffn_a, ffn_b, a, b, own, outs = refs[0], refs[1], refs[2:6], refs[6:10], refs[10], refs[11:]
    for i in range(4):
        rows = slice(i * 128, (i + 1) * 128)
        outs[i][:, :1536] = ffn_a[rows, :]
        outs[4 + i][:, :1536] = ffn_b[rows, :]
        value = a[0][rows, :].astype(f32) + a[1][rows, :].astype(f32) + a[2][rows, :].astype(f32)
        outs[i][:, 1536:] = (value + a[3][rows, :].astype(f32)).astype(bf16)
        head = jnp.where(at[2] == at[3], own[rows, :], b[0][rows, :])
        value = head.astype(f32) + b[1][rows, :].astype(f32) + b[2][rows, :].astype(f32)
        outs[4 + i][:, 1536:] = (value + b[3][rows, :].astype(f32)).astype(bf16)


def finish_body(at, *refs):
    own, a, b = refs[0], refs[1:5], refs[5:9]
    gate, up, down, query, output = refs[9:]
    mine = at[2] == at[3]

    def sum_a(cols):
        head = jnp.where(mine, own[:, cols], a[0][:, cols])
        return head.astype(f32) + a[1][:, cols].astype(f32) + a[2][:, cols].astype(f32) + a[3][:, cols].astype(f32)

    def sum_b(cols):
        return b[0][:, cols].astype(f32) + b[1][:, cols].astype(f32) + b[2][:, cols].astype(f32) + b[3][:, cols].astype(f32)

    for j in range(4):
        cols = slice(j * 256, (j + 1) * 256)
        gate[:, cols] = sum_a(cols)
        up[:, cols] = sum_b(cols)
    for j in range(2):
        cols = slice(FF + j * 256, FF + (j + 1) * 256)
        down[:, j * 256 : (j + 1) * 256] = sum_a(cols)
        down[:, 512 + j * 256 : 512 + (j + 1) * 256] = sum_b(cols)
    query[...] = sum_b(slice(1536, 1792))
    output[...] = sum_b(slice(1792, 2048))


def on_device(
    tokens,
    segments,
    gain_attn,
    w_query,
    w_key,
    w_value,
    w_output,
    gain_ffn,
    w_gate,
    w_up,
    w_down,
    cotangent,
):
    y, lo, core = lax.axis_index(Y), lax.axis_index(XLO), lax.axis_index(CORE)
    hi, z = lax.axis_index(XHI), lax.axis_index(Z)
    at = jnp.stack([y, lo, hi, core, z]).astype(jnp.int32)
    mine = core * 4 + z

    riders = jnp.zeros((16, HEAD), bf16).at[:3].set(segments.reshape(3, HEAD).astype(bf16))
    gains = jnp.zeros((16, 2 * HEAD), bf16)
    gains = gains.at[0, :128].set(gain_attn).at[1, :128].set(gain_ffn)
    hf = FF // 2
    kv_own = jnp.concatenate([w_key, w_value], 1)
    kv_other = kv_partner(kv_own)
    got = swap(jnp.concatenate([tokens, riders, cotangent], 0))
    along_y = jnp.concatenate([w_query, w_output], 1)
    along_y = from_y(jnp.concatenate([along_y, gains, w_up[:, :hf], w_up[:, hf:], w_down[:, hf:]], 0))
    odd = z % 2 == 1
    half = HEAD // 2
    low_kv, high_kv = jnp.where(odd, kv_other, kv_own), jnp.where(odd, kv_own, kv_other)
    along_x = jnp.concatenate([low_kv[:, :half], high_kv[:, :half], low_kv[:, half:], high_kv[:, half:]], 1)
    along_x = jnp.concatenate([along_x, w_gate[:, :hf], w_gate[:, hf:], w_down[:, :hf]], 0)
    along_x = [own_or(x_in(along_x, 0, 0), along_x)] + [x_in(along_x, *flip) for flip in FLIPS[1:]]
    got, *rest = lax.optimization_barrier((got, *along_x, *along_y))
    to_y, to_x = call(
        pack_body,
        "pack",
        [at, *rest],
        [((512, 2 * HEAD), bf16), ((576, 2 * HEAD), bf16)],
        [pltpu.SemaphoreType.DMA((8,))],
        0,
        anywhere=8,
    )
    a_wide, b_wide, a_down, b_down = call(
        riders_body,
        "riders",
        [at, *rest],
        [((512, FF), bf16)] * 2 + [((512, hf), bf16)] * 2,
        [pltpu.SemaphoreType.DMA((24,))],
        0,
        anywhere=8,
    )
    x_own = got[:LEN]
    x_all = team_gather(x_own)
    upstream = team_gather(after(got[784:1552], to_x))
    segment_row = got[LEN : LEN + 3].astype(f32).reshape(1, LEN)
    segment_col = segment_row.reshape(LEN, 1)
    cosine, sine = rope_tables(segment_row[0])
    first = [shift(to_y, Y, -1), shift(to_y, Y, 1)]
    second = [x_in(to_x, *flip) for flip in FLIPS[2:]]
    late_y, late_x, *rest = lax.optimization_barrier((to_y, to_x, *first, *second))
    first, second = rest[:2], rest[2:]
    first = [to_y, first[0], shift(late_y, Y, 2), first[1]]
    second = [own_or(x_in(late_x, 0, 0), to_x), x_in(late_x, *FLIPS[1])] + second
    x_all, cosine, sine, segment_row, segment_col, *rest = lax.optimization_barrier(
        (x_all, cosine, sine, segment_row, segment_col, *first, *second, a_wide, b_wide, a_down, b_down)
    )
    first, second, (a_wide, b_wide, a_down, b_down) = rest[:4], rest[4:8], rest[8:]
    wide_a = [shift(a_wide, Y, -1), shift(a_wide, Y, 1)]
    wide_b = [x_in(b_wide, *flip) for flip in FLIPS[2:]]

    part = ((LEN // 2, WIDTH), bf16)
    act, low, col = ((LEN, WIDTH), bf16), ((LEN, HEAD), bf16), ((LEN, 1), f32)
    a1, r1, x_mine, qr, kr, v, o, lse, peak, gain_rows, give, keep = call(
        forward_body,
        "attention_forward",
        [at, x_all, cosine, sine, segment_row, segment_col, *first, *second],
        [act, col, ((OWN, WIDTH), bf16), low, low, low, low, col, ((8, 128), f32), ((8, WIDTH), f32), part, part],
        [
            pltpu.VMEM((WIDTH, 3 * HEAD), bf16),
            pltpu.VMEM((WIDTH, HEAD), bf16),
            pltpu.VMEM((16, WIDTH), bf16),
            pltpu.SemaphoreType.DMA((48,)),
            pltpu.SemaphoreType.DMA((16,)),
        ],
        2 * LEN * WIDTH * 1024,
        anywhere=8,
    )
    give, keep, upstream, *done = lax.optimization_barrier(
        (give, keep, upstream, *wide_a, *wide_b, a_wide, b_wide, a_down, b_down)
    )
    wide_a, wide_b, (a_wide, b_wide, a_down, b_down) = done[:2], done[2:4], done[4:]
    attn_own = team_scatter(give, keep)
    wide_a = [a_wide, wide_a[0], shift(a_wide, Y, 2), wide_a[1]]
    wide_b = [x_in(b_wide, *flip) for flip in FLIPS[:2]] + wide_b
    down_a = [shift(a_down, Y, -1), shift(a_down, Y, 1)]
    (dy,) = call(reorder_body, "order_upstream", [at, upstream], [((LEN, WIDTH), bf16)], [], 0)


    attn_own, dy, *done = lax.optimization_barrier((attn_own, dy, *wide_a, *wide_b, *down_a, b_wide, a_down, b_down))
    wide_a, wide_b, down_a, (b_wide, a_down, b_down) = done[:4], done[4:8], done[8:10], done[10:]
    down_b = [x_in(b_down, *flip) for flip in FLIPS]
    down_a = [a_down, down_a[0], shift(a_down, Y, 2), down_a[1]]
    hidden_own = x_mine.astype(f32) + attn_own
    hidden = team_gather(hidden_own.astype(bf16))
    wide = ((LEN, FF), bf16)
    a2, hid, dgate, dup, h_cols, give, keep = call(
        ffn_body,
        "feed_forward",
        [at, hidden, gain_rows, dy, *wide_a, *down_a, *wide_b, *down_b, b_wide, b_down],
        [act, wide, wide, wide, low, part, part],
        [
            pltpu.VMEM((WIDTH, FF), bf16),
            pltpu.VMEM((WIDTH, FF), bf16),
            pltpu.VMEM((WIDTH, FF), bf16),
            pltpu.SemaphoreType.DMA((40,)),
        ],
        10 * LEN * WIDTH * FF,
        anywhere=18,
    )
    other = other_core(give)
    wide_out, stack = ((512, FF), bf16), ((4 * LEN, HEAD), bf16)
    work = 2 * LEN * WIDTH * FF
    up_a = call(functools.partial(weight_up_body, 2), "weight_up_first", [at, a2, dup], [wide_out] * 2, [], work / 2)
    keep, other, *up_a = lax.optimization_barrier((keep, other, *up_a))
    both = (keep.astype(f32) + other.astype(f32)).astype(bf16)
    normed_grad = lax.psum_scatter(both, Z, scatter_dimension=0, tiled=True).astype(f32)
    dgate, dup, hid = lax.optimization_barrier((dgate, dup, hid, both))[:3]
    gate_a = call(
        functools.partial(weight_gate_body, (1, 3)), "weight_gate_first", [at, a2, dgate], [wide_out] * 2, [], work / 2
    )
    got_up = [x_out(block, *flip) for block, flip in zip(up_a, FLIPS[2:])]
    got_gate = [shift(gate_a[0], Y, 1), shift(gate_a[1], Y, 3)]
    rest = call(
        weight_rest_body,
        "weight_rest",
        [at, a2, dy, after(dgate, gate_a[0]), dup, hid],
        [wide_out] * 4 + [((512, hf), bf16)] * 8,
        [],
        work * 2,
    )
    out_give, out_keep = call(
        ffn_out_body,
        "feed_forward_out",
        [at, after(hid, rest[0]), *down_a, *down_b, b_down],
        [stack, stack],
        [pltpu.VMEM((WIDTH, FF), bf16), pltpu.SemaphoreType.DMA((20,))],
        work,
        anywhere=9,
    )
    normed_grad, out_give, out_keep, *got = lax.optimization_barrier(
        (normed_grad, out_give, out_keep, *got_up, *got_gate, *rest)
    )
    got_up, got_gate, gate_b, up_b = [got[2 * i : 2 * i + 2] for i in range(4)]
    down_g = got[8:]

    gain_two = gain_rows[1:2]
    factor_own = lax.rsqrt(jnp.mean(hidden_own * hidden_own, axis=1, keepdims=True) + norm_epsilon)
    grad_gain_two = jnp.sum(normed_grad * hidden_own * factor_own, axis=0)
    scaled = normed_grad * gain_two
    grad_res = (
        lax.dynamic_slice_in_dim(dy, mine * OWN, OWN, 0).astype(f32)
        + factor_own * scaled
        - hidden_own * factor_own**3 * jnp.mean(scaled * hidden_own, axis=1, keepdims=True)
    )
    grad_low = grad_res.astype(bf16)
    db = team_gather(grad_low)
    got_gate = [gate_b[0], shift(gate_b[1], Y, 2)] + got_gate
    got_up = [x_out(up_b[0], 0, 0), x_out(up_b[1], *FLIPS[1])] + got_up
    out_both = (out_keep.astype(f32) + other_core(out_give).astype(f32)).astype(bf16)
    db, out_both, *got = lax.optimization_barrier((db, out_both, *got_gate, *got_up, *down_g))
    got_gate, got_up, down_g = got[:4], got[4:8], got[8:]
    got_down_a = [shift(down_g[1], Y, 1), shift(down_g[3], Y, 3)]
    got_down_b = [x_out(block, *flip) for block, flip in zip(down_g[6:], FLIPS[2:])]

    db_cols, dqkv, row_part, gain_part, part_give, part_keep = call(
        backward_body,
        "attention_backward",
        [at, db, cosine, sine, segment_row, segment_col, qr, kr, v, lse, a1, gain_rows, *first, *second],
        [low, ((LEN, 3 * HEAD), bf16), col, ((1, WIDTH), f32), stack, stack],
        [
            pltpu.VMEM((WIDTH, 3 * HEAD), bf16),
            pltpu.VMEM((WIDTH, HEAD), bf16),
            pltpu.VMEM((LEN, HEAD), bf16),
            pltpu.VMEM((LEN, HEAD), f32),
            pltpu.VMEM((LEN, HEAD), f32),
            pltpu.SemaphoreType.DMA((48,)),
        ],
        2 * LEN * WIDTH * 1024,
        anywhere=8,
    )
    part_give, part_keep, dqkv, down_y, down_0, down_1, *got = lax.optimization_barrier(
        (part_give, part_keep, dqkv, down_g[2], down_g[4], down_g[5], *got_down_a, *got_down_b)
    )
    got_down_a = [down_g[0], shift(down_y, Y, 2), *got[:2]]
    got_down_b = [x_out(down_0, 0, 0), x_out(down_1, *FLIPS[1]), *got[2:]]
    part_other = other_core(part_give)
    blocks = call(
        attention_weight_body,
        "attention_weights",
        [at, a1, dqkv, db, o],
        [((512, 512), bf16)] * 8,
        [],
        2 * LEN * WIDTH * 1024,
    )
    part_keep, part_other, *got = lax.optimization_barrier((part_keep, part_other, *blocks, *got_down_a, *got_down_b))
    blocks, got_down_a, got_down_b = got[:8], got[8:12], got[12:]
    part_both = (part_keep.astype(f32) + part_other.astype(f32)).astype(bf16)
    attn_grad = lax.psum_scatter(part_both, Z, scatter_dimension=0, tiled=True).astype(f32)
    got_attn_a = [shift(blocks[1], Y, 1), shift(blocks[3], Y, 3)]
    got_attn_b = [x_out(blocks[4 + i], *FLIPS[i]) for i in (2, 3)]
    row_part = after(row_part, part_both)

    block_at = jnp.stack([((r // 4 - y) % 4) * 4 + ((r // 2 % 2) ^ lo) * 2 + ((r % 2) ^ hi) for r in range(16)])
    pick = (block_at[:, None] == jnp.arange(16)[None, :]).astype(f32)
    gain_parts = jnp.concatenate([gain_part.reshape(16, 128), grad_gain_two.reshape(16, 128)], 1)
    gain_parts = jnp.dot(pick, gain_parts, precision=lax.Precision.HIGHEST)
    peaks = jnp.where((jnp.arange(QUERY_HEADS) == mine)[:, None], peak, 0.0)
    small = jnp.concatenate([row_part.reshape(6, 128), gain_parts[:, :128], gain_parts[:, 128:], peaks], 0)
    is_peak = (jnp.arange(46) >= 38)[:, None]

    def join(values):
        total, most = values[0], values[0]
        for value in values[1:]:
            total, most = total + value, jnp.maximum(most, value)
        return jnp.where(is_peak[-total.shape[0] :], most, total)

    small = join([small, other_core(small)])
    small = join([small, z_other(small, 1)])

    rest = lax.optimization_barrier((blocks[2], blocks[4], blocks[5], small, got_up[2], *got_attn_a, *got_attn_b))
    (block_y, block_0, block_1, small, got_up[2]), got_attn_a, got_attn_b = rest[:5], rest[5:7], rest[7:]
    got_attn_a = [blocks[0], shift(block_y, Y, 2), *got_attn_a]
    got_attn_b = [x_out(block_0, 0, 0), x_out(block_1, *FLIPS[1]), *got_attn_b]
    out_late = after(out_both, part_both)
    ffn_a, ffn_b = call(
        ffn_sum_body,
        "feed_forward_sums",
        [at, *got_gate, *got_down_a, *got_up, *got_down_b, up_b[0], down_0],
        [((512, 1536), bf16)] * 2,
        [],
        0,
    )

    small = join([small, z_other(small, 2)])
    row_sum = small[:6].reshape(LEN, 1)
    small = small[6:]
    small = join([small, y_other(small, 1)])
    got_attn_a, got_attn_b, ffn_a, ffn_b, small, attn_grad = lax.optimization_barrier(
        (got_attn_a, got_attn_b, ffn_a, ffn_b, small, attn_grad)
    )
    sums = call(
        join_body,
        "join_sums",
        [at, ffn_a, ffn_b, *got_attn_a, *got_attn_b, block_0],
        [((128, WIDTH), bf16)] * 8,
        [],
        0,
    )
    sums_a, sums_b = sums[:4], sums[4:]
    sum_b = [shift(sums_b[i], Y, i) for i in (1, 3)]
    sum_a = [x_out(sums_a[i], *FLIPS[i]) for i in (2, 3)]
    small = join([small, y_other(small, 2)])
    small = join([small, x_ring(small, 1)])
    rest = lax.optimization_barrier((*sum_b, *sum_a, sums_b[2], sums_a[0], sums_a[1], small))
    sum_b, sum_a, (late_y, late_0, late_1, small) = rest[:2], rest[2:4], rest[4:]
    sum_b = [sums_b[0], shift(late_y, Y, 2), *sum_b]
    sum_a = [x_out(late_0, 0, 0), x_out(late_1, *FLIPS[1]), *sum_a]
    ffn_own = lax.psum_scatter(out_late, Z, scatter_dimension=0, tiled=True).astype(f32)
    ffn_own = after(ffn_own, small)

    gain_pair = jnp.dot(pick, gain_rows[0].reshape(16, 128), precision=lax.Precision.HIGHEST)
    gain_cols = lax.dynamic_slice(gain_pair, (mine * 2, 0), (2, 128)).reshape(1, HEAD)
    grad_inputs = (
        db_cols.astype(f32) + r1 * attn_grad * gain_cols - x_own.astype(f32) * r1**2 * (row_sum / WIDTH)
    )
    home = [(h_cols.astype(f32) + ffn_own).astype(bf16), grad_inputs.astype(bf16)]
    home = swap(jnp.concatenate(home, 0))
    small = join([small, x_ring(small, 2)])
    sum_a, sum_b, home, small = lax.optimization_barrier((sum_a, sum_b, home, small))
    kv_sum = total([own_or(sum_a[0], sums_a[0]), *sum_a[1:]], slice(1536, None))
    first_halves = jnp.concatenate([kv_sum[:, :half], kv_sum[:, HEAD : HEAD + half]], 1)
    second_halves = jnp.concatenate([kv_sum[:, half:HEAD], kv_sum[:, HEAD + half :]], 1)
    kv_done = jnp.where(odd, second_halves, first_halves) + kv_partner(
        jnp.where(odd, first_halves, second_halves).astype(bf16)
    ).astype(f32)
    grads = call(
        finish_body,
        "finish",
        [at, sums_a[0], *sum_a, *sum_b],
        [((128, FF), f32)] * 3 + [((128, HEAD), f32)] * 2,
        [],
        0,
    )
    tok = y * 4 + lo * 2 + core
    gains_mine = lax.dynamic_slice(small[:32].reshape(2, 16, 128), (0, tok, 0), (2, 1, 128)).reshape(2, 128)
    peaks = small[32:, 0]

    head = hi * 4 + z
    peak_q = lax.dynamic_slice(peaks, (head,), (1,))
    pair = lax.dynamic_slice(peaks, (head // 2 * 2,), (2,))
    scale_q = jnp.sqrt(logit_ceiling / (peak_q + peak_floor_epsilon))
    scale_k = jnp.sqrt(logit_ceiling / (jnp.max(pair, keepdims=True) + peak_floor_epsilon))
    clipped_query = (w_query.astype(f32) * scale_q[None, :]).astype(bf16)
    clipped_key = (w_key.astype(f32) * scale_k[None, :]).astype(bf16)
    return (
        home[:LEN],
        home[LEN:].astype(f32),
        gains_mine[0],
        grads[3],
        kv_done[:, :half],
        kv_done[:, half:],
        grads[4],
        gains_mine[1],
        grads[0],
        grads[1],
        grads[2],
        clipped_query,
        clipped_key,
    )


def solution(mesh):
    torus = Mesh(mesh.devices.reshape(4, 2, 2, 2, 4), (Y, XLO, CORE, XHI, Z))
    both, rows = P(TOK, MDL), P(TOK)
    return jax.shard_map(
        on_device,
        mesh=torus,
        in_specs=(both, P(TOK, None), rows, both, both, both, both, rows, both, both, both, both),
        out_specs=(both, both, rows, both, both, both, both, rows, both, both, both, both, both),
        check_vma=False,
    )
```

```python
import functools
import math

import jax
import jax.numpy as jnp
from jax import lax
from jax.experimental import pallas as pl
from jax.experimental.pallas import tpu as pltpu
from jax.sharding import Mesh
from jax.sharding import PartitionSpec as P

QUERY_HEADS = 8
HEAD = 256
WIDTH = 2048
LEN = 768
OWN = 96
FF = 1024
Y, XLO, CORE, XHI, Z = "tok_0", "tok_1", "tok_2", "mdl_0", "mdl_1"
TOK = (Y, XLO, CORE)
MDL = (XHI, Z)

norm_epsilon = 1e-06
rope_base = 1000042.0
logit_ceiling = 4.0
masked_value = -1e30
peak_floor_epsilon = 1e-06
SCALE = HEAD ** (-0.5)
nt = (((1,), (1,)), ((), ()))
tn = (((0,), (0,)), ((), ()))
f32 = jnp.float32
bf16 = jnp.bfloat16


def dot(a, b, dims=(((1,), (0,)), ((), ()))):
    return lax.dot_general(a, b, dims, preferred_element_type=f32)


def swap(a):
    got = lax.ppermute(a, (CORE, XHI), [(1, 2), (2, 1)])
    return jnp.where(lax.axis_index(CORE) == lax.axis_index(XHI), a, got)


def other_core(a):
    return lax.ppermute(a, CORE, [(0, 1), (1, 0)])


def shift(a, axis, by):
    return lax.ppermute(a, axis, [(i, (i + by) % 4) for i in range(4)])


def z_other(a, mask):
    return lax.ppermute(a, Z, [(i, i ^ mask) for i in range(4)])


def y_other(a, mask):
    return lax.ppermute(a, Y, [(i, i ^ mask) for i in range(4)])


def kv_partner(a):
    return lax.ppermute(a, Z, [(0, 1), (1, 0), (2, 3), (3, 2)])


def plane_pairs(flip_lo, flip_core):
    pairs = []
    for lo in range(2):
        for core in range(2):
            for hi in range(2):
                pairs.append((lo * 4 + core * 2 + hi, (lo ^ flip_lo) * 4 + hi * 2 + (core ^ flip_core)))
    return pairs


def x_pairs(flip_lo, flip_core, back):
    pairs = plane_pairs(flip_lo, flip_core)
    return [(there, here) if back else (here, there) for here, there in pairs if here != there]


def x_in(a, flip_lo, flip_core):
    return lax.ppermute(a, (XLO, CORE, XHI), x_pairs(flip_lo, flip_core, False))


def x_out(a, flip_lo, flip_core):
    return lax.ppermute(a, (XLO, CORE, XHI), x_pairs(flip_lo, flip_core, True))


def own_or(got, own):
    return jnp.where(lax.axis_index(CORE) == lax.axis_index(XHI), own, got)


FLIPS = ((0, 0), (0, 1), (1, 0), (1, 1))


def from_y(a):
    return [a, shift(a, Y, -1), shift(a, Y, 2), shift(a, Y, 1)]


def from_z(a):
    return [a, shift(a, Z, -1), shift(a, Z, 2), shift(a, Z, 1)]


def x_ring(a, mask):
    return lax.ppermute(a, (XLO, XHI), [(i, i ^ mask) for i in range(4)])


def total(pieces, cols=slice(None)):
    return sum(piece[:, cols].astype(f32) for piece in pieces)


def team_gather(own):
    return lax.all_gather(own, (CORE, Z), axis=0, tiled=True)


def team_scatter(give, keep):
    both = (keep.astype(f32) + other_core(give).astype(f32)).astype(bf16)
    return lax.psum_scatter(both, Z, scatter_dimension=0, tiled=True).astype(f32)


def after(value, *others):
    return lax.optimization_barrier((value, *others))[0]


def rope_tables(segment_row):
    earlier = jnp.sum((segment_row[None, :] < segment_row[:, None]).astype(jnp.int32), axis=1)
    places = jnp.arange(LEN, dtype=jnp.int32) - earlier
    half = HEAD // 2
    inverse = jnp.exp(jnp.arange(half, dtype=f32) * (-2.0 * math.log(rope_base) / HEAD))
    angles = places.astype(f32)[:, None] * inverse[None, :]
    return jnp.cos(angles), jnp.sin(angles)


def position(r, at):
    return (((r >> 2) - at[0]) & 3) * 4 + (((r >> 1) & 1) ^ at[1]) * 2 + ((r & 1) ^ at[2])


def lanes(index, size):
    return pl.ds(pl.multiple_of(index * size, size), size)


def owner(at, there, dz):
    return (at[3] ^ there) * 4 + ((at[4] + dz) & 3)


def kdot(a, b, dims=(((1,), (0,)), ((), ()))):
    return lax.dot_general(a, b, dims, preferred_element_type=f32)


def in_vmem(n):
    return [pl.BlockSpec(memory_space=pltpu.VMEM)] * n


def call(body, name, inputs, outs, scratch, flops, megabytes=56, anywhere=0, outs_anywhere=0):
    moved = sum(v.size * v.dtype.itemsize for v in inputs[1:])
    moved += sum(math.prod(s) * jnp.dtype(d).itemsize for s, d in outs)
    specs = [pl.BlockSpec(memory_space=pltpu.SMEM)] + in_vmem(len(inputs) - 1 - anywhere)
    specs += [pl.BlockSpec(memory_space=pl.ANY)] * anywhere
    return list(pl.pallas_call(
        body,
        name=name,
        out_shape=[jax.ShapeDtypeStruct(s, d) for s, d in outs],
        in_specs=specs,
        out_specs=in_vmem(len(outs) - outs_anywhere) + [pl.BlockSpec(memory_space=pl.ANY)] * outs_anywhere,
        scratch_shapes=scratch,
        cost_estimate=pl.CostEstimate(flops=int(flops), bytes_accessed=int(moved), transcendentals=0),
        compiler_params=pltpu.CompilerParams(vmem_limit_bytes=megabytes * 2**20),
    )(*inputs))


def turn(values, cosine, sine):
    first, second = values[:, :128], values[:, 128:]
    return first * cosine - second * sine, second * cosine + first * sine


def attention_weights(a_refs, b_refs, w_qkv, w_o, sem):
    copies = []

    def move(source, to):
        copies.append(pltpu.make_async_copy(source, to, sem.at[len(copies)]))
        copies[-1].start()

    for i in range(4):
        for dy in range(4):
            rows = pl.ds((dy * 4 + i) * 128, 128)
            move(b_refs[i].at[pl.ds(dy * 144, 128), pl.ds(256, 256)], w_o.at[rows])
    for dy in range(4):
        for i in range(4):
            rows = pl.ds((dy * 4 + i) * 128, 128)
            move(b_refs[i].at[pl.ds(dy * 144, 128), pl.ds(0, 256)], w_qkv.at[rows, pl.ds(0, 256)])
            move(a_refs[dy].at[pl.ds(i * 128, 128)], w_qkv.at[rows, pl.ds(256, 512)])
    return copies


def along_y_body(at, *refs):
    riders, gain_one, gain_two = refs[:3]
    tokens, cotangent, w_query, w_output, w_up, w_down, out, mixed, sem = refs[3:]
    pairs = [
        (w_query, out.at[pl.ds(0, 128), pl.ds(0, 256)]),
        (w_output, out.at[pl.ds(0, 128), pl.ds(256, 256)]),
        (w_up.at[:, pl.ds(0, 512)], out.at[pl.ds(144, 128)]),
        (w_up.at[:, pl.ds(512, 512)], out.at[pl.ds(272, 128)]),
        (w_down.at[:, pl.ds(512, 512)], out.at[pl.ds(400, 128)]),
        (tokens, mixed.at[pl.ds(0, 768)]),
        (cotangent, mixed.at[pl.ds(784, 768)]),
    ]
    copies = [pltpu.make_async_copy(a, b, sem.at[i]) for i, (a, b) in enumerate(pairs)]
    for copy in copies:
        copy.start()
    row = lax.broadcasted_iota(jnp.int32, (16, 128), 0)
    gains = jnp.where(row == 0, gain_one[...], jnp.where(row == 1, gain_two[...], 0.0))
    out[128:144, :128] = gains.astype(bf16)
    out[128:144, 128:] = jnp.zeros((16, 384), bf16)
    mixed[768:784, :] = riders[...]
    for copy in copies:
        copy.wait()


def along_x_body(at, *refs):
    key, value, other, w_gate, w_down, out, sem = refs
    pairs = [
        (w_gate.at[:, pl.ds(0, 512)], out.at[pl.ds(128, 128)]),
        (w_gate.at[:, pl.ds(512, 512)], out.at[pl.ds(256, 128)]),
        (w_down.at[:, pl.ds(0, 512)], out.at[pl.ds(384, 128)]),
    ]
    copies = [pltpu.make_async_copy(a, b, sem.at[i]) for i, (a, b) in enumerate(pairs)]
    for copy in copies:
        copy.start()
    odd = at[4] & 1
    out[:128, lanes(odd, 128)] = key[...]
    out[:128, lanes(1 - odd, 128)] = other[:, :128]
    out[:128, lanes(2 + odd, 128)] = value[...]
    out[:128, lanes(3 - odd, 128)] = other[:, 128:]
    for copy in copies:
        copy.wait()


def pack_body(at, *refs):
    xs, ys, to_y, to_x, sem = refs[:4], refs[4:8], refs[8], refs[9], refs[10]
    pairs = [(ref.at[pl.ds(0, 128)], to_y.at[pl.ds(128 * i, 128)]) for i, ref in enumerate(xs)]
    pairs += [(ref.at[pl.ds(0, 144)], to_x.at[pl.ds(144 * i, 144)]) for i, ref in enumerate(ys)]
    copies = [pltpu.make_async_copy(a, b, sem.at[i]) for i, (a, b) in enumerate(pairs)]
    for copy in copies:
        copy.start()
    for copy in copies:
        copy.wait()


def riders_body(at, *refs):
    xs, ys = refs[:4], refs[4:8]
    a_wide, b_wide, a_down, b_down, sem = refs[8:]
    copies = []
    for ref, row, wide, down in [(xs, 128, a_wide, a_down), (ys, 144, b_wide, b_down)]:
        for i in range(4):
            for j in range(3):
                source = ref[i].at[pl.ds(row + j * 128, 128)]
                rows = pl.ds(i * 128, 128)
                to = down.at[rows] if j == 2 else wide.at[rows, pl.ds(j * 512, 512)]
                copies.append(pltpu.make_async_copy(source, to, sem.at[len(copies)]))
    for copy in copies:
        copy.start()
    for copy in copies:
        copy.wait()


def allowed_block(i, seg_col, seg_row):
    rows, cols = 256, (i + 1) * 256
    same = seg_col[i * 256 : (i + 1) * 256, :] == seg_row[:, :cols]
    row = i * 256 + lax.broadcasted_iota(jnp.int32, (rows, cols), 0)
    return same & (row >= lax.broadcasted_iota(jnp.int32, (rows, cols), 1))


def forward_body(at, *refs):
    x, cosine, sine, seg_row, seg_col = refs[:5]
    a_refs, b_refs = refs[5:9], refs[9:13]
    a1, r1, x_mine, qr, kr, v, o, lse, peak, gains, give, keep = refs[13:25]
    w_qkv, w_o, gain_rows, sem, gain_sem = refs[25:]
    gain_copies = []
    for dy in range(4):
        for i in range(4):
            source = b_refs[i].at[pl.ds(dy * 144 + 128, 16), pl.ds(0, 128)]
            to = gain_rows.at[:, pl.ds((dy * 4 + i) * 128, 128)]
            gain_copies.append(pltpu.make_async_copy(source, to, gain_sem.at[len(gain_copies)]))
            gain_copies[-1].start()
    copies = attention_weights(a_refs, b_refs, w_qkv, w_o, sem)
    for copy in gain_copies:
        copy.wait()
    gains[...] = gain_rows[...].astype(f32)[:8]
    own = at[3] * 4 + at[4]
    for r in range(16):
        rows = pl.ds(pl.multiple_of((r // 2) * LEN + own * OWN, OWN), OWN)
        x_mine[:, lanes(position(r, at), 128)] = x[rows, (r % 2) * 128 : (r % 2 + 1) * 128]

    def norm(step, carry):
        rows = pl.ds(pl.multiple_of(step * 128, 128), 128)
        total = jnp.zeros((128, 1), f32)
        for m in range(8):
            value = x[pl.ds(pl.multiple_of(m * LEN + step * 128, 128), 128), :].astype(f32)
            total = total + jnp.sum(value * value, axis=1, keepdims=True)
        factor = lax.rsqrt(total / WIDTH + norm_epsilon)
        r1[rows, :] = factor
        for r in range(16):
            at_lanes = lanes(position(r, at), 128)
            from_rows = pl.ds(pl.multiple_of((r // 2) * LEN + step * 128, 128), 128)
            value = x[from_rows, (r % 2) * 128 : (r % 2 + 1) * 128].astype(f32)
            a1[rows, at_lanes] = (value * factor * gains[0:1, at_lanes]).astype(bf16)
        return carry

    lax.fori_loop(0, 6, norm, 0)
    for copy in copies:
        copy.wait()
    for i in range(3):
        rows = slice(i * 256, (i + 1) * 256)
        qk = kdot(a1[rows, :], w_qkv[:, :512])
        cos_i, sin_i = cosine[rows, :], sine[rows, :]
        for ref, at_col in ((qr, 0), (kr, 256)):
            one, two = turn(qk[:, at_col : at_col + 256], cos_i, sin_i)
            ref[rows, :128] = one.astype(bf16)
            ref[rows, 128:] = two.astype(bf16)
        v[rows, :] = kdot(a1[rows, :], w_qkv[:, 512:]).astype(bf16)
    largest = jnp.zeros((1, 1), f32)
    for i in range(3):
        rows, cols = slice(i * 256, (i + 1) * 256), (i + 1) * 256
        allowed = allowed_block(i, seg_col, seg_row)
        scores = kdot(qr[rows, :], kr[:cols, :], nt) * SCALE
        masked = jnp.where(allowed, scores, masked_value)
        size = jnp.where(allowed, jnp.abs(scores), 0.0)
        largest = jnp.maximum(largest, jnp.max(jnp.max(size, axis=1, keepdims=True), axis=0, keepdims=True))
        top = jnp.max(masked, axis=1, keepdims=True)
        log_total = top + jnp.log(jnp.sum(jnp.exp(masked - top), axis=1, keepdims=True))
        lse[rows, :] = log_total
        probs = jnp.exp(masked - log_total).astype(bf16)
        o[rows, :] = kdot(probs, v[:cols, :]).astype(bf16)
    peak[...] = jnp.broadcast_to(largest, (8, 128))
    for ref, c in ((give, 1 - at[3]), (keep, at[3])):
        rows = pl.ds(pl.multiple_of(c * 384, 384), 384)
        for half in range(2):
            cols = slice(half * 1024, (half + 1) * 1024)
            ref[:, cols] = kdot(o[rows, :], w_o[cols, :], nt).astype(bf16)


def reorder_body(at, whole, out):
    for r in range(16):
        rows = slice((r // 2) * LEN, (r // 2 + 1) * LEN)
        out[:, lanes(position(r, at), 128)] = whole[rows, (r % 2) * 128 : (r % 2 + 1) * 128]


def start_either(at, own, got, to, sem):
    mine = at[2] == at[3]

    @pl.when(mine)
    def _():
        pltpu.make_async_copy(own, to, sem).start()

    @pl.when(jnp.logical_not(mine))
    def _():
        pltpu.make_async_copy(got, to, sem).start()

    return pltpu.make_async_copy(got, to, sem)


def rows_a(refs, to_ref, cols, sem, copies):
    for i, ref in enumerate(refs):
        to = to_ref.at[pl.ds(i * 512, 512), cols]
        copies.append(pltpu.make_async_copy(ref, to, sem.at[len(copies)]))
        copies[-1].start()


def rows_b(at, own, refs, to_ref, cols, sem, copies):
    for i, ref in enumerate(refs):
        for j in range(4):
            to = to_ref.at[pl.ds((j * 4 + i) * 128, 128), cols]
            rows = pl.ds(j * 128, 128)
            if i == 0:
                copies.append(start_either(at, own.at[rows], ref.at[rows], to, sem.at[len(copies)]))
            else:
                copies.append(pltpu.make_async_copy(ref.at[rows], to, sem.at[len(copies)]))
                copies[-1].start()


def ffn_body(at, *refs):
    gains, h_in, dy_in = refs[:3]
    wide_a, down_a, wide_b, down_b = [refs[3 + 4 * i : 7 + 4 * i] for i in range(4)]
    own_wide, own_down = refs[19:21]
    h_cols, a2_out, hid_out, dgate_out, dup_out, give_out, keep_out = refs[21:28]
    up_outs, gate_outs = refs[28:30], refs[30:32]
    h, dy, a2, hid, dgate, dup, give, keep, up_0, up_1, gate_0, gate_1 = refs[32:44]
    w_gate, w_up, w_down, sem, out_sem = refs[44:]
    h_copy = pltpu.make_async_copy(h_in, h, out_sem.at[14])
    h_copy.start()
    copies = []
    rows_a(wide_a, w_gate, pl.ds(0, FF), sem, copies)
    rows_b(at, own_wide, wide_b, w_up, pl.ds(0, FF), sem, copies)
    rows_a(down_a, w_down, pl.ds(0, 512), sem, copies)
    rows_b(at, own_down, down_b, w_down, pl.ds(512, 512), sem, copies)
    copies.append(pltpu.make_async_copy(dy_in, dy, out_sem.at[15]))
    copies[-1].start()
    sent = []

    def send(source, to):
        sent.append(pltpu.make_async_copy(source, to, out_sem.at[len(sent)]))
        sent[-1].start()

    h_copy.wait()
    own = at[3] * 4 + at[4]
    for j in range(2):
        h_cols[:, j * 128 : (j + 1) * 128] = h[:, lanes(position(2 * own + j, at), 128)]
    for i in range(6):
        rows = slice(i * 128, (i + 1) * 128)
        value = h[rows, :].astype(f32)
        factor = lax.rsqrt(jnp.mean(value * value, axis=1, keepdims=True) + norm_epsilon)
        a2[rows, :] = (value * factor * gains[1:2, :]).astype(bf16)
    send(a2, a2_out)
    for copy in copies:
        copy.wait()
    for half in range(2):
        rows = slice(half * 384, (half + 1) * 384)
        for j in range(4):
            cols = slice(j * 256, (j + 1) * 256)
            gate = kdot(a2[rows, :], w_gate[:, cols])
            up = kdot(a2[rows, :], w_up[:, cols])
            grad = kdot(dy[rows, :], w_down[:, cols])
            sig = 1.0 / (1.0 + jnp.exp(-gate))
            act = gate * sig
            hid[rows, cols] = (act * up).astype(bf16)
            dgate[rows, cols] = (grad * up * sig * (1.0 + gate * (1.0 - sig))).astype(bf16)
            dup[rows, cols] = (grad * act).astype(bf16)
    for source, to in ((hid, hid_out), (dgate, dgate_out), (dup, dup_out)):
        send(source, to)
    for ref, to, c in ((give, give_out, 1 - at[3]), (keep, keep_out, at[3])):
        rows = pl.ds(pl.multiple_of(c * 384, 384), 384)
        for j in range(4):
            cols = slice(j * 512, (j + 1) * 512)
            ref[:, cols] = (
                kdot(dgate[rows, :], w_gate[cols, :], nt) + kdot(dup[rows, :], w_up[cols, :], nt)
            ).astype(bf16)
        send(ref, to)
    for i, ref, to in ((1, gate_0, gate_outs[0]), (3, gate_1, gate_outs[1])):
        for j in range(2):
            n = slice(j * 512, (j + 1) * 512)
            ref[:, n] = kdot(a2[:, i * 512 : (i + 1) * 512], dgate[:, n], tn).astype(bf16)
        send(ref, to)
    for i in range(4):
        cols = slice((i * 4 + 2) * 128, (i * 4 + 4) * 128)
        for j in range(2):
            n = slice(j * 512, (j + 1) * 512)
            value = kdot(a2[:, cols], dup[:, n], tn).astype(bf16)
            up_0[i * 128 : (i + 1) * 128, n] = value[:128]
            up_1[i * 128 : (i + 1) * 128, n] = value[128:]
    send(up_0, up_outs[0])
    send(up_1, up_outs[1])
    for copy in sent:
        copy.wait()


def ffn_out_body(at, hid, *refs):
    down_a, down_b, own_down = refs[:4], refs[4:8], refs[8]
    give, keep, w_down, sem = refs[9:]
    copies = []
    rows_a(down_a, w_down, pl.ds(0, 512), sem, copies)
    rows_b(at, own_down, down_b, w_down, pl.ds(512, 512), sem, copies)
    for copy in copies:
        copy.wait()
    for ref, c in ((give, 1 - at[3]), (keep, at[3])):
        for dz in range(4):
            m = c * 4 + dz
            pair = pl.ds(pl.multiple_of((position(2 * m, at) >> 1) * 256, 256), 256)
            value = kdot(hid[...], w_down[pair, :], nt)
            rows = slice(dz * LEN, (dz + 1) * LEN)
            for j in range(2):
                ref[rows, lanes(at[2] ^ j, 128)] = value[:, j * 128 : (j + 1) * 128].astype(bf16)


def weight_rest_body(at, a2, dy, dgate, dup, hid, *outs):
    a_wide, b_wide, a_down, b_down = outs[:2], outs[2:4], outs[4:8], outs[8:]
    for i in range(4):
        cols, rows = slice(i * 512, (i + 1) * 512), slice(i * 128, (i + 1) * 128)
        for j in range(2):
            n = slice(j * 512, (j + 1) * 512)
            value = kdot(a2[:, i * 512 : i * 512 + 256], dup[:, n], tn).astype(bf16)
            for k in range(2):
                b_wide[k][rows, n] = value[k * 128 : (k + 1) * 128]
            if i % 2 == 0:
                a_wide[i // 2][:, n] = kdot(a2[:, cols], dgate[:, n], tn).astype(bf16)
        a_down[i][...] = kdot(dy[:, cols], hid[:, :512], tn).astype(bf16)
        value = kdot(dy[:, cols], hid[:, 512:], tn).astype(bf16)
        for k in range(4):
            b_down[k][rows, :] = value[k * 128 : (k + 1) * 128]


def backward_body(at, *refs):
    db, cosine, sine, seg_row, seg_col, qr, kr, v, lse, a1, gains = refs[:11]
    a_refs, b_refs = refs[11:15], refs[15:19]
    db_cols, dqkv, row_part, gain_part, give, keep = refs[19:25]
    w_qkv, w_o, d_o, dk_sum, dv_sum, sem = refs[25:]
    copies = attention_weights(a_refs, b_refs, w_qkv, w_o, sem)
    own = at[3] * 4 + at[4]
    for j in range(2):
        db_cols[:, j * 128 : (j + 1) * 128] = db[:, lanes(position(2 * own + j, at), 128)]
    for copy in copies:
        copy.wait()
    for i in range(3):
        rows = slice(i * 256, (i + 1) * 256)
        d_o[rows, :] = kdot(db[rows, :], w_o[...]).astype(bf16)
    for i in (2, 1, 0):
        rows, cols = slice(i * 256, (i + 1) * 256), (i + 1) * 256
        allowed = allowed_block(i, seg_col, seg_row)
        scores = kdot(qr[rows, :], kr[:cols, :], nt) * SCALE
        probs = jnp.exp(jnp.where(allowed, scores, masked_value) - lse[rows, :])
        low = probs.astype(bf16)
        dp = kdot(d_o[rows, :], v[:cols, :], nt)
        delta = jnp.sum(dp * probs, axis=1, keepdims=True)
        ds = (probs * (dp - delta)).astype(bf16)
        dq = kdot(ds, kr[:cols, :]) * SCALE
        row_part[rows, :] = jnp.sum(dq * qr[rows, :].astype(f32), axis=1, keepdims=True)
        one, two = turn(dq, cosine[rows, :], -sine[rows, :])
        dqkv[rows, :128] = one.astype(bf16)
        dqkv[rows, 128:256] = two.astype(bf16)
        dk_new = kdot(ds, qr[rows, :], tn)
        dv_new = kdot(low, d_o[rows, :], tn)
        if i == 2:
            dk_sum[...] = dk_new
            dv_sum[...] = dv_new
        else:
            dk_sum[:cols, :] = dk_sum[:cols, :] + dk_new
            dv_sum[:cols, :] = dv_sum[:cols, :] + dv_new
    for i in range(3):
        rows = slice(i * 256, (i + 1) * 256)
        dk = dk_sum[rows, :] * SCALE
        dv_i = dv_sum[rows, :]
        row_part[rows, :] = (
            row_part[rows, :]
            + jnp.sum(dk * kr[rows, :].astype(f32), axis=1, keepdims=True)
            + jnp.sum(dv_i * v[rows, :].astype(f32), axis=1, keepdims=True)
        )
        one, two = turn(dk, cosine[rows, :], -sine[rows, :])
        dqkv[rows, 256:384] = one.astype(bf16)
        dqkv[rows, 384:512] = two.astype(bf16)
        dqkv[rows, 512:] = dv_i.astype(bf16)
    for m, ref in [(j, give) for j in range(4)] + [(j, keep) for j in range(4)]:
        half = 1 - at[3] if ref is give else at[3]
        pair = lanes(position(2 * (half * 4 + m), at) >> 1, 256)
        value = kdot(dqkv[...], w_qkv[pair, :], nt)
        gain_part[:, pair] = jnp.sum(value * a1[:, pair].astype(f32), axis=0, keepdims=True) / gains[0:1, pair]
        rows = slice(m * LEN, (m + 1) * LEN)
        for j in range(2):
            ref[rows, lanes(at[2] ^ j, 128)] = value[:, j * 128 : (j + 1) * 128].astype(bf16)


def attention_weight_body(at, a1, dqkv, db, o, *outs):
    a_outs, b_outs = outs[:4], outs[4:]
    for i in range(4):
        cols, rows = slice(i * 512, (i + 1) * 512), slice(i * 128, (i + 1) * 128)
        a_outs[i][...] = kdot(a1[:, cols], dqkv[:, 256:], tn).astype(bf16)
        for n, left, right in ((slice(0, 256), a1, dqkv.at[:, :256]), (slice(256, 512), db, o)):
            value = kdot(left[:, cols], right[...], tn).astype(bf16)
            for k in range(4):
                b_outs[k][rows, n] = value[k * 128 : (k + 1) * 128]


def ffn_sum_body(at, *refs):
    wide_a, down_a, wide_b, down_b = [refs[4 * i : 4 * i + 4] for i in range(4)]
    own_wide, own_down, out_a, out_b = refs[16:]
    mine = at[2] == at[3]
    for cols, a, b, own in ((slice(0, FF), wide_a, wide_b, own_wide), (slice(FF, 1536), down_a, down_b, own_down)):
        value = a[0][...].astype(f32) + a[1][...].astype(f32) + a[2][...].astype(f32) + a[3][...].astype(f32)
        out_a[:, cols] = value.astype(bf16)
        value = jnp.where(mine, own[...], b[0][...]).astype(f32) + b[1][...].astype(f32)
        value = value + b[2][...].astype(f32) + b[3][...].astype(f32)
        out_b[:, cols] = value.astype(bf16)


def join_body(at, *refs):
    ffn_a, ffn_b, a, b, own, outs = refs[0], refs[1], refs[2:6], refs[6:10], refs[10], refs[11:]
    for i in range(4):
        rows = slice(i * 128, (i + 1) * 128)
        outs[i][:, :1536] = ffn_a[rows, :]
        outs[4 + i][:, :1536] = ffn_b[rows, :]
        value = a[0][rows, :].astype(f32) + a[1][rows, :].astype(f32) + a[2][rows, :].astype(f32)
        outs[i][:, 1536:] = (value + a[3][rows, :].astype(f32)).astype(bf16)
        head = jnp.where(at[2] == at[3], own[rows, :], b[0][rows, :])
        value = head.astype(f32) + b[1][rows, :].astype(f32) + b[2][rows, :].astype(f32)
        outs[4 + i][:, 1536:] = (value + b[3][rows, :].astype(f32)).astype(bf16)


def finish_body(at, *refs):
    own, a, b = refs[0], refs[1:5], refs[5:9]
    gate, up, down, query, output = refs[9:]
    mine = at[2] == at[3]

    def sum_a(cols):
        head = jnp.where(mine, own[:, cols], a[0][:, cols])
        return head.astype(f32) + a[1][:, cols].astype(f32) + a[2][:, cols].astype(f32) + a[3][:, cols].astype(f32)

    def sum_b(cols):
        return b[0][:, cols].astype(f32) + b[1][:, cols].astype(f32) + b[2][:, cols].astype(f32) + b[3][:, cols].astype(f32)

    for j in range(4):
        cols = slice(j * 256, (j + 1) * 256)
        gate[:, cols] = sum_a(cols)
        up[:, cols] = sum_b(cols)
    for j in range(2):
        cols = slice(FF + j * 256, FF + (j + 1) * 256)
        down[:, j * 256 : (j + 1) * 256] = sum_a(cols)
        down[:, 512 + j * 256 : 512 + (j + 1) * 256] = sum_b(cols)
    query[...] = sum_b(slice(1536, 1792))
    output[...] = sum_b(slice(1792, 2048))


def on_device(
    tokens,
    segments,
    gain_attn,
    w_query,
    w_key,
    w_value,
    w_output,
    gain_ffn,
    w_gate,
    w_up,
    w_down,
    cotangent,
):
    y, lo, core = lax.axis_index(Y), lax.axis_index(XLO), lax.axis_index(CORE)
    hi, z = lax.axis_index(XHI), lax.axis_index(Z)
    at = jnp.stack([y, lo, hi, core, z]).astype(jnp.int32)
    mine = core * 4 + z

    riders = jnp.zeros((16, HEAD), bf16).at[:3].set(segments.reshape(3, HEAD).astype(bf16))
    hf = FF // 2
    odd = z % 2 == 1
    half = HEAD // 2
    kv_other = kv_partner(jnp.concatenate([w_key, w_value], 1))
    y_rows, mixed = call(
        along_y_body,
        "lay_out_y",
        [
            at,
            riders,
            gain_attn.astype(f32).reshape(1, 128),
            gain_ffn.astype(f32).reshape(1, 128),
            tokens,
            cotangent,
            w_query,
            w_output,
            w_up,
            w_down,
        ],
        [((528, 2 * HEAD), bf16), ((1552, HEAD), bf16)],
        [pltpu.SemaphoreType.DMA((7,))],
        0,
        anywhere=6,
    )
    (x_rows,) = call(
        along_x_body,
        "lay_out_x",
        [at, w_key, w_value, kv_other, w_gate, w_down],
        [((512, 2 * HEAD), bf16)],
        [pltpu.SemaphoreType.DMA((3,))],
        0,
        anywhere=2,
    )
    got = swap(mixed)
    along_y = [shift(y_rows, Y, -1), shift(y_rows, Y, 1)]
    along_x = [x_in(x_rows, *flip) for flip in FLIPS[2:]]
    got, late_y, late_x, *rest = lax.optimization_barrier((got, y_rows, x_rows, *along_y, *along_x))
    along_y = [y_rows, rest[0], shift(late_y, Y, 2), rest[1]]
    along_x = [own_or(x_in(late_x, 0, 0), x_rows), x_in(late_x, *FLIPS[1]), *rest[2:]]
    rest = lax.optimization_barrier((*along_x, *along_y))
    to_y, to_x = call(
        pack_body,
        "pack",
        [at, *rest],
        [((512, 2 * HEAD), bf16), ((576, 2 * HEAD), bf16)],
        [pltpu.SemaphoreType.DMA((8,))],
        0,
        anywhere=8,
    )
    a_wide, b_wide, a_down, b_down = call(
        riders_body,
        "riders",
        [at, *rest],
        [((512, FF), bf16)] * 2 + [((512, hf), bf16)] * 2,
        [pltpu.SemaphoreType.DMA((24,))],
        0,
        anywhere=8,
    )
    x_own = got[:LEN]
    x_all = team_gather(x_own)
    upstream = team_gather(after(got[784:1552], to_x))
    segment_row = got[LEN : LEN + 3].astype(f32).reshape(1, LEN)
    segment_col = segment_row.reshape(LEN, 1)
    cosine, sine = rope_tables(segment_row[0])
    first = [shift(to_y, Y, -1), shift(to_y, Y, 1)]
    second = [x_in(to_x, *flip) for flip in FLIPS[2:]]
    late_y, late_x, *rest = lax.optimization_barrier((to_y, to_x, *first, *second))
    first, second = rest[:2], rest[2:]
    first = [to_y, first[0], shift(late_y, Y, 2), first[1]]
    second = [own_or(x_in(late_x, 0, 0), to_x), x_in(late_x, *FLIPS[1])] + second
    x_all, cosine, sine, segment_row, segment_col, *rest = lax.optimization_barrier(
        (x_all, cosine, sine, segment_row, segment_col, *first, *second, a_wide, b_wide, a_down, b_down)
    )
    first, second, (a_wide, b_wide, a_down, b_down) = rest[:4], rest[4:8], rest[8:]
    wide_a = [shift(a_wide, Y, -1), shift(a_wide, Y, 1)]
    wide_b = [x_in(b_wide, *flip) for flip in FLIPS[2:]]

    part = ((LEN // 2, WIDTH), bf16)
    act, low, col = ((LEN, WIDTH), bf16), ((LEN, HEAD), bf16), ((LEN, 1), f32)
    a1, r1, x_mine, qr, kr, v, o, lse, peak, gain_rows, give, keep = call(
        forward_body,
        "attention_forward",
        [at, x_all, cosine, sine, segment_row, segment_col, *first, *second],
        [act, col, ((OWN, WIDTH), bf16), low, low, low, low, col, ((8, 128), f32), ((8, WIDTH), f32), part, part],
        [
            pltpu.VMEM((WIDTH, 3 * HEAD), bf16),
            pltpu.VMEM((WIDTH, HEAD), bf16),
            pltpu.VMEM((16, WIDTH), bf16),
            pltpu.SemaphoreType.DMA((48,)),
            pltpu.SemaphoreType.DMA((16,)),
        ],
        2 * LEN * WIDTH * 1024,
        anywhere=8,
    )
    give, keep, upstream, *done = lax.optimization_barrier(
        (give, keep, upstream, *wide_a, *wide_b, a_wide, b_wide, a_down, b_down)
    )
    wide_a, wide_b, (a_wide, b_wide, a_down, b_down) = done[:2], done[2:4], done[4:]
    attn_own = team_scatter(give, keep)
    wide_a = [a_wide, wide_a[0], shift(a_wide, Y, 2), wide_a[1]]
    wide_b = [x_in(b_wide, *flip) for flip in FLIPS[:2]] + wide_b
    down_a = [shift(a_down, Y, -1), shift(a_down, Y, 1)]
    (dy,) = call(reorder_body, "order_upstream", [at, upstream], [((LEN, WIDTH), bf16)], [], 0)


    attn_own, dy, *done = lax.optimization_barrier((attn_own, dy, *wide_a, *wide_b, *down_a, b_wide, a_down, b_down))
    wide_a, wide_b, down_a, (b_wide, a_down, b_down) = done[:4], done[4:8], done[8:10], done[10:]
    down_b = [x_in(b_down, *flip) for flip in FLIPS]
    down_a = [a_down, down_a[0], shift(a_down, Y, 2), down_a[1]]
    hidden_own = x_mine.astype(f32) + attn_own
    hidden = team_gather(hidden_own.astype(bf16))
    wide = ((LEN, FF), bf16)
    block = ((512, FF), bf16)
    h_cols, a2, hid, dgate, dup, give, keep, up_2, up_3, gate_1, gate_3 = call(
        ffn_body,
        "feed_forward",
        [at, gain_rows, hidden, dy, *wide_a, *down_a, *wide_b, *down_b, b_wide, b_down],
        [low, act, wide, wide, wide, part, part, block, block, block, block],
        [
            *[pltpu.VMEM(*v) for v in (act, act, act, wide, wide, wide, part, part, block, block, block, block)],
            pltpu.VMEM((WIDTH, FF), bf16),
            pltpu.VMEM((WIDTH, FF), bf16),
            pltpu.VMEM((WIDTH, FF), bf16),
            pltpu.SemaphoreType.DMA((40,)),
            pltpu.SemaphoreType.DMA((16,)),
        ],
        14 * LEN * WIDTH * FF,
        anywhere=20,
        outs_anywhere=10,
    )
    other = other_core(give)
    wide_out, stack = ((512, FF), bf16), ((4 * LEN, HEAD), bf16)
    work = 2 * LEN * WIDTH * FF
    both = (keep.astype(f32) + other.astype(f32)).astype(bf16)
    normed_grad = lax.psum_scatter(both, Z, scatter_dimension=0, tiled=True).astype(f32)
    dgate, dup, hid = lax.optimization_barrier((dgate, dup, hid, both))[:3]
    got_up = [x_out(up_2, *FLIPS[2]), x_out(up_3, *FLIPS[3])]
    got_gate = [shift(gate_1, Y, 1), shift(gate_3, Y, 3)]
    rest = call(
        weight_rest_body,
        "weight_rest",
        [at, a2, dy, dgate, dup, hid],
        [wide_out] * 4 + [((512, hf), bf16)] * 8,
        [],
        work * 2,
    )
    out_give, out_keep = call(
        ffn_out_body,
        "feed_forward_out",
        [at, after(hid, rest[0]), *down_a, *down_b, b_down],
        [stack, stack],
        [pltpu.VMEM((WIDTH, FF), bf16), pltpu.SemaphoreType.DMA((20,))],
        work,
        anywhere=9,
    )
    normed_grad, out_give, out_keep, *got = lax.optimization_barrier(
        (normed_grad, out_give, out_keep, *got_up, *got_gate, *rest)
    )
    got_up, got_gate, gate_b, up_b = [got[2 * i : 2 * i + 2] for i in range(4)]
    down_g = got[8:]

    gain_two = gain_rows[1:2]
    factor_own = lax.rsqrt(jnp.mean(hidden_own * hidden_own, axis=1, keepdims=True) + norm_epsilon)
    grad_gain_two = jnp.sum(normed_grad * hidden_own * factor_own, axis=0)
    scaled = normed_grad * gain_two
    grad_res = (
        lax.dynamic_slice_in_dim(dy, mine * OWN, OWN, 0).astype(f32)
        + factor_own * scaled
        - hidden_own * factor_own**3 * jnp.mean(scaled * hidden_own, axis=1, keepdims=True)
    )
    grad_low = grad_res.astype(bf16)
    db = team_gather(grad_low)
    got_gate = [gate_b[0], shift(gate_b[1], Y, 2)] + got_gate
    got_up = [x_out(up_b[0], 0, 0), x_out(up_b[1], *FLIPS[1])] + got_up
    out_both = (out_keep.astype(f32) + other_core(out_give).astype(f32)).astype(bf16)
    db, out_both, *got = lax.optimization_barrier((db, out_both, *got_gate, *got_up, *down_g))
    got_gate, got_up, down_g = got[:4], got[4:8], got[8:]
    got_down_a = [shift(down_g[1], Y, 1), shift(down_g[3], Y, 3)]
    got_down_b = [x_out(block, *flip) for block, flip in zip(down_g[6:], FLIPS[2:])]

    db_cols, dqkv, row_part, gain_part, part_give, part_keep = call(
        backward_body,
        "attention_backward",
        [at, db, cosine, sine, segment_row, segment_col, qr, kr, v, lse, a1, gain_rows, *first, *second],
        [low, ((LEN, 3 * HEAD), bf16), col, ((1, WIDTH), f32), stack, stack],
        [
            pltpu.VMEM((WIDTH, 3 * HEAD), bf16),
            pltpu.VMEM((WIDTH, HEAD), bf16),
            pltpu.VMEM((LEN, HEAD), bf16),
            pltpu.VMEM((LEN, HEAD), f32),
            pltpu.VMEM((LEN, HEAD), f32),
            pltpu.SemaphoreType.DMA((48,)),
        ],
        2 * LEN * WIDTH * 1024,
        anywhere=8,
    )
    part_give, part_keep, dqkv, down_y, down_0, down_1, *got = lax.optimization_barrier(
        (part_give, part_keep, dqkv, down_g[2], down_g[4], down_g[5], *got_down_a, *got_down_b)
    )
    got_down_a = [down_g[0], shift(down_y, Y, 2), *got[:2]]
    got_down_b = [x_out(down_0, 0, 0), x_out(down_1, *FLIPS[1]), *got[2:]]
    part_other = other_core(part_give)
    blocks = call(
        attention_weight_body,
        "attention_weights",
        [at, a1, dqkv, db, o],
        [((512, 512), bf16)] * 8,
        [],
        2 * LEN * WIDTH * 1024,
    )
    part_keep, part_other, *got = lax.optimization_barrier((part_keep, part_other, *blocks, *got_down_a, *got_down_b))
    blocks, got_down_a, got_down_b = got[:8], got[8:12], got[12:]
    part_both = (part_keep.astype(f32) + part_other.astype(f32)).astype(bf16)
    attn_grad = lax.psum_scatter(part_both, Z, scatter_dimension=0, tiled=True).astype(f32)
    got_attn_a = [shift(blocks[1], Y, 1), shift(blocks[3], Y, 3)]
    got_attn_b = [x_out(blocks[4 + i], *FLIPS[i]) for i in (2, 3)]
    row_part = after(row_part, part_both)

    block_at = jnp.stack([((r // 4 - y) % 4) * 4 + ((r // 2 % 2) ^ lo) * 2 + ((r % 2) ^ hi) for r in range(16)])
    pick = (block_at[:, None] == jnp.arange(16)[None, :]).astype(f32)
    gain_parts = jnp.concatenate([gain_part.reshape(16, 128), grad_gain_two.reshape(16, 128)], 1)
    gain_parts = jnp.dot(pick, gain_parts, precision=lax.Precision.HIGHEST)
    peaks = jnp.where((jnp.arange(QUERY_HEADS) == mine)[:, None], peak, 0.0)
    small = jnp.concatenate([row_part.reshape(6, 128), gain_parts[:, :128], gain_parts[:, 128:], peaks], 0)
    is_peak = (jnp.arange(46) >= 38)[:, None]

    def join(values):
        total, most = values[0], values[0]
        for value in values[1:]:
            total, most = total + value, jnp.maximum(most, value)
        return jnp.where(is_peak[-total.shape[0] :], most, total)

    small = join([small, other_core(small)])
    small = join([small, z_other(small, 1)])

    rest = lax.optimization_barrier((blocks[2], blocks[4], blocks[5], small, got_up[2], *got_attn_a, *got_attn_b))
    (block_y, block_0, block_1, small, got_up[2]), got_attn_a, got_attn_b = rest[:5], rest[5:7], rest[7:]
    got_attn_a = [blocks[0], shift(block_y, Y, 2), *got_attn_a]
    got_attn_b = [x_out(block_0, 0, 0), x_out(block_1, *FLIPS[1]), *got_attn_b]
    out_late = after(out_both, part_both)
    ffn_a, ffn_b = call(
        ffn_sum_body,
        "feed_forward_sums",
        [at, *got_gate, *got_down_a, *got_up, *got_down_b, up_b[0], down_0],
        [((512, 1536), bf16)] * 2,
        [],
        0,
    )

    small = join([small, z_other(small, 2)])
    row_sum = small[:6].reshape(LEN, 1)
    small = small[6:]
    small = join([small, y_other(small, 1)])
    got_attn_a, got_attn_b, ffn_a, ffn_b, small, attn_grad = lax.optimization_barrier(
        (got_attn_a, got_attn_b, ffn_a, ffn_b, small, attn_grad)
    )
    sums = call(
        join_body,
        "join_sums",
        [at, ffn_a, ffn_b, *got_attn_a, *got_attn_b, block_0],
        [((128, WIDTH), bf16)] * 8,
        [],
        0,
    )
    sums_a, sums_b = sums[:4], sums[4:]
    sum_b = [shift(sums_b[i], Y, i) for i in (1, 3)]
    sum_a = [x_out(sums_a[i], *FLIPS[i]) for i in (2, 3)]
    small = join([small, y_other(small, 2)])
    small = join([small, x_ring(small, 1)])
    rest = lax.optimization_barrier((*sum_b, *sum_a, sums_b[2], sums_a[0], sums_a[1], small))
    sum_b, sum_a, (late_y, late_0, late_1, small) = rest[:2], rest[2:4], rest[4:]
    sum_b = [sums_b[0], shift(late_y, Y, 2), *sum_b]
    sum_a = [x_out(late_0, 0, 0), x_out(late_1, *FLIPS[1]), *sum_a]
    ffn_own = lax.psum_scatter(out_late, Z, scatter_dimension=0, tiled=True).astype(f32)
    ffn_own = after(ffn_own, small)

    gain_pair = jnp.dot(pick, gain_rows[0].reshape(16, 128), precision=lax.Precision.HIGHEST)
    gain_cols = lax.dynamic_slice(gain_pair, (mine * 2, 0), (2, 128)).reshape(1, HEAD)
    grad_inputs = (
        db_cols.astype(f32) + r1 * attn_grad * gain_cols - x_own.astype(f32) * r1**2 * (row_sum / WIDTH)
    )
    home = [(h_cols.astype(f32) + ffn_own).astype(bf16), grad_inputs.astype(bf16)]
    home = swap(jnp.concatenate(home, 0))
    small = join([small, x_ring(small, 2)])
    sum_a, sum_b, home, small = lax.optimization_barrier((sum_a, sum_b, home, small))
    kv_sum = total([own_or(sum_a[0], sums_a[0]), *sum_a[1:]], slice(1536, None))
    first_halves = jnp.concatenate([kv_sum[:, :half], kv_sum[:, HEAD : HEAD + half]], 1)
    second_halves = jnp.concatenate([kv_sum[:, half:HEAD], kv_sum[:, HEAD + half :]], 1)
    kv_done = jnp.where(odd, second_halves, first_halves) + kv_partner(
        jnp.where(odd, first_halves, second_halves).astype(bf16)
    ).astype(f32)
    grads = call(
        finish_body,
        "finish",
        [at, sums_a[0], *sum_a, *sum_b],
        [((128, FF), f32)] * 3 + [((128, HEAD), f32)] * 2,
        [],
        0,
    )
    tok = y * 4 + lo * 2 + core
    gains_mine = lax.dynamic_slice(small[:32].reshape(2, 16, 128), (0, tok, 0), (2, 1, 128)).reshape(2, 128)
    peaks = small[32:, 0]

    head = hi * 4 + z
    peak_q = lax.dynamic_slice(peaks, (head,), (1,))
    pair = lax.dynamic_slice(peaks, (head // 2 * 2,), (2,))
    scale_q = jnp.sqrt(logit_ceiling / (peak_q + peak_floor_epsilon))
    scale_k = jnp.sqrt(logit_ceiling / (jnp.max(pair, keepdims=True) + peak_floor_epsilon))
    clipped_query = (w_query.astype(f32) * scale_q[None, :]).astype(bf16)
    clipped_key = (w_key.astype(f32) * scale_k[None, :]).astype(bf16)
    return (
        home[:LEN],
        home[LEN:].astype(f32),
        gains_mine[0],
        grads[3],
        kv_done[:, :half],
        kv_done[:, half:],
        grads[4],
        gains_mine[1],
        grads[0],
        grads[1],
        grads[2],
        clipped_query,
        clipped_key,
    )


def solution(mesh):
    torus = Mesh(mesh.devices.reshape(4, 2, 2, 2, 4), (Y, XLO, CORE, XHI, Z))
    both, rows = P(TOK, MDL), P(TOK)
    return jax.shard_map(
        on_device,
        mesh=torus,
        in_specs=(both, P(TOK, None), rows, both, both, both, both, rows, both, both, both, both),
        out_specs=(both, both, rows, both, both, both, both, rows, both, both, both, both, both),
        check_vma=False,
    )
```

```python
import functools
import math

import jax
import jax.numpy as jnp
from jax import lax
from jax.experimental import pallas as pl
from jax.experimental.pallas import tpu as pltpu
from jax.sharding import Mesh
from jax.sharding import PartitionSpec as P

QUERY_HEADS = 8
HEAD = 256
WIDTH = 2048
LEN = 768
OWN = 96
FF = 1024
Y, XLO, CORE, XHI, Z = "tok_0", "tok_1", "tok_2", "mdl_0", "mdl_1"
TOK = (Y, XLO, CORE)
MDL = (XHI, Z)

norm_epsilon = 1e-06
rope_base = 1000042.0
logit_ceiling = 4.0
masked_value = -1e30
peak_floor_epsilon = 1e-06
SCALE = HEAD ** (-0.5)
nt = (((1,), (1,)), ((), ()))
tn = (((0,), (0,)), ((), ()))
f32 = jnp.float32
bf16 = jnp.bfloat16


def dot(a, b, dims=(((1,), (0,)), ((), ()))):
    return lax.dot_general(a, b, dims, preferred_element_type=f32)


def swap(a):
    got = lax.ppermute(a, (CORE, XHI), [(1, 2), (2, 1)])
    return jnp.where(lax.axis_index(CORE) == lax.axis_index(XHI), a, got)


def other_core(a):
    return lax.ppermute(a, CORE, [(0, 1), (1, 0)])


def shift(a, axis, by):
    return lax.ppermute(a, axis, [(i, (i + by) % 4) for i in range(4)])


def z_other(a, mask):
    return lax.ppermute(a, Z, [(i, i ^ mask) for i in range(4)])


def y_other(a, mask):
    return lax.ppermute(a, Y, [(i, i ^ mask) for i in range(4)])


def kv_partner(a):
    return lax.ppermute(a, Z, [(0, 1), (1, 0), (2, 3), (3, 2)])


def plane_pairs(flip_lo, flip_core):
    pairs = []
    for lo in range(2):
        for core in range(2):
            for hi in range(2):
                pairs.append((lo * 4 + core * 2 + hi, (lo ^ flip_lo) * 4 + hi * 2 + (core ^ flip_core)))
    return pairs


def x_pairs(flip_lo, flip_core, back):
    pairs = plane_pairs(flip_lo, flip_core)
    return [(there, here) if back else (here, there) for here, there in pairs if here != there]


def x_in(a, flip_lo, flip_core):
    return lax.ppermute(a, (XLO, CORE, XHI), x_pairs(flip_lo, flip_core, False))


def x_out(a, flip_lo, flip_core):
    return lax.ppermute(a, (XLO, CORE, XHI), x_pairs(flip_lo, flip_core, True))


def own_or(got, own):
    return jnp.where(lax.axis_index(CORE) == lax.axis_index(XHI), own, got)


FLIPS = ((0, 0), (0, 1), (1, 0), (1, 1))


def from_y(a):
    return [a, shift(a, Y, -1), shift(a, Y, 2), shift(a, Y, 1)]


def from_z(a):
    return [a, shift(a, Z, -1), shift(a, Z, 2), shift(a, Z, 1)]


def x_ring(a, mask):
    return lax.ppermute(a, (XLO, XHI), [(i, i ^ mask) for i in range(4)])


def total(pieces, cols=slice(None)):
    return sum(piece[:, cols].astype(f32) for piece in pieces)


def team_gather(own):
    return lax.all_gather(own, (CORE, Z), axis=0, tiled=True)


def team_scatter(give, keep):
    both = (keep.astype(f32) + other_core(give).astype(f32)).astype(bf16)
    return lax.psum_scatter(both, Z, scatter_dimension=0, tiled=True).astype(f32)


def after(value, *others):
    return lax.optimization_barrier((value, *others))[0]


def rope_tables(segment_row):
    earlier = jnp.sum((segment_row[None, :] < segment_row[:, None]).astype(jnp.int32), axis=1)
    places = jnp.arange(LEN, dtype=jnp.int32) - earlier
    half = HEAD // 2
    inverse = jnp.exp(jnp.arange(half, dtype=f32) * (-2.0 * math.log(rope_base) / HEAD))
    angles = places.astype(f32)[:, None] * inverse[None, :]
    return jnp.cos(angles), jnp.sin(angles)


def position(r, at):
    return (((r >> 2) - at[0]) & 3) * 4 + (((r >> 1) & 1) ^ at[1]) * 2 + ((r & 1) ^ at[2])


def lanes(index, size):
    return pl.ds(pl.multiple_of(index * size, size), size)


def owner(at, there, dz):
    return (at[3] ^ there) * 4 + ((at[4] + dz) & 3)


def kdot(a, b, dims=(((1,), (0,)), ((), ()))):
    return lax.dot_general(a, b, dims, preferred_element_type=f32)


def in_vmem(n):
    return [pl.BlockSpec(memory_space=pltpu.VMEM)] * n


def call(body, name, inputs, outs, scratch, flops, megabytes=56, anywhere=0, outs_anywhere=0, alias=0):
    moved = sum(v.size * v.dtype.itemsize for v in inputs[1:])
    moved += sum(math.prod(s) * jnp.dtype(d).itemsize for s, d in outs)
    specs = [pl.BlockSpec(memory_space=pltpu.SMEM)] + in_vmem(len(inputs) - 1 - anywhere)
    specs += [pl.BlockSpec(memory_space=pl.ANY)] * anywhere
    return list(pl.pallas_call(
        body,
        name=name,
        out_shape=[jax.ShapeDtypeStruct(s, d) for s, d in outs],
        in_specs=specs,
        out_specs=in_vmem(len(outs) - outs_anywhere) + [pl.BlockSpec(memory_space=pl.ANY)] * outs_anywhere,
        scratch_shapes=scratch,
        input_output_aliases={len(inputs) - alias + i: i for i in range(alias)},
        cost_estimate=pl.CostEstimate(flops=int(flops), bytes_accessed=int(moved), transcendentals=0),
        compiler_params=pltpu.CompilerParams(vmem_limit_bytes=megabytes * 2**20),
    )(*inputs))


def turn(values, cosine, sine):
    first, second = values[:, :128], values[:, 128:]
    return first * cosine - second * sine, second * cosine + first * sine


def attention_weights(a_refs, b_refs, w_qkv, w_o, sem):
    copies = []

    def move(source, to):
        copies.append(pltpu.make_async_copy(source, to, sem.at[len(copies)]))
        copies[-1].start()

    for i in range(4):
        for dy in range(4):
            rows = pl.ds((dy * 4 + i) * 128, 128)
            move(b_refs[i].at[pl.ds(dy * 144, 128), pl.ds(256, 256)], w_o.at[rows])
    for dy in range(4):
        for i in range(4):
            rows = pl.ds((dy * 4 + i) * 128, 128)
            move(b_refs[i].at[pl.ds(dy * 144, 128), pl.ds(0, 256)], w_qkv.at[rows, pl.ds(0, 256)])
            move(a_refs[dy].at[pl.ds(i * 128, 128)], w_qkv.at[rows, pl.ds(256, 512)])
    return copies


def along_y_body(at, *refs):
    riders, gain_one, gain_two = refs[:3]
    tokens, cotangent, w_query, w_output, w_up, w_down, out, mixed, sem = refs[3:]
    pairs = [
        (w_query, out.at[pl.ds(0, 128), pl.ds(0, 256)]),
        (w_output, out.at[pl.ds(0, 128), pl.ds(256, 256)]),
        (w_up.at[:, pl.ds(0, 512)], out.at[pl.ds(144, 128)]),
        (w_up.at[:, pl.ds(512, 512)], out.at[pl.ds(272, 128)]),
        (w_down.at[:, pl.ds(512, 512)], out.at[pl.ds(400, 128)]),
        (tokens, mixed.at[pl.ds(0, 768)]),
        (cotangent, mixed.at[pl.ds(784, 768)]),
    ]
    copies = [pltpu.make_async_copy(a, b, sem.at[i]) for i, (a, b) in enumerate(pairs)]
    for copy in copies:
        copy.start()
    row = lax.broadcasted_iota(jnp.int32, (16, 128), 0)
    gains = jnp.where(row == 0, gain_one[...], jnp.where(row == 1, gain_two[...], 0.0))
    out[128:144, :128] = gains.astype(bf16)
    out[128:144, 128:] = jnp.zeros((16, 384), bf16)
    mixed[768:784, :] = riders[...]
    for copy in copies:
        copy.wait()


def along_x_body(at, *refs):
    key, value, other, w_gate, w_down, out, sem = refs
    pairs = [
        (w_gate.at[:, pl.ds(0, 512)], out.at[pl.ds(128, 128)]),
        (w_gate.at[:, pl.ds(512, 512)], out.at[pl.ds(256, 128)]),
        (w_down.at[:, pl.ds(0, 512)], out.at[pl.ds(384, 128)]),
    ]
    copies = [pltpu.make_async_copy(a, b, sem.at[i]) for i, (a, b) in enumerate(pairs)]
    for copy in copies:
        copy.start()
    odd = at[4] & 1
    out[:128, lanes(odd, 128)] = key[...]
    out[:128, lanes(1 - odd, 128)] = other[:, :128]
    out[:128, lanes(2 + odd, 128)] = value[...]
    out[:128, lanes(3 - odd, 128)] = other[:, 128:]
    for copy in copies:
        copy.wait()


def pack_body(at, *refs):
    xs, ys, to_y, to_x, sem = refs[:4], refs[4:8], refs[8], refs[9], refs[10]
    pairs = [(ref.at[pl.ds(0, 128)], to_y.at[pl.ds(128 * i, 128)]) for i, ref in enumerate(xs)]
    pairs += [(ref.at[pl.ds(0, 144)], to_x.at[pl.ds(144 * i, 144)]) for i, ref in enumerate(ys)]
    copies = [pltpu.make_async_copy(a, b, sem.at[i]) for i, (a, b) in enumerate(pairs)]
    for copy in copies:
        copy.start()
    for copy in copies:
        copy.wait()


def riders_body(at, *refs):
    xs, ys = refs[:4], refs[4:8]
    a_wide, b_wide, a_down, b_down, sem = refs[8:]
    copies = []
    for ref, row, wide, down in [(xs, 128, a_wide, a_down), (ys, 144, b_wide, b_down)]:
        for i in range(4):
            for j in range(3):
                source = ref[i].at[pl.ds(row + j * 128, 128)]
                rows = pl.ds(i * 128, 128)
                to = down.at[rows] if j == 2 else wide.at[rows, pl.ds(j * 512, 512)]
                copies.append(pltpu.make_async_copy(source, to, sem.at[len(copies)]))
    for copy in copies:
        copy.start()
    for copy in copies:
        copy.wait()


def allowed_block(i, seg_col, seg_row):
    rows, cols = 256, (i + 1) * 256
    same = seg_col[i * 256 : (i + 1) * 256, :] == seg_row[:, :cols]
    row = i * 256 + lax.broadcasted_iota(jnp.int32, (rows, cols), 0)
    return same & (row >= lax.broadcasted_iota(jnp.int32, (rows, cols), 1))


def forward_body(at, *refs):
    x, cosine, sine, seg_row, seg_col = refs[:5]
    a_refs, b_refs = refs[5:9], refs[9:13]
    a1, r1, x_mine, qr, kr, v, o, lse, peak, gains, give, keep = refs[13:25]
    w_qkv, w_o, gain_rows, sem, gain_sem = refs[25:]
    gain_copies = []
    for dy in range(4):
        for i in range(4):
            source = b_refs[i].at[pl.ds(dy * 144 + 128, 16), pl.ds(0, 128)]
            to = gain_rows.at[:, pl.ds((dy * 4 + i) * 128, 128)]
            gain_copies.append(pltpu.make_async_copy(source, to, gain_sem.at[len(gain_copies)]))
            gain_copies[-1].start()
    copies = attention_weights(a_refs, b_refs, w_qkv, w_o, sem)
    for copy in gain_copies:
        copy.wait()
    gains[...] = gain_rows[...].astype(f32)[:8]
    own = at[3] * 4 + at[4]
    for r in range(16):
        rows = pl.ds(pl.multiple_of((r // 2) * LEN + own * OWN, OWN), OWN)
        x_mine[:, lanes(position(r, at), 128)] = x[rows, (r % 2) * 128 : (r % 2 + 1) * 128]

    def norm(step, carry):
        rows = pl.ds(pl.multiple_of(step * 128, 128), 128)
        total = jnp.zeros((128, 1), f32)
        for m in range(8):
            value = x[pl.ds(pl.multiple_of(m * LEN + step * 128, 128), 128), :].astype(f32)
            total = total + jnp.sum(value * value, axis=1, keepdims=True)
        factor = lax.rsqrt(total / WIDTH + norm_epsilon)
        r1[rows, :] = factor
        for r in range(16):
            at_lanes = lanes(position(r, at), 128)
            from_rows = pl.ds(pl.multiple_of((r // 2) * LEN + step * 128, 128), 128)
            value = x[from_rows, (r % 2) * 128 : (r % 2 + 1) * 128].astype(f32)
            a1[rows, at_lanes] = (value * factor * gains[0:1, at_lanes]).astype(bf16)
        return carry

    lax.fori_loop(0, 6, norm, 0)
    for copy in copies:
        copy.wait()
    for i in range(3):
        rows = slice(i * 256, (i + 1) * 256)
        qk = kdot(a1[rows, :], w_qkv[:, :512])
        cos_i, sin_i = cosine[rows, :], sine[rows, :]
        for ref, at_col in ((qr, 0), (kr, 256)):
            one, two = turn(qk[:, at_col : at_col + 256], cos_i, sin_i)
            ref[rows, :128] = one.astype(bf16)
            ref[rows, 128:] = two.astype(bf16)
        v[rows, :] = kdot(a1[rows, :], w_qkv[:, 512:]).astype(bf16)
    largest = jnp.zeros((1, 1), f32)
    for i in range(3):
        rows, cols = slice(i * 256, (i + 1) * 256), (i + 1) * 256
        allowed = allowed_block(i, seg_col, seg_row)
        scores = kdot(qr[rows, :], kr[:cols, :], nt) * SCALE
        masked = jnp.where(allowed, scores, masked_value)
        size = jnp.where(allowed, jnp.abs(scores), 0.0)
        largest = jnp.maximum(largest, jnp.max(jnp.max(size, axis=1, keepdims=True), axis=0, keepdims=True))
        top = jnp.max(masked, axis=1, keepdims=True)
        log_total = top + jnp.log(jnp.sum(jnp.exp(masked - top), axis=1, keepdims=True))
        lse[rows, :] = log_total
        probs = jnp.exp(masked - log_total).astype(bf16)
        o[rows, :] = kdot(probs, v[:cols, :]).astype(bf16)
    peak[...] = jnp.broadcast_to(largest, (8, 128))
    for ref, c in ((give, 1 - at[3]), (keep, at[3])):
        rows = pl.ds(pl.multiple_of(c * 384, 384), 384)
        for half in range(2):
            cols = slice(half * 1024, (half + 1) * 1024)
            ref[:, cols] = kdot(o[rows, :], w_o[cols, :], nt).astype(bf16)


def reorder_body(at, whole, out):
    for r in range(16):
        rows = slice((r // 2) * LEN, (r // 2 + 1) * LEN)
        out[:, lanes(position(r, at), 128)] = whole[rows, (r % 2) * 128 : (r % 2 + 1) * 128]


def start_either(at, own, got, to, sem):
    mine = at[2] == at[3]

    @pl.when(mine)
    def _():
        pltpu.make_async_copy(own, to, sem).start()

    @pl.when(jnp.logical_not(mine))
    def _():
        pltpu.make_async_copy(got, to, sem).start()

    return pltpu.make_async_copy(got, to, sem)


def rows_a(refs, to_ref, cols, sem, copies):
    row = 0
    for ref in refs:
        to = to_ref.at[pl.ds(row, ref.shape[0]), cols]
        row += ref.shape[0]
        copies.append(pltpu.make_async_copy(ref, to, sem.at[len(copies)]))
        copies[-1].start()


def rows_b(at, own, refs, to_ref, cols, sem, copies):
    for i, ref in enumerate(refs):
        for j in range(4):
            to = to_ref.at[pl.ds((j * 4 + i) * 128, 128), cols]
            rows = pl.ds(j * 128, 128)
            if i == 0:
                copies.append(start_either(at, own.at[rows], ref.at[rows], to, sem.at[len(copies)]))
            else:
                copies.append(pltpu.make_async_copy(ref.at[rows], to, sem.at[len(copies)]))
                copies[-1].start()


def ffn_body(at, *refs):
    gains, h_in, dy_in = refs[:3]
    wide_a, (down_a, wide_b, down_b) = refs[3:8], [refs[8 + 4 * i : 12 + 4 * i] for i in range(3)]
    own_wide, own_down = refs[20:22]
    h_cols, a2_out, hid_out, dgate_out, dup_out, give_out, keep_out = refs[22:29]
    up_outs, gate_outs = refs[29:31], refs[31:33]
    h, dy, a2, hid, dgate, dup, give, keep, up_0, up_1, gate_0, gate_1 = refs[33:45]
    w_gate, w_up, w_down, sem, out_sem = refs[45:]
    h_copy = pltpu.make_async_copy(h_in, h, out_sem.at[14])
    h_copy.start()
    copies = []
    rows_a(wide_a, w_gate, pl.ds(0, FF), sem, copies)
    rows_b(at, own_wide, wide_b, w_up, pl.ds(0, FF), sem, copies)
    rows_a(down_a, w_down, pl.ds(0, 512), sem, copies)
    rows_b(at, own_down, down_b, w_down, pl.ds(512, 512), sem, copies)
    copies.append(pltpu.make_async_copy(dy_in, dy, out_sem.at[15]))
    copies[-1].start()
    sent = []

    def send(source, to):
        sent.append(pltpu.make_async_copy(source, to, out_sem.at[len(sent)]))
        sent[-1].start()

    h_copy.wait()
    own = at[3] * 4 + at[4]
    for j in range(2):
        h_cols[:, j * 128 : (j + 1) * 128] = h[:, lanes(position(2 * own + j, at), 128)]
    for i in range(6):
        rows = slice(i * 128, (i + 1) * 128)
        value = h[rows, :].astype(f32)
        factor = lax.rsqrt(jnp.mean(value * value, axis=1, keepdims=True) + norm_epsilon)
        a2[rows, :] = (value * factor * gains[1:2, :]).astype(bf16)
    send(a2, a2_out)
    for copy in copies:
        copy.wait()
    for half in range(2):
        rows = slice(half * 384, (half + 1) * 384)
        for j in range(4):
            cols = slice(j * 256, (j + 1) * 256)
            gate = kdot(a2[rows, :], w_gate[:, cols])
            up = kdot(a2[rows, :], w_up[:, cols])
            grad = kdot(dy[rows, :], w_down[:, cols])
            sig = 1.0 / (1.0 + jnp.exp(-gate))
            act = gate * sig
            hid[rows, cols] = (act * up).astype(bf16)
            dgate[rows, cols] = (grad * up * sig * (1.0 + gate * (1.0 - sig))).astype(bf16)
            dup[rows, cols] = (grad * act).astype(bf16)
    for source, to in ((hid, hid_out), (dgate, dgate_out), (dup, dup_out)):
        send(source, to)
    for ref, to, c in ((give, give_out, 1 - at[3]), (keep, keep_out, at[3])):
        rows = pl.ds(pl.multiple_of(c * 384, 384), 384)
        for j in range(4):
            cols = slice(j * 512, (j + 1) * 512)
            ref[:, cols] = (
                kdot(dgate[rows, :], w_gate[cols, :], nt) + kdot(dup[rows, :], w_up[cols, :], nt)
            ).astype(bf16)
        send(ref, to)
    for i, ref, to in ((1, gate_0, gate_outs[0]), (3, gate_1, gate_outs[1])):
        for j in range(2):
            n = slice(j * 512, (j + 1) * 512)
            ref[:, n] = kdot(a2[:, i * 512 : (i + 1) * 512], dgate[:, n], tn).astype(bf16)
        send(ref, to)
    for i in range(4):
        cols = slice((i * 4 + 2) * 128, (i * 4 + 4) * 128)
        for j in range(2):
            n = slice(j * 512, (j + 1) * 512)
            value = kdot(a2[:, cols], dup[:, n], tn).astype(bf16)
            up_0[i * 128 : (i + 1) * 128, n] = value[:128]
            up_1[i * 128 : (i + 1) * 128, n] = value[128:]
    send(up_0, up_outs[0])
    send(up_1, up_outs[1])
    for copy in sent:
        copy.wait()


def ffn_out_body(at, hid, *refs):
    down_a, down_b, own_down = refs[:4], refs[4:8], refs[8]
    give, keep, w_down, sem = refs[9:]
    copies = []
    rows_a(down_a, w_down, pl.ds(0, 512), sem, copies)
    rows_b(at, own_down, down_b, w_down, pl.ds(512, 512), sem, copies)
    for copy in copies:
        copy.wait()
    for ref, c in ((give, 1 - at[3]), (keep, at[3])):
        for dz in range(4):
            m = c * 4 + dz
            pair = pl.ds(pl.multiple_of((position(2 * m, at) >> 1) * 256, 256), 256)
            value = kdot(hid[...], w_down[pair, :], nt)
            rows = slice(dz * LEN, (dz + 1) * LEN)
            for j in range(2):
                ref[rows, lanes(at[2] ^ j, 128)] = value[:, j * 128 : (j + 1) * 128].astype(bf16)


def weight_rest_body(at, a2, dy, dgate, dup, hid, *outs):
    a_wide, b_wide, a_down, b_down = outs[:2], outs[2:4], outs[4:8], outs[8:]
    for i in range(4):
        cols, rows = slice(i * 512, (i + 1) * 512), slice(i * 128, (i + 1) * 128)
        for j in range(2):
            n = slice(j * 512, (j + 1) * 512)
            value = kdot(a2[:, i * 512 : i * 512 + 256], dup[:, n], tn).astype(bf16)
            for k in range(2):
                b_wide[k][rows, n] = value[k * 128 : (k + 1) * 128]
            if i % 2 == 0:
                a_wide[i // 2][:, n] = kdot(a2[:, cols], dgate[:, n], tn).astype(bf16)
        a_down[i][...] = kdot(dy[:, cols], hid[:, :512], tn).astype(bf16)
        value = kdot(dy[:, cols], hid[:, 512:], tn).astype(bf16)
        for k in range(4):
            b_down[k][rows, :] = value[k * 128 : (k + 1) * 128]


def backward_body(at, *refs):
    db, cosine, sine, seg_row, seg_col, qr, kr, v, lse, a1, gains = refs[:11]
    a_refs, b_refs = refs[11:15], refs[15:19]
    db_cols, dqkv, row_part, gain_part, give, keep = refs[19:25]
    w_qkv, w_o, d_o, dk_sum, dv_sum, sem = refs[25:]
    copies = attention_weights(a_refs, b_refs, w_qkv, w_o, sem)
    own = at[3] * 4 + at[4]
    for j in range(2):
        db_cols[:, j * 128 : (j + 1) * 128] = db[:, lanes(position(2 * own + j, at), 128)]
    for copy in copies:
        copy.wait()
    for i in range(3):
        rows = slice(i * 256, (i + 1) * 256)
        d_o[rows, :] = kdot(db[rows, :], w_o[...]).astype(bf16)
    for i in (2, 1, 0):
        rows, cols = slice(i * 256, (i + 1) * 256), (i + 1) * 256
        allowed = allowed_block(i, seg_col, seg_row)
        scores = kdot(qr[rows, :], kr[:cols, :], nt) * SCALE
        probs = jnp.exp(jnp.where(allowed, scores, masked_value) - lse[rows, :])
        low = probs.astype(bf16)
        dp = kdot(d_o[rows, :], v[:cols, :], nt)
        delta = jnp.sum(dp * probs, axis=1, keepdims=True)
        ds = (probs * (dp - delta)).astype(bf16)
        dq = kdot(ds, kr[:cols, :]) * SCALE
        row_part[rows, :] = jnp.sum(dq * qr[rows, :].astype(f32), axis=1, keepdims=True)
        one, two = turn(dq, cosine[rows, :], -sine[rows, :])
        dqkv[rows, :128] = one.astype(bf16)
        dqkv[rows, 128:256] = two.astype(bf16)
        dk_new = kdot(ds, qr[rows, :], tn)
        dv_new = kdot(low, d_o[rows, :], tn)
        if i == 2:
            dk_sum[...] = dk_new
            dv_sum[...] = dv_new
        else:
            dk_sum[:cols, :] = dk_sum[:cols, :] + dk_new
            dv_sum[:cols, :] = dv_sum[:cols, :] + dv_new
    for i in range(3):
        rows = slice(i * 256, (i + 1) * 256)
        dk = dk_sum[rows, :] * SCALE
        dv_i = dv_sum[rows, :]
        row_part[rows, :] = (
            row_part[rows, :]
            + jnp.sum(dk * kr[rows, :].astype(f32), axis=1, keepdims=True)
            + jnp.sum(dv_i * v[rows, :].astype(f32), axis=1, keepdims=True)
        )
        one, two = turn(dk, cosine[rows, :], -sine[rows, :])
        dqkv[rows, 256:384] = one.astype(bf16)
        dqkv[rows, 384:512] = two.astype(bf16)
        dqkv[rows, 512:] = dv_i.astype(bf16)
    for m, ref in [(j, give) for j in range(4)] + [(j, keep) for j in range(4)]:
        half = 1 - at[3] if ref is give else at[3]
        pair = lanes(position(2 * (half * 4 + m), at) >> 1, 256)
        value = kdot(dqkv[...], w_qkv[pair, :], nt)
        gain_part[:, pair] = jnp.sum(value * a1[:, pair].astype(f32), axis=0, keepdims=True) / gains[0:1, pair]
        rows = slice(m * LEN, (m + 1) * LEN)
        for j in range(2):
            ref[rows, lanes(at[2] ^ j, 128)] = value[:, j * 128 : (j + 1) * 128].astype(bf16)


def attention_weight_body(at, a1, dqkv, db, o, *refs):
    outs, values, sem = refs[:8], refs[8:16], refs[16]
    for i in range(4):
        cols, rows = slice(i * 512, (i + 1) * 512), slice(i * 128, (i + 1) * 128)
        values[i][...] = kdot(a1[:, cols], dqkv[:, 256:], tn).astype(bf16)
        for n, left, right in ((slice(0, 256), a1, dqkv.at[:, :256]), (slice(256, 512), db, o)):
            value = kdot(left[:, cols], right[...], tn).astype(bf16)
            for k in range(4):
                values[4 + k][rows, n] = value[k * 128 : (k + 1) * 128]
    copies = [pltpu.make_async_copy(v, o_.at[pl.ds(0, 512)], sem.at[i]) for i, (v, o_) in enumerate(zip(values, outs))]
    for copy in copies:
        copy.start()
    for copy in copies:
        copy.wait()


def ffn_sum_body(row, at, *refs):
    a, b, own, outs, values, sem = refs[:4], refs[4:8], refs[8], refs[17:25], refs[25:33], refs[33]
    mine = at[2] == at[3]
    copies = []
    for i in range(4):
        rows = slice(i * 128, (i + 1) * 128)
        head = jnp.where(mine, own[rows, :], b[0][rows, :])
        for value, terms in ((values[i], [b[k][rows, :] for k in (1, 2, 3)]), (values[4 + i], [a[k][rows, :] for k in (1, 2, 3)])):
            first = head if value is values[i] else a[0][rows, :]
            total = first.astype(f32) + terms[0].astype(f32) + terms[1].astype(f32) + terms[2].astype(f32)
            for j in range(total.shape[1] // 512):
                value[j * 128 : (j + 1) * 128, :] = total[:, j * 512 : (j + 1) * 512].astype(bf16)
    for i in range(8):
        to = outs[i].at[pl.ds(row, values[i].shape[0])]
        copies.append(pltpu.make_async_copy(values[i], to, sem.at[i]))
        copies[-1].start()
    for copy in copies:
        copy.wait()


def join_body(at, *refs):
    a, b, own, outs = refs[:4], refs[4:8], refs[8], refs[9:13]
    kv_give, kv_keep, va, vb, v_own, sem = refs[13], refs[14], refs[15:19], refs[19:23], refs[23], refs[24]
    pairs = list(zip([*a, *b, own], [*va, *vb, v_own]))
    copies = [pltpu.make_async_copy(x.at[pl.ds(0, 512)], v, sem.at[i]) for i, (x, v) in enumerate(pairs)]
    for copy in copies:
        copy.start()
    for copy in copies:
        copy.wait()
    odd = (at[4] & 1) == 1
    for i in range(4):
        rows = slice(i * 128, (i + 1) * 128)
        head = jnp.where(at[2] == at[3], v_own[rows, :], vb[0][rows, :])
        value = head.astype(f32) + vb[1][rows, :].astype(f32) + vb[2][rows, :].astype(f32) + vb[3][rows, :].astype(f32)
        outs[i][...] = value.astype(bf16)
        value = va[0][rows, :].astype(f32) + va[1][rows, :].astype(f32) + va[2][rows, :].astype(f32) + va[3][rows, :].astype(f32)
        for half in range(2):
            one, two = value[:, half * 256 : half * 256 + 128], value[:, half * 256 + 128 : (half + 1) * 256]
            n = slice(half * 128, (half + 1) * 128)
            kv_keep[rows, n] = jnp.where(odd, two, one)
            kv_give[rows, n] = jnp.where(odd, one, two).astype(bf16)


def finish_body(at, *refs):
    a, b, own = refs[:4], refs[4:8], refs[8]
    gate, up, down, va, vb, v_own, sem = refs[9], refs[10], refs[11], refs[12:16], refs[16:20], refs[20], refs[21]
    pairs = list(zip([*a, *b, own], [*va, *vb, v_own]))
    copies = [pltpu.make_async_copy(x.at[pl.ds(512, 384)], v, sem.at[i]) for i, (x, v) in enumerate(pairs)]
    for copy in copies:
        copy.start()
    for copy in copies:
        copy.wait()
    mine = at[2] == at[3]
    for j in range(3):
        rows = slice(j * 128, (j + 1) * 128)
        head = jnp.where(mine, v_own[rows, :], vb[0][rows, :])
        of_a = head.astype(f32) + vb[1][rows, :].astype(f32) + vb[2][rows, :].astype(f32) + vb[3][rows, :].astype(f32)
        of_b = va[0][rows, :].astype(f32) + va[1][rows, :].astype(f32) + va[2][rows, :].astype(f32) + va[3][rows, :].astype(f32)
        if j < 2:
            gate[:, j * 512 : (j + 1) * 512] = of_a
            up[:, j * 512 : (j + 1) * 512] = of_b
        else:
            down[:, :512] = of_a
            down[:, 512:] = of_b


def on_device(
    tokens,
    segments,
    gain_attn,
    w_query,
    w_key,
    w_value,
    w_output,
    gain_ffn,
    w_gate,
    w_up,
    w_down,
    cotangent,
):
    y, lo, core = lax.axis_index(Y), lax.axis_index(XLO), lax.axis_index(CORE)
    hi, z = lax.axis_index(XHI), lax.axis_index(Z)
    at = jnp.stack([y, lo, hi, core, z]).astype(jnp.int32)
    mine = core * 4 + z

    riders = jnp.zeros((16, HEAD), bf16).at[:3].set(segments.reshape(3, HEAD).astype(bf16))
    hf = FF // 2
    odd = z % 2 == 1
    half = HEAD // 2
    kv_other = kv_partner(jnp.concatenate([w_key, w_value], 1))
    y_rows, mixed = call(
        along_y_body,
        "lay_out_y",
        [
            at,
            riders,
            gain_attn.astype(f32).reshape(1, 128),
            gain_ffn.astype(f32).reshape(1, 128),
            tokens,
            cotangent,
            w_query,
            w_output,
            w_up,
            w_down,
        ],
        [((528, 2 * HEAD), bf16), ((1552, HEAD), bf16)],
        [pltpu.SemaphoreType.DMA((7,))],
        0,
        anywhere=6,
    )
    (x_rows,) = call(
        along_x_body,
        "lay_out_x",
        [at, w_key, w_value, kv_other, w_gate, w_down],
        [((512, 2 * HEAD), bf16)],
        [pltpu.SemaphoreType.DMA((3,))],
        0,
        anywhere=2,
    )
    got = swap(mixed)
    along_y = [shift(y_rows, Y, -1), shift(y_rows, Y, 1)]
    along_x = [x_in(x_rows, *flip) for flip in FLIPS[2:]]
    got, late_y, late_x, *rest = lax.optimization_barrier((got, y_rows, x_rows, *along_y, *along_x))
    along_y = [y_rows, rest[0], shift(late_y, Y, 2), rest[1]]
    along_x = [own_or(x_in(late_x, 0, 0), x_rows), x_in(late_x, *FLIPS[1]), *rest[2:]]
    rest = lax.optimization_barrier((*along_x, *along_y))
    to_y, to_x = call(
        pack_body,
        "pack",
        [at, *rest],
        [((512, 2 * HEAD), bf16), ((576, 2 * HEAD), bf16)],
        [pltpu.SemaphoreType.DMA((8,))],
        0,
        anywhere=8,
    )
    a_wide, b_wide, a_down, b_down = call(
        riders_body,
        "riders",
        [at, *rest],
        [((512, FF), bf16)] * 2 + [((512, hf), bf16)] * 2,
        [pltpu.SemaphoreType.DMA((24,))],
        0,
        anywhere=8,
    )
    x_own = got[:LEN]
    x_all = team_gather(x_own)
    upstream = team_gather(after(got[784:1552], to_x))
    segment_row = got[LEN : LEN + 3].astype(f32).reshape(1, LEN)
    segment_col = segment_row.reshape(LEN, 1)
    cosine, sine = rope_tables(segment_row[0])
    first = [shift(to_y, Y, -1), shift(to_y, Y, 1)]
    second = [x_in(to_x, *flip) for flip in FLIPS[2:]]
    late_y, late_x, *rest = lax.optimization_barrier((to_y, to_x, *first, *second))
    first, second = rest[:2], rest[2:]
    first = [to_y, first[0], shift(late_y, Y, 2), first[1]]
    second = [own_or(x_in(late_x, 0, 0), to_x), x_in(late_x, *FLIPS[1])] + second
    x_all, cosine, sine, segment_row, segment_col, *rest = lax.optimization_barrier(
        (x_all, cosine, sine, segment_row, segment_col, *first, *second, a_wide, b_wide, a_down, b_down)
    )
    first, second, (a_wide, b_wide, a_down, b_down) = rest[:4], rest[4:8], rest[8:]
    wide_a = [shift(a_wide, Y, -1), shift(a_wide, Y, 1)]
    wide_b = [x_in(b_wide, *flip) for flip in FLIPS[2:]]

    part = ((LEN // 2, WIDTH), bf16)
    act, low, col = ((LEN, WIDTH), bf16), ((LEN, HEAD), bf16), ((LEN, 1), f32)
    a1, r1, x_mine, qr, kr, v, o, lse, peak, gain_rows, give, keep = call(
        forward_body,
        "attention_forward",
        [at, x_all, cosine, sine, segment_row, segment_col, *first, *second],
        [act, col, ((OWN, WIDTH), bf16), low, low, low, low, col, ((8, 128), f32), ((8, WIDTH), f32), part, part],
        [
            pltpu.VMEM((WIDTH, 3 * HEAD), bf16),
            pltpu.VMEM((WIDTH, HEAD), bf16),
            pltpu.VMEM((16, WIDTH), bf16),
            pltpu.SemaphoreType.DMA((48,)),
            pltpu.SemaphoreType.DMA((16,)),
        ],
        2 * LEN * WIDTH * 1024,
        anywhere=8,
    )
    give, keep, upstream, *done = lax.optimization_barrier(
        (give, keep, upstream, *wide_a, *wide_b, a_wide, b_wide, a_down, b_down)
    )
    wide_a, wide_b, (a_wide, b_wide, a_down, b_down) = done[:2], done[2:4], done[4:]
    attn_own = team_scatter(give, keep)
    halves = [shift(wide_a[0][:256], Y, -1), shift(wide_a[1][256:], Y, 1)]
    wide_a = [a_wide, wide_a[0], *halves, wide_a[1]]
    wide_b = [x_in(b_wide, *flip) for flip in FLIPS[:2]] + wide_b
    down_a = [shift(a_down, Y, -1), shift(a_down, Y, 1)]
    (dy,) = call(reorder_body, "order_upstream", [at, upstream], [((LEN, WIDTH), bf16)], [], 0)


    attn_own, dy, *done = lax.optimization_barrier((attn_own, dy, *wide_a, *wide_b, *down_a, b_wide, a_down, b_down))
    wide_a, wide_b, down_a, (b_wide, a_down, b_down) = done[:5], done[5:9], done[9:11], done[11:]
    down_b = [x_in(b_down, *flip) for flip in FLIPS]
    down_a = [a_down, down_a[0], shift(a_down, Y, 2), down_a[1]]
    hidden_own = x_mine.astype(f32) + attn_own
    hidden = team_gather(hidden_own.astype(bf16))
    wide = ((LEN, FF), bf16)
    block = ((512, FF), bf16)
    h_cols, a2, hid, dgate, dup, give, keep, up_2, up_3, gate_1, gate_3 = call(
        ffn_body,
        "feed_forward",
        [at, gain_rows, hidden, dy, *wide_a, *down_a, *wide_b, *down_b, b_wide, b_down],
        [low, act, wide, wide, wide, part, part, block, block, block, block],
        [
            *[pltpu.VMEM(*v) for v in (act, act, act, wide, wide, wide, part, part, block, block, block, block)],
            pltpu.VMEM((WIDTH, FF), bf16),
            pltpu.VMEM((WIDTH, FF), bf16),
            pltpu.VMEM((WIDTH, FF), bf16),
            pltpu.SemaphoreType.DMA((44,)),
            pltpu.SemaphoreType.DMA((16,)),
        ],
        14 * LEN * WIDTH * FF,
        anywhere=21,
        outs_anywhere=10,
    )
    other = other_core(give)
    wide_out, stack = ((512, FF), bf16), ((4 * LEN, HEAD), bf16)
    work = 2 * LEN * WIDTH * FF
    both = (keep.astype(f32) + other.astype(f32)).astype(bf16)
    normed_grad = lax.psum_scatter(both, Z, scatter_dimension=0, tiled=True).astype(f32)
    dgate, dup, hid = lax.optimization_barrier((dgate, dup, hid, both))[:3]
    got_up = [x_out(up_2, *FLIPS[2]), x_out(up_3, *FLIPS[3])]
    got_gate = [shift(gate_1, Y, 1), shift(gate_3, Y, 3)]
    rest = call(
        weight_rest_body,
        "weight_rest",
        [at, a2, dy, dgate, dup, hid],
        [wide_out] * 4 + [((512, hf), bf16)] * 8,
        [],
        work * 2,
    )
    out_give, out_keep = call(
        ffn_out_body,
        "feed_forward_out",
        [at, after(hid, rest[0]), *down_a, *down_b, b_down],
        [stack, stack],
        [pltpu.VMEM((WIDTH, FF), bf16), pltpu.SemaphoreType.DMA((20,))],
        work,
        anywhere=9,
    )
    normed_grad, out_give, out_keep, *got = lax.optimization_barrier(
        (normed_grad, out_give, out_keep, *got_up, *got_gate, *rest)
    )
    got_up, got_gate, gate_b, up_b = [got[2 * i : 2 * i + 2] for i in range(4)]
    down_g = got[8:]

    gain_two = gain_rows[1:2]
    factor_own = lax.rsqrt(jnp.mean(hidden_own * hidden_own, axis=1, keepdims=True) + norm_epsilon)
    grad_gain_two = jnp.sum(normed_grad * hidden_own * factor_own, axis=0)
    scaled = normed_grad * gain_two
    grad_res = (
        lax.dynamic_slice_in_dim(dy, mine * OWN, OWN, 0).astype(f32)
        + factor_own * scaled
        - hidden_own * factor_own**3 * jnp.mean(scaled * hidden_own, axis=1, keepdims=True)
    )
    grad_low = grad_res.astype(bf16)
    db = team_gather(grad_low)
    got_gate = [gate_b[0], shift(gate_b[1], Y, 2)] + got_gate
    got_up = [x_out(up_b[0], 0, 0), x_out(up_b[1], *FLIPS[1])] + got_up
    out_both = (out_keep.astype(f32) + other_core(out_give).astype(f32)).astype(bf16)
    db, out_both, *got = lax.optimization_barrier((db, out_both, *got_gate, *got_up, *down_g))
    got_gate, got_up, down_g = got[:4], got[4:8], got[8:]
    got_down_a = [shift(down_g[1], Y, 1), shift(down_g[3], Y, 3)]
    got_down_b = [x_out(block, *flip) for block, flip in zip(down_g[6:], FLIPS[2:])]

    db_cols, dqkv, row_part, gain_part, part_give, part_keep = call(
        backward_body,
        "attention_backward",
        [at, db, cosine, sine, segment_row, segment_col, qr, kr, v, lse, a1, gain_rows, *first, *second],
        [low, ((LEN, 3 * HEAD), bf16), col, ((1, WIDTH), f32), stack, stack],
        [
            pltpu.VMEM((WIDTH, 3 * HEAD), bf16),
            pltpu.VMEM((WIDTH, HEAD), bf16),
            pltpu.VMEM((LEN, HEAD), bf16),
            pltpu.VMEM((LEN, HEAD), f32),
            pltpu.VMEM((LEN, HEAD), f32),
            pltpu.SemaphoreType.DMA((48,)),
        ],
        2 * LEN * WIDTH * 1024,
        anywhere=8,
    )
    part_give, part_keep, dqkv, down_y, down_0, down_1, *got = lax.optimization_barrier(
        (part_give, part_keep, dqkv, down_g[2], down_g[4], down_g[5], *got_down_a, *got_down_b)
    )
    got_down_a = [down_g[0], shift(down_y, Y, 2), *got[:2]]
    got_down_b = [x_out(down_0, 0, 0), x_out(down_1, *FLIPS[1]), *got[2:]]
    part_other = other_core(part_give)
    message = ((896, 512), bf16)
    blocks = call(
        attention_weight_body,
        "attention_weights",
        [at, a1, dqkv, db, o],
        [message] * 8,
        [pltpu.VMEM((512, 512), bf16)] * 8 + [pltpu.SemaphoreType.DMA((8,))],
        2 * LEN * WIDTH * 1024,
        outs_anywhere=8,
    )
    blocks = call(
        functools.partial(ffn_sum_body, 512),
        "feed_forward_sums_wide",
        [at, *got_gate, *got_up, up_b[0], *blocks],
        [message] * 8,
        [pltpu.VMEM((256, 512), bf16)] * 8 + [pltpu.SemaphoreType.DMA((8,))],
        0,
        anywhere=8,
        outs_anywhere=8,
        alias=8,
    )
    part_keep, part_other, *got = lax.optimization_barrier((part_keep, part_other, *blocks, *got_down_a, *got_down_b))
    blocks, got_down_a, got_down_b = got[:8], got[8:12], got[12:]
    blocks = call(
        functools.partial(ffn_sum_body, 768),
        "feed_forward_sums_down",
        [at, *got_down_a, *got_down_b, down_0, *blocks],
        [message] * 8,
        [pltpu.VMEM((128, 512), bf16)] * 8 + [pltpu.SemaphoreType.DMA((8,))],
        0,
        anywhere=8,
        outs_anywhere=8,
        alias=8,
    )
    part_both = (part_keep.astype(f32) + part_other.astype(f32)).astype(bf16)
    attn_grad = lax.psum_scatter(part_both, Z, scatter_dimension=0, tiled=True).astype(f32)
    got_attn_a = [shift(blocks[1], Y, 1), shift(blocks[3], Y, 3)]
    got_attn_b = [x_out(blocks[4 + i], *FLIPS[i]) for i in (2, 3)]
    row_part = after(row_part, part_both)

    block_at = jnp.stack([((r // 4 - y) % 4) * 4 + ((r // 2 % 2) ^ lo) * 2 + ((r % 2) ^ hi) for r in range(16)])
    pick = (block_at[:, None] == jnp.arange(16)[None, :]).astype(f32)
    gain_parts = jnp.concatenate([gain_part.reshape(16, 128), grad_gain_two.reshape(16, 128)], 1)
    gain_parts = jnp.dot(pick, gain_parts, precision=lax.Precision.HIGHEST)
    peaks = jnp.where((jnp.arange(QUERY_HEADS) == mine)[:, None], peak, 0.0)
    small = jnp.concatenate([row_part.reshape(6, 128), gain_parts[:, :128], gain_parts[:, 128:], peaks], 0)
    is_peak = (jnp.arange(46) >= 38)[:, None]

    def join(values):
        total, most = values[0], values[0]
        for value in values[1:]:
            total, most = total + value, jnp.maximum(most, value)
        return jnp.where(is_peak[-total.shape[0] :], most, total)

    small = join([small, other_core(small)])
    small = join([small, z_other(small, 1)])

    rest = lax.optimization_barrier((blocks[2], blocks[4], blocks[5], small, *got_attn_a, *got_attn_b))
    (block_y, block_0, block_1, small), got_attn_a, got_attn_b = rest[:4], rest[4:6], rest[6:]
    got_attn_a = [blocks[0], shift(block_y, Y, 2), *got_attn_a]
    got_attn_b = [x_out(block_0, 0, 0), x_out(block_1, *FLIPS[1]), *got_attn_b]
    out_late = after(out_both, part_both)
    small = join([small, z_other(small, 2)])
    row_sum = small[:6].reshape(LEN, 1)
    small = small[6:]
    small = join([small, y_other(small, 1)])
    got_attn_a, got_attn_b, small, attn_grad = lax.optimization_barrier((got_attn_a, got_attn_b, small, attn_grad))
    *sum_b, kv_give, kv_keep = call(
        join_body,
        "join_sums",
        [at, *got_attn_a, *got_attn_b, block_0],
        [((128, 512), bf16)] * 4 + [((512, HEAD), bf16), ((512, HEAD), f32)],
        [pltpu.VMEM((512, 512), bf16)] * 9 + [pltpu.SemaphoreType.DMA((9,))],
        0,
        anywhere=9,
    )
    kv_sum = (kv_keep + kv_partner(kv_give).astype(f32)).astype(bf16)
    sum_b = [sum_b[0]] + [shift(sum_b[i], Y, i) for i in (1, 2, 3)]
    small = join([small, y_other(small, 2)])
    small = join([small, x_ring(small, 1)])
    kv_sum, small, *sum_b = lax.optimization_barrier((kv_sum, small, *sum_b))
    sum_a = [x_out(kv_sum[i * 128 : (i + 1) * 128], *flip) for i, flip in enumerate(FLIPS)]
    sum_a[0] = own_or(sum_a[0], kv_sum[:128])
    grads = call(
        finish_body,
        "finish",
        [at, *got_attn_a, *got_attn_b, after(block_0, kv_sum)],
        [((128, FF), f32)] * 3,
        [pltpu.VMEM((384, 512), bf16)] * 9 + [pltpu.SemaphoreType.DMA((9,))],
        0,
        anywhere=9,
    )
    ffn_own = lax.psum_scatter(out_late, Z, scatter_dimension=0, tiled=True).astype(f32)
    ffn_own = after(ffn_own, small)

    gain_pair = jnp.dot(pick, gain_rows[0].reshape(16, 128), precision=lax.Precision.HIGHEST)
    gain_cols = lax.dynamic_slice(gain_pair, (mine * 2, 0), (2, 128)).reshape(1, HEAD)
    grad_inputs = (
        db_cols.astype(f32) + r1 * attn_grad * gain_cols - x_own.astype(f32) * r1**2 * (row_sum / WIDTH)
    )
    home = [(h_cols.astype(f32) + ffn_own).astype(bf16), grad_inputs.astype(bf16)]
    home = swap(jnp.concatenate(home, 0))
    small = join([small, x_ring(small, 2)])
    sum_a, home, small, grads = lax.optimization_barrier((sum_a, home, small, grads))
    query_output = total(sum_b)
    kv_done = total(sum_a)
    tok = y * 4 + lo * 2 + core
    gains_mine = lax.dynamic_slice(small[:32].reshape(2, 16, 128), (0, tok, 0), (2, 1, 128)).reshape(2, 128)
    peaks = small[32:, 0]

    head = hi * 4 + z
    peak_q = lax.dynamic_slice(peaks, (head,), (1,))
    pair = lax.dynamic_slice(peaks, (head // 2 * 2,), (2,))
    scale_q = jnp.sqrt(logit_ceiling / (peak_q + peak_floor_epsilon))
    scale_k = jnp.sqrt(logit_ceiling / (jnp.max(pair, keepdims=True) + peak_floor_epsilon))
    clipped_query = (w_query.astype(f32) * scale_q[None, :]).astype(bf16)
    clipped_key = (w_key.astype(f32) * scale_k[None, :]).astype(bf16)
    return (
        home[:LEN],
        home[LEN:].astype(f32),
        gains_mine[0],
        query_output[:, :HEAD],
        kv_done[:, :half],
        kv_done[:, half:],
        query_output[:, HEAD:],
        gains_mine[1],
        grads[0],
        grads[1],
        grads[2],
        clipped_query,
        clipped_key,
    )


def solution(mesh):
    torus = Mesh(mesh.devices.reshape(4, 2, 2, 2, 4), (Y, XLO, CORE, XHI, Z))
    both, rows = P(TOK, MDL), P(TOK)
    return jax.shard_map(
        on_device,
        mesh=torus,
        in_specs=(both, P(TOK, None), rows, both, both, both, both, rows, both, both, both, both),
        out_specs=(both, both, rows, both, both, both, both, rows, both, both, both, both, both),
        check_vma=False,
    )
```

```python
import functools
import math

import jax
import jax.numpy as jnp
from jax import lax
from jax.experimental import pallas as pl
from jax.experimental.pallas import tpu as pltpu
from jax.sharding import Mesh
from jax.sharding import PartitionSpec as P

QUERY_HEADS = 8
HEAD = 256
WIDTH = 2048
LEN = 768
OWN = 96
FF = 1024
Y, XLO, CORE, XHI, Z = "tok_0", "tok_1", "tok_2", "mdl_0", "mdl_1"
TOK = (Y, XLO, CORE)
MDL = (XHI, Z)

norm_epsilon = 1e-06
rope_base = 1000042.0
logit_ceiling = 4.0
masked_value = -1e30
peak_floor_epsilon = 1e-06
SCALE = HEAD ** (-0.5)
nt = (((1,), (1,)), ((), ()))
tn = (((0,), (0,)), ((), ()))
f32 = jnp.float32
bf16 = jnp.bfloat16


def dot(a, b, dims=(((1,), (0,)), ((), ()))):
    return lax.dot_general(a, b, dims, preferred_element_type=f32)


def swap(a):
    got = lax.ppermute(a, (CORE, XHI), [(1, 2), (2, 1)])
    return jnp.where(lax.axis_index(CORE) == lax.axis_index(XHI), a, got)


def other_core(a):
    return lax.ppermute(a, CORE, [(0, 1), (1, 0)])


def shift(a, axis, by):
    return lax.ppermute(a, axis, [(i, (i + by) % 4) for i in range(4)])


def z_other(a, mask):
    return lax.ppermute(a, Z, [(i, i ^ mask) for i in range(4)])


def y_other(a, mask):
    return lax.ppermute(a, Y, [(i, i ^ mask) for i in range(4)])


def kv_partner(a):
    return lax.ppermute(a, Z, [(0, 1), (1, 0), (2, 3), (3, 2)])


def plane_pairs(flip_lo, flip_core):
    pairs = []
    for lo in range(2):
        for core in range(2):
            for hi in range(2):
                pairs.append((lo * 4 + core * 2 + hi, (lo ^ flip_lo) * 4 + hi * 2 + (core ^ flip_core)))
    return pairs


def x_pairs(flip_lo, flip_core, back):
    pairs = plane_pairs(flip_lo, flip_core)
    return [(there, here) if back else (here, there) for here, there in pairs if here != there]


def x_in(a, flip_lo, flip_core):
    return lax.ppermute(a, (XLO, CORE, XHI), x_pairs(flip_lo, flip_core, False))


def x_out(a, flip_lo, flip_core):
    return lax.ppermute(a, (XLO, CORE, XHI), x_pairs(flip_lo, flip_core, True))


def own_or(got, own):
    return jnp.where(lax.axis_index(CORE) == lax.axis_index(XHI), own, got)


FLIPS = ((0, 0), (0, 1), (1, 0), (1, 1))


def from_y(a):
    return [a, shift(a, Y, -1), shift(a, Y, 2), shift(a, Y, 1)]


def from_z(a):
    return [a, shift(a, Z, -1), shift(a, Z, 2), shift(a, Z, 1)]


def x_ring(a, mask):
    return lax.ppermute(a, (XLO, XHI), [(i, i ^ mask) for i in range(4)])


def total(pieces, cols=slice(None)):
    return sum(piece[:, cols].astype(f32) for piece in pieces)


def team_gather(own):
    return lax.all_gather(own, (CORE, Z), axis=0, tiled=True)


def team_scatter(other, keep):
    both = (keep.astype(f32) + other.astype(f32)).astype(bf16)
    return lax.psum_scatter(both, Z, scatter_dimension=0, tiled=True).astype(f32)


def after(value, *others):
    return lax.optimization_barrier((value, *others))[0]


def rope_tables(segment_row):
    earlier = jnp.sum((segment_row[None, :] < segment_row[:, None]).astype(jnp.int32), axis=1)
    places = jnp.arange(LEN, dtype=jnp.int32) - earlier
    half = HEAD // 2
    inverse = jnp.exp(jnp.arange(half, dtype=f32) * (-2.0 * math.log(rope_base) / HEAD))
    angles = places.astype(f32)[:, None] * inverse[None, :]
    return jnp.cos(angles), jnp.sin(angles)


def position(r, at):
    return (((r >> 2) - at[0]) & 3) * 4 + (((r >> 1) & 1) ^ at[1]) * 2 + ((r & 1) ^ at[2])


def lanes(index, size):
    return pl.ds(pl.multiple_of(index * size, size), size)


def owner(at, there, dz):
    return (at[3] ^ there) * 4 + ((at[4] + dz) & 3)


def kdot(a, b, dims=(((1,), (0,)), ((), ()))):
    return lax.dot_general(a, b, dims, preferred_element_type=f32)


def in_vmem(n):
    return [pl.BlockSpec(memory_space=pltpu.VMEM)] * n


def call(body, name, inputs, outs, scratch, flops, megabytes=56, anywhere=0, outs_anywhere=0, alias=0):
    moved = sum(v.size * v.dtype.itemsize for v in inputs[1:])
    moved += sum(math.prod(s) * jnp.dtype(d).itemsize for s, d in outs)
    specs = [pl.BlockSpec(memory_space=pltpu.SMEM)] + in_vmem(len(inputs) - 1 - anywhere)
    specs += [pl.BlockSpec(memory_space=pl.ANY)] * anywhere
    return list(pl.pallas_call(
        body,
        name=name,
        out_shape=[jax.ShapeDtypeStruct(s, d) for s, d in outs],
        in_specs=specs,
        out_specs=in_vmem(len(outs) - outs_anywhere) + [pl.BlockSpec(memory_space=pl.ANY)] * outs_anywhere,
        scratch_shapes=scratch,
        input_output_aliases={len(inputs) - alias + i: i for i in range(alias)},
        cost_estimate=pl.CostEstimate(flops=int(flops), bytes_accessed=int(moved), transcendentals=0),
        compiler_params=pltpu.CompilerParams(vmem_limit_bytes=megabytes * 2**20),
    )(*inputs))


def turn(values, cosine, sine):
    first, second = values[:, :128], values[:, 128:]
    return first * cosine - second * sine, second * cosine + first * sine


def attention_weights(a_refs, b_refs, w_qkv, w_o, sem):
    copies = []

    def move(source, to):
        copies.append(pltpu.make_async_copy(source, to, sem.at[len(copies)]))
        copies[-1].start()

    for i in range(4):
        for dy in range(4):
            rows = pl.ds((dy * 4 + i) * 128, 128)
            move(b_refs[i].at[pl.ds(dy * 144, 128), pl.ds(256, 256)], w_o.at[rows])
    for dy in range(4):
        for i in range(4):
            rows = pl.ds((dy * 4 + i) * 128, 128)
            move(b_refs[i].at[pl.ds(dy * 144, 128), pl.ds(0, 256)], w_qkv.at[rows, pl.ds(0, 256)])
            move(a_refs[dy].at[pl.ds(i * 128, 128)], w_qkv.at[rows, pl.ds(256, 512)])
    return copies


def along_y_body(at, *refs):
    riders, gain_one, gain_two = refs[:3]
    tokens, cotangent, w_query, w_output, w_up, w_down, out, mixed, sem = refs[3:]
    pairs = [
        (w_query, out.at[pl.ds(0, 128), pl.ds(0, 256)]),
        (w_output, out.at[pl.ds(0, 128), pl.ds(256, 256)]),
        (w_up.at[:, pl.ds(0, 512)], out.at[pl.ds(144, 128)]),
        (w_up.at[:, pl.ds(512, 512)], out.at[pl.ds(272, 128)]),
        (w_down.at[:, pl.ds(512, 512)], out.at[pl.ds(400, 128)]),
        (tokens, mixed.at[pl.ds(0, 768)]),
        (cotangent, mixed.at[pl.ds(784, 768)]),
    ]
    copies = [pltpu.make_async_copy(a, b, sem.at[i]) for i, (a, b) in enumerate(pairs)]
    for copy in copies:
        copy.start()
    row = lax.broadcasted_iota(jnp.int32, (16, 128), 0)
    gains = jnp.where(row == 0, gain_one[...], jnp.where(row == 1, gain_two[...], 0.0))
    out[128:144, :128] = gains.astype(bf16)
    out[128:144, 128:] = jnp.zeros((16, 384), bf16)
    mixed[768:784, :] = riders[...]
    for copy in copies:
        copy.wait()


def along_x_body(at, *refs):
    key, value, other, w_gate, w_down, out, sem = refs
    pairs = [
        (w_gate.at[:, pl.ds(0, 512)], out.at[pl.ds(128, 128)]),
        (w_gate.at[:, pl.ds(512, 512)], out.at[pl.ds(256, 128)]),
        (w_down.at[:, pl.ds(0, 512)], out.at[pl.ds(384, 128)]),
    ]
    copies = [pltpu.make_async_copy(a, b, sem.at[i]) for i, (a, b) in enumerate(pairs)]
    for copy in copies:
        copy.start()
    odd = at[4] & 1
    out[:128, lanes(odd, 128)] = key[...]
    out[:128, lanes(1 - odd, 128)] = other[:, :128]
    out[:128, lanes(2 + odd, 128)] = value[...]
    out[:128, lanes(3 - odd, 128)] = other[:, 128:]
    for copy in copies:
        copy.wait()


def pack_body(at, *refs):
    xs, ys, to_y, to_x, sem = refs[:4], refs[4:8], refs[8], refs[9], refs[10]
    pairs = [(ref.at[pl.ds(0, 128)], to_y.at[pl.ds(128 * i, 128)]) for i, ref in enumerate(xs)]
    pairs += [(ref.at[pl.ds(0, 144)], to_x.at[pl.ds(144 * i, 144)]) for i, ref in enumerate(ys)]
    copies = [pltpu.make_async_copy(a, b, sem.at[i]) for i, (a, b) in enumerate(pairs)]
    for copy in copies:
        copy.start()
    for copy in copies:
        copy.wait()


def riders_body(at, *refs):
    xs, ys = refs[:4], refs[4:8]
    a_wide, b_wide, a_down, b_down, sem = refs[8:]
    copies = []
    for ref, row, wide, down in [(xs, 128, a_wide, a_down), (ys, 144, b_wide, b_down)]:
        for i in range(4):
            for j in range(3):
                source = ref[i].at[pl.ds(row + j * 128, 128)]
                rows = pl.ds(i * 128, 128)
                to = down.at[rows] if j == 2 else wide.at[rows, pl.ds(j * 512, 512)]
                copies.append(pltpu.make_async_copy(source, to, sem.at[len(copies)]))
    for copy in copies:
        copy.start()
    for copy in copies:
        copy.wait()


def allowed_block(i, seg_col, seg_row):
    rows, cols = 256, (i + 1) * 256
    same = seg_col[i * 256 : (i + 1) * 256, :] == seg_row[:, :cols]
    row = i * 256 + lax.broadcasted_iota(jnp.int32, (rows, cols), 0)
    return same & (row >= lax.broadcasted_iota(jnp.int32, (rows, cols), 1))


def forward_body(at, *refs):
    x, cosine, sine, seg_row, seg_col = refs[:5]
    a_refs, b_refs = refs[5:9], refs[9:13]
    a1, r1, x_mine, qr, kr, v, o, lse, peak, gains, give, keep = refs[13:25]
    w_qkv, w_o, gain_rows, sem, gain_sem = refs[25:]
    gain_copies = []
    for dy in range(4):
        for i in range(4):
            source = b_refs[i].at[pl.ds(dy * 144 + 128, 16), pl.ds(0, 128)]
            to = gain_rows.at[:, pl.ds((dy * 4 + i) * 128, 128)]
            gain_copies.append(pltpu.make_async_copy(source, to, gain_sem.at[len(gain_copies)]))
            gain_copies[-1].start()
    copies = attention_weights(a_refs, b_refs, w_qkv, w_o, sem)
    for copy in gain_copies:
        copy.wait()
    gains[...] = gain_rows[...].astype(f32)[:8]
    own = at[3] * 4 + at[4]
    for r in range(16):
        rows = pl.ds(pl.multiple_of((r // 2) * LEN + own * OWN, OWN), OWN)
        x_mine[:, lanes(position(r, at), 128)] = x[rows, (r % 2) * 128 : (r % 2 + 1) * 128]

    def norm(step, carry):
        rows = pl.ds(pl.multiple_of(step * 128, 128), 128)
        total = jnp.zeros((128, 1), f32)
        for m in range(8):
            value = x[pl.ds(pl.multiple_of(m * LEN + step * 128, 128), 128), :].astype(f32)
            total = total + jnp.sum(value * value, axis=1, keepdims=True)
        factor = lax.rsqrt(total / WIDTH + norm_epsilon)
        r1[rows, :] = factor
        for r in range(16):
            at_lanes = lanes(position(r, at), 128)
            from_rows = pl.ds(pl.multiple_of((r // 2) * LEN + step * 128, 128), 128)
            value = x[from_rows, (r % 2) * 128 : (r % 2 + 1) * 128].astype(f32)
            a1[rows, at_lanes] = (value * factor * gains[0:1, at_lanes]).astype(bf16)
        return carry

    lax.fori_loop(0, 6, norm, 0)
    for copy in copies:
        copy.wait()
    for i in range(3):
        rows = slice(i * 256, (i + 1) * 256)
        qk = kdot(a1[rows, :], w_qkv[:, :512])
        cos_i, sin_i = cosine[rows, :], sine[rows, :]
        for ref, at_col in ((qr, 0), (kr, 256)):
            one, two = turn(qk[:, at_col : at_col + 256], cos_i, sin_i)
            ref[rows, :128] = one.astype(bf16)
            ref[rows, 128:] = two.astype(bf16)
        v[rows, :] = kdot(a1[rows, :], w_qkv[:, 512:]).astype(bf16)
    largest = jnp.zeros((1, 1), f32)
    for i in range(3):
        rows, cols = slice(i * 256, (i + 1) * 256), (i + 1) * 256
        allowed = allowed_block(i, seg_col, seg_row)
        scores = kdot(qr[rows, :], kr[:cols, :], nt) * SCALE
        masked = jnp.where(allowed, scores, masked_value)
        size = jnp.where(allowed, jnp.abs(scores), 0.0)
        largest = jnp.maximum(largest, jnp.max(jnp.max(size, axis=1, keepdims=True), axis=0, keepdims=True))
        top = jnp.max(masked, axis=1, keepdims=True)
        log_total = top + jnp.log(jnp.sum(jnp.exp(masked - top), axis=1, keepdims=True))
        lse[rows, :] = log_total
        probs = jnp.exp(masked - log_total).astype(bf16)
        o[rows, :] = kdot(probs, v[:cols, :]).astype(bf16)
    peak[...] = jnp.broadcast_to(largest, (8, 128))
    for ref, c in ((give, 1 - at[3]), (keep, at[3])):
        rows = pl.ds(pl.multiple_of(c * 384, 384), 384)
        for half in range(2):
            cols = slice(half * 1024, (half + 1) * 1024)
            ref[:, cols] = kdot(o[rows, :], w_o[cols, :], nt).astype(bf16)


def reorder_body(at, whole, out):
    for r in range(16):
        rows = slice((r // 2) * LEN, (r // 2 + 1) * LEN)
        out[:, lanes(position(r, at), 128)] = whole[rows, (r % 2) * 128 : (r % 2 + 1) * 128]


def start_either(at, own, got, to, sem):
    mine = at[2] == at[3]

    @pl.when(mine)
    def _():
        pltpu.make_async_copy(own, to, sem).start()

    @pl.when(jnp.logical_not(mine))
    def _():
        pltpu.make_async_copy(got, to, sem).start()

    return pltpu.make_async_copy(got, to, sem)


def rows_a(refs, to_ref, cols, sem, copies):
    row = 0
    for ref in refs:
        to = to_ref.at[pl.ds(row, ref.shape[0]), cols]
        row += ref.shape[0]
        copies.append(pltpu.make_async_copy(ref, to, sem.at[len(copies)]))
        copies[-1].start()


def rows_b(at, own, refs, to_ref, cols, sem, copies):
    for i, ref in enumerate(refs):
        for j in range(4):
            to = to_ref.at[pl.ds((j * 4 + i) * 128, 128), cols]
            rows = pl.ds(j * 128, 128)
            if i == 0:
                copies.append(start_either(at, own.at[rows], ref.at[rows], to, sem.at[len(copies)]))
            else:
                copies.append(pltpu.make_async_copy(ref.at[rows], to, sem.at[len(copies)]))
                copies[-1].start()


def ffn_body(at, *refs):
    gains, h_in, dy_in = refs[:3]
    wide_a, (down_a, wide_b, down_b) = refs[3:8], [refs[8 + 4 * i : 12 + 4 * i] for i in range(3)]
    own_wide, own_down = refs[20:22]
    h_cols, a2_out, hid_out, dgate_out, dup_out, give_out, keep_out = refs[22:29]
    up_outs, gate_outs = refs[29:31], refs[31:33]
    h, dy, a2, hid, dgate, dup, give, keep, up_0, up_1, gate_0, gate_1 = refs[33:45]
    w_gate, w_up, w_down, sem, out_sem = refs[45:]
    h_copy = pltpu.make_async_copy(h_in, h, out_sem.at[14])
    h_copy.start()
    copies = []
    rows_a(wide_a, w_gate, pl.ds(0, FF), sem, copies)
    rows_b(at, own_wide, wide_b, w_up, pl.ds(0, FF), sem, copies)
    rows_a(down_a, w_down, pl.ds(0, 512), sem, copies)
    rows_b(at, own_down, down_b, w_down, pl.ds(512, 512), sem, copies)
    copies.append(pltpu.make_async_copy(dy_in, dy, out_sem.at[15]))
    copies[-1].start()
    sent = []

    def send(source, to):
        sent.append(pltpu.make_async_copy(source, to, out_sem.at[len(sent)]))
        sent[-1].start()

    h_copy.wait()
    own = at[3] * 4 + at[4]
    for j in range(2):
        h_cols[:, j * 128 : (j + 1) * 128] = h[:, lanes(position(2 * own + j, at), 128)]
    for i in range(6):
        rows = slice(i * 128, (i + 1) * 128)
        value = h[rows, :].astype(f32)
        factor = lax.rsqrt(jnp.mean(value * value, axis=1, keepdims=True) + norm_epsilon)
        a2[rows, :] = (value * factor * gains[1:2, :]).astype(bf16)
    send(a2, a2_out)
    for copy in copies:
        copy.wait()
    for j in range(4):
        cols = slice(j * 256, (j + 1) * 256)
        gate = kdot(a2[...], w_gate[:, cols])
        up = kdot(a2[...], w_up[:, cols])
        grad = kdot(dy[...], w_down[:, cols])
        sig = 1.0 / (1.0 + jnp.exp(-gate))
        act = gate * sig
        hid[:, cols] = (act * up).astype(bf16)
        dgate[:, cols] = (grad * up * sig * (1.0 + gate * (1.0 - sig))).astype(bf16)
        dup[:, cols] = (grad * act).astype(bf16)
    for source, to in ((hid, hid_out), (dgate, dgate_out), (dup, dup_out)):
        send(source, to)
    for ref, to, c in ((give, give_out, 1 - at[3]), (keep, keep_out, at[3])):
        rows = pl.ds(pl.multiple_of(c * 384, 384), 384)
        for j in range(4):
            cols = slice(j * 512, (j + 1) * 512)
            ref[:, cols] = (
                kdot(dgate[rows, :], w_gate[cols, :], nt) + kdot(dup[rows, :], w_up[cols, :], nt)
            ).astype(bf16)
        send(ref, to)
    for i, ref, to in ((1, gate_0, gate_outs[0]), (3, gate_1, gate_outs[1])):
        for j in range(2):
            n = slice(j * 512, (j + 1) * 512)
            ref[:, n] = kdot(a2[:, i * 512 : (i + 1) * 512], dgate[:, n], tn).astype(bf16)
        send(ref, to)
    for i in range(4):
        cols = slice((i * 4 + 2) * 128, (i * 4 + 4) * 128)
        for j in range(2):
            n = slice(j * 512, (j + 1) * 512)
            value = kdot(a2[:, cols], dup[:, n], tn).astype(bf16)
            up_0[i * 128 : (i + 1) * 128, n] = value[:128]
            up_1[i * 128 : (i + 1) * 128, n] = value[128:]
    send(up_0, up_outs[0])
    send(up_1, up_outs[1])
    for copy in sent:
        copy.wait()


def ffn_out_body(at, hid, *refs):
    down_a, down_b, own_down = refs[:4], refs[4:8], refs[8]
    give, keep, w_down, sem = refs[9:]
    copies = []
    rows_a(down_a, w_down, pl.ds(0, 512), sem, copies)
    rows_b(at, own_down, down_b, w_down, pl.ds(512, 512), sem, copies)
    for copy in copies:
        copy.wait()
    for ref, c in ((give, 1 - at[3]), (keep, at[3])):
        for dz in range(4):
            m = c * 4 + dz
            pair = pl.ds(pl.multiple_of((position(2 * m, at) >> 1) * 256, 256), 256)
            value = kdot(hid[...], w_down[pair, :], nt)
            rows = slice(dz * LEN, (dz + 1) * LEN)
            for j in range(2):
                ref[rows, lanes(at[2] ^ j, 128)] = value[:, j * 128 : (j + 1) * 128].astype(bf16)


def weight_rest_body(at, a2, dy, dgate, dup, hid, *outs):
    a_wide, b_wide, a_down, b_down = outs[:2], outs[2:4], outs[4:8], outs[8:]
    for i in range(4):
        cols, rows = slice(i * 512, (i + 1) * 512), slice(i * 128, (i + 1) * 128)
        for j in range(2):
            n = slice(j * 512, (j + 1) * 512)
            value = kdot(a2[:, i * 512 : i * 512 + 256], dup[:, n], tn).astype(bf16)
            for k in range(2):
                b_wide[k][rows, n] = value[k * 128 : (k + 1) * 128]
            if i % 2 == 0:
                a_wide[i // 2][:, n] = kdot(a2[:, cols], dgate[:, n], tn).astype(bf16)
        a_down[i][...] = kdot(dy[:, cols], hid[:, :512], tn).astype(bf16)
        value = kdot(dy[:, cols], hid[:, 512:], tn).astype(bf16)
        for k in range(4):
            b_down[k][rows, :] = value[k * 128 : (k + 1) * 128]


def backward_body(at, *refs):
    db, cosine, sine, seg_row, seg_col, qr, kr, v, lse, a1, gains = refs[:11]
    a_refs, b_refs = refs[11:15], refs[15:19]
    db_cols, dqkv, row_part, gain_part, give, keep = refs[19:25]
    w_qkv, w_o, d_o, dk_sum, dv_sum, sem = refs[25:]
    copies = attention_weights(a_refs, b_refs, w_qkv, w_o, sem)
    own = at[3] * 4 + at[4]
    for j in range(2):
        db_cols[:, j * 128 : (j + 1) * 128] = db[:, lanes(position(2 * own + j, at), 128)]
    for copy in copies:
        copy.wait()
    for i in range(3):
        rows = slice(i * 256, (i + 1) * 256)
        d_o[rows, :] = kdot(db[rows, :], w_o[...]).astype(bf16)
    for i in (2, 1, 0):
        rows, cols = slice(i * 256, (i + 1) * 256), (i + 1) * 256
        allowed = allowed_block(i, seg_col, seg_row)
        scores = kdot(qr[rows, :], kr[:cols, :], nt) * SCALE
        probs = jnp.exp(jnp.where(allowed, scores, masked_value) - lse[rows, :])
        low = probs.astype(bf16)
        dp = kdot(d_o[rows, :], v[:cols, :], nt)
        delta = jnp.sum(dp * probs, axis=1, keepdims=True)
        ds = (probs * (dp - delta)).astype(bf16)
        dq = kdot(ds, kr[:cols, :]) * SCALE
        row_part[rows, :] = jnp.sum(dq * qr[rows, :].astype(f32), axis=1, keepdims=True)
        one, two = turn(dq, cosine[rows, :], -sine[rows, :])
        dqkv[rows, :128] = one.astype(bf16)
        dqkv[rows, 128:256] = two.astype(bf16)
        dk_new = kdot(ds, qr[rows, :], tn)
        dv_new = kdot(low, d_o[rows, :], tn)
        if i == 2:
            dk_sum[...] = dk_new
            dv_sum[...] = dv_new
        else:
            dk_sum[:cols, :] = dk_sum[:cols, :] + dk_new
            dv_sum[:cols, :] = dv_sum[:cols, :] + dv_new
    for i in range(3):
        rows = slice(i * 256, (i + 1) * 256)
        dk = dk_sum[rows, :] * SCALE
        dv_i = dv_sum[rows, :]
        row_part[rows, :] = (
            row_part[rows, :]
            + jnp.sum(dk * kr[rows, :].astype(f32), axis=1, keepdims=True)
            + jnp.sum(dv_i * v[rows, :].astype(f32), axis=1, keepdims=True)
        )
        one, two = turn(dk, cosine[rows, :], -sine[rows, :])
        dqkv[rows, 256:384] = one.astype(bf16)
        dqkv[rows, 384:512] = two.astype(bf16)
        dqkv[rows, 512:] = dv_i.astype(bf16)
    for m, ref in [(j, give) for j in range(4)] + [(j, keep) for j in range(4)]:
        half = 1 - at[3] if ref is give else at[3]
        pair = lanes(position(2 * (half * 4 + m), at) >> 1, 256)
        value = kdot(dqkv[...], w_qkv[pair, :], nt)
        gain_part[:, pair] = jnp.sum(value * a1[:, pair].astype(f32), axis=0, keepdims=True) / gains[0:1, pair]
        rows = slice(m * LEN, (m + 1) * LEN)
        for j in range(2):
            ref[rows, lanes(at[2] ^ j, 128)] = value[:, j * 128 : (j + 1) * 128].astype(bf16)


def wide_sums(at, a, b, own, values):
    for i in range(4):
        rows = slice(i * 128, (i + 1) * 128)
        head = jnp.where(at[2] == at[3], own[rows, :], b[0][rows, :])
        of_b = head.astype(f32) + b[1][rows, :].astype(f32) + b[2][rows, :].astype(f32) + b[3][rows, :].astype(f32)
        of_a = a[0][rows, :].astype(f32) + a[1][rows, :].astype(f32) + a[2][rows, :].astype(f32) + a[3][rows, :].astype(f32)
        for value, total_ in ((values[i], of_b), (values[4 + i], of_a)):
            for j in range(2):
                value[j * 128 : (j + 1) * 128, :] = total_[:, j * 512 : (j + 1) * 512].astype(bf16)


def attention_weight_body(at, a1, dqkv, db, o, *refs):
    pieces, outs, values, sums = refs[:9], refs[9:17], refs[17:25], refs[25:33]
    held, sem, out_sem = refs[33:42], refs[42], refs[43]
    arriving = [pltpu.make_async_copy(x, v, sem.at[i]) for i, (x, v) in enumerate(zip(pieces, held))]
    for copy in arriving:
        copy.start()
    sent = []

    def send(source, to):
        sent.append(pltpu.make_async_copy(source, to, out_sem.at[len(sent)]))
        sent[-1].start()

    for i in range(4):
        cols, rows = slice(i * 512, (i + 1) * 512), slice(i * 128, (i + 1) * 128)
        values[i][...] = kdot(a1[:, cols], dqkv[:, 256:], tn).astype(bf16)
        send(values[i], outs[i].at[pl.ds(0, 512)])
        for n, left, right in ((slice(0, 256), a1, dqkv.at[:, :256]), (slice(256, 512), db, o)):
            value = kdot(left[:, cols], right[...], tn).astype(bf16)
            for k in range(4):
                values[4 + k][rows, n] = value[k * 128 : (k + 1) * 128]
    for i in range(4, 8):
        send(values[i], outs[i].at[pl.ds(0, 512)])
    for copy in arriving:
        copy.wait()
    wide_sums(at, held[:4], held[4:8], held[8], sums)
    for i in range(8):
        send(sums[i], outs[i].at[pl.ds(512, 256)])
    for copy in sent:
        copy.wait()


def ffn_sum_body(row, at, *refs):
    a, b, own, outs, values, sem = refs[:4], refs[4:8], refs[8], refs[17:25], refs[25:33], refs[33]
    mine = at[2] == at[3]
    copies = []
    for i in range(4):
        rows = slice(i * 128, (i + 1) * 128)
        head = jnp.where(mine, own[rows, :], b[0][rows, :])
        for value, terms in ((values[i], [b[k][rows, :] for k in (1, 2, 3)]), (values[4 + i], [a[k][rows, :] for k in (1, 2, 3)])):
            first = head if value is values[i] else a[0][rows, :]
            total = first.astype(f32) + terms[0].astype(f32) + terms[1].astype(f32) + terms[2].astype(f32)
            for j in range(total.shape[1] // 512):
                value[j * 128 : (j + 1) * 128, :] = total[:, j * 512 : (j + 1) * 512].astype(bf16)
    for i in range(8):
        to = outs[i].at[pl.ds(row, values[i].shape[0])]
        copies.append(pltpu.make_async_copy(values[i], to, sem.at[i]))
        copies[-1].start()
    for copy in copies:
        copy.wait()


def join_body(at, *refs):
    a, b, own, outs = refs[:4], refs[4:8], refs[8], refs[9:13]
    kv_give, kv_keep, va, vb, v_own, sem = refs[13], refs[14], refs[15:19], refs[19:23], refs[23], refs[24]
    pairs = list(zip([*a, *b, own], [*va, *vb, v_own]))
    copies = [pltpu.make_async_copy(x.at[pl.ds(0, 512)], v, sem.at[i]) for i, (x, v) in enumerate(pairs)]
    for copy in copies:
        copy.start()
    for copy in copies:
        copy.wait()
    odd = (at[4] & 1) == 1
    for i in range(4):
        rows = slice(i * 128, (i + 1) * 128)
        head = jnp.where(at[2] == at[3], v_own[rows, :], vb[0][rows, :])
        value = head.astype(f32) + vb[1][rows, :].astype(f32) + vb[2][rows, :].astype(f32) + vb[3][rows, :].astype(f32)
        outs[i][...] = value.astype(bf16)
        value = va[0][rows, :].astype(f32) + va[1][rows, :].astype(f32) + va[2][rows, :].astype(f32) + va[3][rows, :].astype(f32)
        for half in range(2):
            one, two = value[:, half * 256 : half * 256 + 128], value[:, half * 256 + 128 : (half + 1) * 256]
            n = slice(half * 128, (half + 1) * 128)
            kv_keep[rows, n] = jnp.where(odd, two, one)
            kv_give[rows, n] = jnp.where(odd, one, two).astype(bf16)


def finish_body(at, *refs):
    a, b, own = refs[:4], refs[4:8], refs[8]
    gate, up, down, va, vb, v_own, sem = refs[9], refs[10], refs[11], refs[12:16], refs[16:20], refs[20], refs[21]
    pairs = list(zip([*a, *b, own], [*va, *vb, v_own]))
    copies = [pltpu.make_async_copy(x.at[pl.ds(512, 384)], v, sem.at[i]) for i, (x, v) in enumerate(pairs)]
    for copy in copies:
        copy.start()
    for copy in copies:
        copy.wait()
    mine = at[2] == at[3]
    for j in range(3):
        rows = slice(j * 128, (j + 1) * 128)
        head = jnp.where(mine, v_own[rows, :], vb[0][rows, :])
        of_a = head.astype(f32) + vb[1][rows, :].astype(f32) + vb[2][rows, :].astype(f32) + vb[3][rows, :].astype(f32)
        of_b = va[0][rows, :].astype(f32) + va[1][rows, :].astype(f32) + va[2][rows, :].astype(f32) + va[3][rows, :].astype(f32)
        if j < 2:
            gate[:, j * 512 : (j + 1) * 512] = of_a
            up[:, j * 512 : (j + 1) * 512] = of_b
        else:
            down[:, :512] = of_a
            down[:, 512:] = of_b


def on_device(
    tokens,
    segments,
    gain_attn,
    w_query,
    w_key,
    w_value,
    w_output,
    gain_ffn,
    w_gate,
    w_up,
    w_down,
    cotangent,
):
    y, lo, core = lax.axis_index(Y), lax.axis_index(XLO), lax.axis_index(CORE)
    hi, z = lax.axis_index(XHI), lax.axis_index(Z)
    at = jnp.stack([y, lo, hi, core, z]).astype(jnp.int32)
    mine = core * 4 + z

    riders = jnp.zeros((16, HEAD), bf16).at[:3].set(segments.reshape(3, HEAD).astype(bf16))
    hf = FF // 2
    odd = z % 2 == 1
    half = HEAD // 2
    kv_other = kv_partner(jnp.concatenate([w_key, w_value], 1))
    y_rows, mixed = call(
        along_y_body,
        "lay_out_y",
        [
            at,
            riders,
            gain_attn.astype(f32).reshape(1, 128),
            gain_ffn.astype(f32).reshape(1, 128),
            tokens,
            cotangent,
            w_query,
            w_output,
            w_up,
            w_down,
        ],
        [((528, 2 * HEAD), bf16), ((1552, HEAD), bf16)],
        [pltpu.SemaphoreType.DMA((7,))],
        0,
        anywhere=6,
    )
    (x_rows,) = call(
        along_x_body,
        "lay_out_x",
        [at, w_key, w_value, kv_other, w_gate, w_down],
        [((512, 2 * HEAD), bf16)],
        [pltpu.SemaphoreType.DMA((3,))],
        0,
        anywhere=2,
    )
    got = swap(mixed)
    along_y = [shift(y_rows, Y, -1), shift(y_rows, Y, 1)]
    along_x = [x_in(x_rows, *flip) for flip in FLIPS[2:]]
    got, late_y, late_x, *rest = lax.optimization_barrier((got, y_rows, x_rows, *along_y, *along_x))
    along_y = [y_rows, rest[0], shift(late_y, Y, 2), rest[1]]
    along_x = [own_or(x_in(late_x, 0, 0), x_rows), x_in(late_x, *FLIPS[1]), *rest[2:]]
    rest = lax.optimization_barrier((*along_x, *along_y))
    to_y, to_x = call(
        pack_body,
        "pack",
        [at, *rest],
        [((512, 2 * HEAD), bf16), ((576, 2 * HEAD), bf16)],
        [pltpu.SemaphoreType.DMA((8,))],
        0,
        anywhere=8,
    )
    a_wide, b_wide, a_down, b_down = call(
        riders_body,
        "riders",
        [at, *rest],
        [((512, FF), bf16)] * 2 + [((512, hf), bf16)] * 2,
        [pltpu.SemaphoreType.DMA((24,))],
        0,
        anywhere=8,
    )
    x_own = got[:LEN]
    x_all = team_gather(x_own)
    upstream = team_gather(after(got[784:1552], to_x))
    segment_row = got[LEN : LEN + 3].astype(f32).reshape(1, LEN)
    segment_col = segment_row.reshape(LEN, 1)
    cosine, sine = rope_tables(segment_row[0])
    first = [shift(to_y, Y, -1), shift(to_y, Y, 1)]
    second = [x_in(to_x, *flip) for flip in FLIPS[2:]]
    late_y, late_x, *rest = lax.optimization_barrier((to_y, to_x, *first, *second))
    first, second = rest[:2], rest[2:]
    first = [to_y, first[0], shift(late_y, Y, 2), first[1]]
    second = [own_or(x_in(late_x, 0, 0), to_x), x_in(late_x, *FLIPS[1])] + second
    x_all, cosine, sine, segment_row, segment_col, *rest = lax.optimization_barrier(
        (x_all, cosine, sine, segment_row, segment_col, *first, *second, a_wide, b_wide, a_down, b_down)
    )
    first, second, (a_wide, b_wide, a_down, b_down) = rest[:4], rest[4:8], rest[8:]
    wide_a = [shift(a_wide, Y, -1), shift(a_wide, Y, 1)]
    wide_b = [x_in(b_wide, *flip) for flip in FLIPS[2:]]

    part = ((LEN // 2, WIDTH), bf16)
    act, low, col = ((LEN, WIDTH), bf16), ((LEN, HEAD), bf16), ((LEN, 1), f32)
    a1, r1, x_mine, qr, kr, v, o, lse, peak, gain_rows, give, keep = call(
        forward_body,
        "attention_forward",
        [at, x_all, cosine, sine, segment_row, segment_col, *first, *second],
        [act, col, ((OWN, WIDTH), bf16), low, low, low, low, col, ((8, 128), f32), ((8, WIDTH), f32), part, part],
        [
            pltpu.VMEM((WIDTH, 3 * HEAD), bf16),
            pltpu.VMEM((WIDTH, HEAD), bf16),
            pltpu.VMEM((16, WIDTH), bf16),
            pltpu.SemaphoreType.DMA((48,)),
            pltpu.SemaphoreType.DMA((16,)),
        ],
        2 * LEN * WIDTH * 1024,
        anywhere=8,
    )
    give, keep, upstream, *done = lax.optimization_barrier(
        (give, keep, upstream, *wide_a, *wide_b, a_wide, b_wide, a_down, b_down)
    )
    wide_a, wide_b, (a_wide, b_wide, a_down, b_down) = done[:2], done[2:4], done[4:]
    attn_own = team_scatter(other_core(give), keep)
    halves = [shift(wide_a[0][:256], Y, -1), shift(wide_a[1][256:], Y, 1)]
    wide_a = [a_wide, wide_a[0], *halves, wide_a[1]]
    wide_b = [x_in(b_wide, *flip) for flip in FLIPS[:2]] + wide_b
    down_a = [shift(a_down, Y, -1), shift(a_down, Y, 1)]
    (dy,) = call(reorder_body, "order_upstream", [at, upstream], [((LEN, WIDTH), bf16)], [], 0)


    attn_own, dy, *done = lax.optimization_barrier((attn_own, dy, *wide_a, *wide_b, *down_a, b_wide, a_down, b_down))
    wide_a, wide_b, down_a, (b_wide, a_down, b_down) = done[:5], done[5:9], done[9:11], done[11:]
    down_b = [x_in(b_down, *flip) for flip in FLIPS]
    down_a = [a_down, down_a[0], shift(a_down, Y, 2), down_a[1]]
    hidden_own = x_mine.astype(f32) + attn_own
    hidden = team_gather(hidden_own.astype(bf16))
    wide = ((LEN, FF), bf16)
    block = ((512, FF), bf16)
    h_cols, a2, hid, dgate, dup, give, keep, up_2, up_3, gate_1, gate_3 = call(
        ffn_body,
        "feed_forward",
        [at, gain_rows, hidden, dy, *wide_a, *down_a, *wide_b, *down_b, b_wide, b_down],
        [low, act, wide, wide, wide, part, part, block, block, block, block],
        [
            *[pltpu.VMEM(*v) for v in (act, act, act, wide, wide, wide, part, part, block, block, block, block)],
            pltpu.VMEM((WIDTH, FF), bf16),
            pltpu.VMEM((WIDTH, FF), bf16),
            pltpu.VMEM((WIDTH, FF), bf16),
            pltpu.SemaphoreType.DMA((44,)),
            pltpu.SemaphoreType.DMA((16,)),
        ],
        14 * LEN * WIDTH * FF,
        anywhere=21,
        outs_anywhere=10,
    )
    other = other_core(give)
    wide_out, stack = ((512, FF), bf16), ((4 * LEN, HEAD), bf16)
    work = 2 * LEN * WIDTH * FF
    both = (keep.astype(f32) + other.astype(f32)).astype(bf16)
    normed_grad = lax.psum_scatter(both, Z, scatter_dimension=0, tiled=True).astype(f32)
    dgate, dup, hid = lax.optimization_barrier((dgate, dup, hid, both))[:3]
    got_up = [x_out(up_2, *FLIPS[2]), x_out(up_3, *FLIPS[3])]
    got_gate = [shift(gate_1, Y, 1), shift(gate_3, Y, 3)]
    rest = call(
        weight_rest_body,
        "weight_rest",
        [at, a2, dy, dgate, dup, hid],
        [wide_out] * 4 + [((512, hf), bf16)] * 8,
        [],
        work * 2,
    )
    out_give, out_keep = call(
        ffn_out_body,
        "feed_forward_out",
        [at, after(hid, rest[0]), *down_a, *down_b, b_down],
        [stack, stack],
        [pltpu.VMEM((WIDTH, FF), bf16), pltpu.SemaphoreType.DMA((20,))],
        work,
        anywhere=9,
    )
    normed_grad, out_give, out_keep, *got = lax.optimization_barrier(
        (normed_grad, out_give, out_keep, *got_up, *got_gate, *rest)
    )
    got_up, got_gate, gate_b, up_b = [got[2 * i : 2 * i + 2] for i in range(4)]
    down_g = got[8:]

    gain_two = gain_rows[1:2]
    factor_own = lax.rsqrt(jnp.mean(hidden_own * hidden_own, axis=1, keepdims=True) + norm_epsilon)
    grad_gain_two = jnp.sum(normed_grad * hidden_own * factor_own, axis=0)
    scaled = normed_grad * gain_two
    grad_res = (
        lax.dynamic_slice_in_dim(dy, mine * OWN, OWN, 0).astype(f32)
        + factor_own * scaled
        - hidden_own * factor_own**3 * jnp.mean(scaled * hidden_own, axis=1, keepdims=True)
    )
    grad_low = grad_res.astype(bf16)
    db = team_gather(grad_low)
    got_gate = [gate_b[0], shift(gate_b[1], Y, 2)] + got_gate
    got_up = [x_out(up_b[0], 0, 0), x_out(up_b[1], *FLIPS[1])] + got_up
    out_both = (out_keep.astype(f32) + other_core(out_give).astype(f32)).astype(bf16)
    db, out_both, *got = lax.optimization_barrier((db, out_both, *got_gate, *got_up, *down_g))
    got_gate, got_up, down_g = got[:4], got[4:8], got[8:]
    got_down_a = [shift(down_g[1], Y, 1), shift(down_g[3], Y, 3)]
    got_down_b = [x_out(block, *flip) for block, flip in zip(down_g[6:], FLIPS[2:])]

    db_cols, dqkv, row_part, gain_part, part_give, part_keep = call(
        backward_body,
        "attention_backward",
        [at, db, cosine, sine, segment_row, segment_col, qr, kr, v, lse, a1, gain_rows, *first, *second],
        [low, ((LEN, 3 * HEAD), bf16), col, ((1, WIDTH), f32), stack, stack],
        [
            pltpu.VMEM((WIDTH, 3 * HEAD), bf16),
            pltpu.VMEM((WIDTH, HEAD), bf16),
            pltpu.VMEM((LEN, HEAD), bf16),
            pltpu.VMEM((LEN, HEAD), f32),
            pltpu.VMEM((LEN, HEAD), f32),
            pltpu.SemaphoreType.DMA((48,)),
        ],
        2 * LEN * WIDTH * 1024,
        anywhere=8,
    )
    part_give, part_keep, dqkv, down_y, down_0, down_1, *got = lax.optimization_barrier(
        (part_give, part_keep, dqkv, down_g[2], down_g[4], down_g[5], *got_down_a, *got_down_b)
    )
    got_down_a = [down_g[0], shift(down_y, Y, 2), *got[:2]]
    got_down_b = [x_out(down_0, 0, 0), x_out(down_1, *FLIPS[1]), *got[2:]]
    part_other = other_core(part_give)
    message = ((896, 512), bf16)
    blocks = call(
        attention_weight_body,
        "attention_weights",
        [at, a1, dqkv, db, o, *got_gate, *got_up, up_b[0]],
        [message] * 8,
        [
            *[pltpu.VMEM((512, 512), bf16)] * 8,
            *[pltpu.VMEM((256, 512), bf16)] * 8,
            *[pltpu.VMEM((512, FF), bf16)] * 9,
            pltpu.SemaphoreType.DMA((9,)),
            pltpu.SemaphoreType.DMA((16,)),
        ],
        2 * LEN * WIDTH * 1024,
        anywhere=9,
        outs_anywhere=8,
    )
    part_keep, part_other, *got = lax.optimization_barrier((part_keep, part_other, *blocks, *got_down_a, *got_down_b))
    blocks, got_down_a, got_down_b = got[:8], got[8:12], got[12:]
    blocks = call(
        functools.partial(ffn_sum_body, 768),
        "feed_forward_sums_down",
        [at, *got_down_a, *got_down_b, down_0, *blocks],
        [message] * 8,
        [pltpu.VMEM((128, 512), bf16)] * 8 + [pltpu.SemaphoreType.DMA((8,))],
        0,
        anywhere=8,
        outs_anywhere=8,
        alias=8,
    )
    part_both = (part_keep.astype(f32) + part_other.astype(f32)).astype(bf16)
    attn_grad = lax.psum_scatter(part_both, Z, scatter_dimension=0, tiled=True).astype(f32)
    got_attn_a = [shift(blocks[1], Y, 1), shift(blocks[3], Y, 3)]
    got_attn_b = [x_out(blocks[4 + i], *FLIPS[i]) for i in (2, 3)]
    row_part = after(row_part, part_both)

    block_at = jnp.stack([((r // 4 - y) % 4) * 4 + ((r // 2 % 2) ^ lo) * 2 + ((r % 2) ^ hi) for r in range(16)])
    pick = (block_at[:, None] == jnp.arange(16)[None, :]).astype(f32)
    gain_parts = jnp.concatenate([gain_part.reshape(16, 128), grad_gain_two.reshape(16, 128)], 1)
    gain_parts = jnp.dot(pick, gain_parts, precision=lax.Precision.HIGHEST)
    peaks = jnp.where((jnp.arange(QUERY_HEADS) == mine)[:, None], peak, 0.0)
    small = jnp.concatenate([row_part.reshape(6, 128), gain_parts[:, :128], gain_parts[:, 128:], peaks], 0)
    is_peak = (jnp.arange(46) >= 38)[:, None]

    def join(values):
        total, most = values[0], values[0]
        for value in values[1:]:
            total, most = total + value, jnp.maximum(most, value)
        return jnp.where(is_peak[-total.shape[0] :], most, total)

    small = join([small, other_core(small)])
    small = join([small, z_other(small, 1)])

    rest = lax.optimization_barrier((blocks[2], blocks[4], blocks[5], small, *got_attn_a, *got_attn_b))
    (block_y, block_0, block_1, small), got_attn_a, got_attn_b = rest[:4], rest[4:6], rest[6:]
    got_attn_a = [blocks[0], shift(block_y, Y, 2), *got_attn_a]
    got_attn_b = [x_out(block_0, 0, 0), x_out(block_1, *FLIPS[1]), *got_attn_b]
    out_late = after(out_both, part_both)
    small = join([small, z_other(small, 2)])
    row_sum = small[:6].reshape(LEN, 1)
    small = small[6:]
    small = join([small, y_other(small, 1)])
    got_attn_a, got_attn_b, small, attn_grad = lax.optimization_barrier((got_attn_a, got_attn_b, small, attn_grad))
    ffn_own = lax.psum_scatter(out_late, Z, scatter_dimension=0, tiled=True).astype(f32)

    gain_pair = jnp.dot(pick, gain_rows[0].reshape(16, 128), precision=lax.Precision.HIGHEST)
    gain_cols = lax.dynamic_slice(gain_pair, (mine * 2, 0), (2, 128)).reshape(1, HEAD)
    grad_inputs = (
        db_cols.astype(f32) + r1 * attn_grad * gain_cols - x_own.astype(f32) * r1**2 * (row_sum / WIDTH)
    )
    home = [(h_cols.astype(f32) + ffn_own).astype(bf16), grad_inputs.astype(bf16)]
    home = swap(jnp.concatenate(home, 0))
    *sum_b, kv_give, kv_keep = call(
        join_body,
        "join_sums",
        [at, *got_attn_a, *got_attn_b, block_0],
        [((128, 512), bf16)] * 4 + [((512, HEAD), bf16), ((512, HEAD), f32)],
        [pltpu.VMEM((512, 512), bf16)] * 9 + [pltpu.SemaphoreType.DMA((9,))],
        0,
        anywhere=9,
    )
    kv_sum = (kv_keep + kv_partner(kv_give).astype(f32)).astype(bf16)
    sum_b = [sum_b[0]] + [shift(sum_b[i], Y, i) for i in (1, 2, 3)]
    first_y = sum_b[1]
    small = join([small, y_other(small, 2)])
    kv_sum, home, small, *sum_b = lax.optimization_barrier((kv_sum, home, small, *sum_b))
    sum_a = [x_out(kv_sum[i * 128 : (i + 1) * 128], *flip) for i, flip in enumerate(FLIPS)]
    sum_a[0] = own_or(sum_a[0], kv_sum[:128])
    grads = call(
        finish_body,
        "finish",
        [at, *got_attn_a, *got_attn_b, after(block_0, first_y)],
        [((128, FF), f32)] * 3,
        [pltpu.VMEM((384, 512), bf16)] * 9 + [pltpu.SemaphoreType.DMA((9,))],
        0,
        anywhere=9,
    )
    for mask in (1, 2):
        small = join([small, x_ring(small, mask)])
    sum_a, small, grads = lax.optimization_barrier((sum_a, small, grads))
    query_output = total(sum_b)
    kv_done = total(sum_a)
    tok = y * 4 + lo * 2 + core
    gains_mine = lax.dynamic_slice(small[:32].reshape(2, 16, 128), (0, tok, 0), (2, 1, 128)).reshape(2, 128)
    peaks = small[32:, 0]

    head = hi * 4 + z
    peak_q = lax.dynamic_slice(peaks, (head,), (1,))
    pair = lax.dynamic_slice(peaks, (head // 2 * 2,), (2,))
    scale_q = jnp.sqrt(logit_ceiling / (peak_q + peak_floor_epsilon))
    scale_k = jnp.sqrt(logit_ceiling / (jnp.max(pair, keepdims=True) + peak_floor_epsilon))
    clipped_query = (w_query.astype(f32) * scale_q[None, :]).astype(bf16)
    clipped_key = (w_key.astype(f32) * scale_k[None, :]).astype(bf16)
    return (
        home[:LEN],
        home[LEN:].astype(f32),
        gains_mine[0],
        query_output[:, :HEAD],
        kv_done[:, :half],
        kv_done[:, half:],
        query_output[:, HEAD:],
        gains_mine[1],
        grads[0],
        grads[1],
        grads[2],
        clipped_query,
        clipped_key,
    )


def solution(mesh):
    torus = Mesh(mesh.devices.reshape(4, 2, 2, 2, 4), (Y, XLO, CORE, XHI, Z))
    both, rows = P(TOK, MDL), P(TOK)
    return jax.shard_map(
        on_device,
        mesh=torus,
        in_specs=(both, P(TOK, None), rows, both, both, both, both, rows, both, both, both, both),
        out_specs=(both, both, rows, both, both, both, both, rows, both, both, both, both, both),
        check_vma=False,
    )
```

```python
import functools
import math

import jax
import jax.numpy as jnp
from jax import lax
from jax.experimental import pallas as pl
from jax.experimental.pallas import tpu as pltpu
from jax.sharding import Mesh
from jax.sharding import PartitionSpec as P

QUERY_HEADS = 8
HEAD = 256
WIDTH = 2048
LEN = 768
OWN = 96
FF = 1024
Y, XLO, CORE, XHI, Z = "tok_0", "tok_1", "tok_2", "mdl_0", "mdl_1"
TOK = (Y, XLO, CORE)
MDL = (XHI, Z)

norm_epsilon = 1e-06
rope_base = 1000042.0
logit_ceiling = 4.0
masked_value = -1e30
peak_floor_epsilon = 1e-06
SCALE = HEAD ** (-0.5)
nt = (((1,), (1,)), ((), ()))
tn = (((0,), (0,)), ((), ()))
f32 = jnp.float32
bf16 = jnp.bfloat16


def dot(a, b, dims=(((1,), (0,)), ((), ()))):
    return lax.dot_general(a, b, dims, preferred_element_type=f32)


def swap(a):
    got = lax.ppermute(a, (CORE, XHI), [(1, 2), (2, 1)])
    return jnp.where(lax.axis_index(CORE) == lax.axis_index(XHI), a, got)


def other_core(a):
    return lax.ppermute(a, CORE, [(0, 1), (1, 0)])


def shift(a, axis, by):
    return lax.ppermute(a, axis, [(i, (i + by) % 4) for i in range(4)])


def z_other(a, mask):
    return lax.ppermute(a, Z, [(i, i ^ mask) for i in range(4)])


def y_other(a, mask):
    return lax.ppermute(a, Y, [(i, i ^ mask) for i in range(4)])


def kv_partner(a):
    return lax.ppermute(a, Z, [(0, 1), (1, 0), (2, 3), (3, 2)])


def plane_pairs(flip_lo, flip_core):
    pairs = []
    for lo in range(2):
        for core in range(2):
            for hi in range(2):
                pairs.append((lo * 4 + core * 2 + hi, (lo ^ flip_lo) * 4 + hi * 2 + (core ^ flip_core)))
    return pairs


def x_pairs(flip_lo, flip_core, back):
    pairs = plane_pairs(flip_lo, flip_core)
    return [(there, here) if back else (here, there) for here, there in pairs if here != there]


def x_in(a, flip_lo, flip_core):
    return lax.ppermute(a, (XLO, CORE, XHI), x_pairs(flip_lo, flip_core, False))


def x_out(a, flip_lo, flip_core):
    return lax.ppermute(a, (XLO, CORE, XHI), x_pairs(flip_lo, flip_core, True))


def own_or(got, own):
    return jnp.where(lax.axis_index(CORE) == lax.axis_index(XHI), own, got)


FLIPS = ((0, 0), (0, 1), (1, 0), (1, 1))


def from_y(a):
    return [a, shift(a, Y, -1), shift(a, Y, 2), shift(a, Y, 1)]


def from_z(a):
    return [a, shift(a, Z, -1), shift(a, Z, 2), shift(a, Z, 1)]


def x_ring(a, mask):
    return lax.ppermute(a, (XLO, XHI), [(i, i ^ mask) for i in range(4)])


def total(pieces, cols=slice(None)):
    return sum(piece[:, cols].astype(f32) for piece in pieces)


def team_gather(own):
    return lax.all_gather(own, (CORE, Z), axis=0, tiled=True)


def team_scatter(other, keep):
    both = (keep.astype(f32) + other.astype(f32)).astype(bf16)
    return lax.psum_scatter(both, Z, scatter_dimension=0, tiled=True).astype(f32)


def after(value, *others):
    return lax.optimization_barrier((value, *others))[0]


def rope_tables(segment_row):
    earlier = jnp.sum((segment_row[None, :] < segment_row[:, None]).astype(jnp.int32), axis=1)
    places = jnp.arange(LEN, dtype=jnp.int32) - earlier
    half = HEAD // 2
    inverse = jnp.exp(jnp.arange(half, dtype=f32) * (-2.0 * math.log(rope_base) / HEAD))
    angles = places.astype(f32)[:, None] * inverse[None, :]
    return jnp.cos(angles), jnp.sin(angles)


def position(r, at):
    return (((r >> 2) - at[0]) & 3) * 4 + (((r >> 1) & 1) ^ at[1]) * 2 + ((r & 1) ^ at[2])


def lanes(index, size):
    return pl.ds(pl.multiple_of(index * size, size), size)


def owner(at, there, dz):
    return (at[3] ^ there) * 4 + ((at[4] + dz) & 3)


def kdot(a, b, dims=(((1,), (0,)), ((), ()))):
    return lax.dot_general(a, b, dims, preferred_element_type=f32)


def in_vmem(n):
    return [pl.BlockSpec(memory_space=pltpu.VMEM)] * n


def call(body, name, inputs, outs, scratch, flops, megabytes=56, anywhere=0, outs_anywhere=0, alias=0):
    moved = sum(v.size * v.dtype.itemsize for v in inputs[1:])
    moved += sum(math.prod(s) * jnp.dtype(d).itemsize for s, d in outs)
    specs = [pl.BlockSpec(memory_space=pltpu.SMEM)] + in_vmem(len(inputs) - 1 - anywhere)
    specs += [pl.BlockSpec(memory_space=pl.ANY)] * anywhere
    return list(pl.pallas_call(
        body,
        name=name,
        out_shape=[jax.ShapeDtypeStruct(s, d) for s, d in outs],
        in_specs=specs,
        out_specs=in_vmem(len(outs) - outs_anywhere) + [pl.BlockSpec(memory_space=pl.ANY)] * outs_anywhere,
        scratch_shapes=scratch,
        input_output_aliases={len(inputs) - alias + i: i for i in range(alias)},
        cost_estimate=pl.CostEstimate(flops=int(flops), bytes_accessed=int(moved), transcendentals=0),
        compiler_params=pltpu.CompilerParams(vmem_limit_bytes=megabytes * 2**20),
    )(*inputs))


def turn(values, cosine, sine):
    first, second = values[:, :128], values[:, 128:]
    return first * cosine - second * sine, second * cosine + first * sine


def attention_weights(a_refs, b_refs, w_qkv, w_o, sem):
    copies = []

    def move(source, to):
        copies.append(pltpu.make_async_copy(source, to, sem.at[len(copies)]))
        copies[-1].start()

    for i in range(4):
        for dy in range(4):
            rows = pl.ds((dy * 4 + i) * 128, 128)
            move(b_refs[i].at[pl.ds(dy * 144, 128), pl.ds(256, 256)], w_o.at[rows])
    for dy in range(4):
        for i in range(4):
            rows = pl.ds((dy * 4 + i) * 128, 128)
            move(b_refs[i].at[pl.ds(dy * 144, 128), pl.ds(0, 256)], w_qkv.at[rows, pl.ds(0, 256)])
            move(a_refs[dy].at[pl.ds(i * 128, 128)], w_qkv.at[rows, pl.ds(256, 512)])
    return copies


def along_y_body(at, *refs):
    riders, gain_one, gain_two = refs[:3]
    tokens, cotangent, w_query, w_output, w_up, w_down, out, mixed, sem = refs[3:]
    pairs = [
        (w_query, out.at[pl.ds(0, 128), pl.ds(0, 256)]),
        (w_output, out.at[pl.ds(0, 128), pl.ds(256, 256)]),
        (w_up.at[:, pl.ds(0, 512)], out.at[pl.ds(144, 128)]),
        (w_up.at[:, pl.ds(512, 512)], out.at[pl.ds(272, 128)]),
        (w_down.at[:, pl.ds(512, 512)], out.at[pl.ds(400, 128)]),
        (tokens, mixed.at[pl.ds(0, 768)]),
        (cotangent, mixed.at[pl.ds(784, 768)]),
    ]
    copies = [pltpu.make_async_copy(a, b, sem.at[i]) for i, (a, b) in enumerate(pairs)]
    for copy in copies:
        copy.start()
    row = lax.broadcasted_iota(jnp.int32, (16, 128), 0)
    gains = jnp.where(row == 0, gain_one[...], jnp.where(row == 1, gain_two[...], 0.0))
    out[128:144, :128] = gains.astype(bf16)
    out[128:144, 128:] = jnp.zeros((16, 384), bf16)
    mixed[768:784, :] = riders[...]
    for copy in copies:
        copy.wait()


def along_x_body(at, *refs):
    key, value, other, w_gate, w_down, out, sem = refs
    pairs = [
        (w_gate.at[:, pl.ds(0, 512)], out.at[pl.ds(128, 128)]),
        (w_gate.at[:, pl.ds(512, 512)], out.at[pl.ds(256, 128)]),
        (w_down.at[:, pl.ds(0, 512)], out.at[pl.ds(384, 128)]),
    ]
    copies = [pltpu.make_async_copy(a, b, sem.at[i]) for i, (a, b) in enumerate(pairs)]
    for copy in copies:
        copy.start()
    odd = at[4] & 1
    out[:128, lanes(odd, 128)] = key[...]
    out[:128, lanes(1 - odd, 128)] = other[:, :128]
    out[:128, lanes(2 + odd, 128)] = value[...]
    out[:128, lanes(3 - odd, 128)] = other[:, 128:]
    for copy in copies:
        copy.wait()


def pack_body(at, *refs):
    xs, ys, to_y, to_x, sem = refs[:4], refs[4:8], refs[8], refs[9], refs[10]
    pairs = [(ref.at[pl.ds(0, 128)], to_y.at[pl.ds(128 * i, 128)]) for i, ref in enumerate(xs)]
    pairs += [(ref.at[pl.ds(0, 144)], to_x.at[pl.ds(144 * i, 144)]) for i, ref in enumerate(ys)]
    copies = [pltpu.make_async_copy(a, b, sem.at[i]) for i, (a, b) in enumerate(pairs)]
    for copy in copies:
        copy.start()
    for copy in copies:
        copy.wait()


def riders_body(at, *refs):
    xs, ys = refs[:4], refs[4:8]
    a_wide, b_wide, a_down, b_down, sem = refs[8:]
    copies = []
    for ref, row, wide, down in [(xs, 128, a_wide, a_down), (ys, 144, b_wide, b_down)]:
        for i in range(4):
            for j in range(3):
                source = ref[i].at[pl.ds(row + j * 128, 128)]
                rows = pl.ds(i * 128, 128)
                to = down.at[rows] if j == 2 else wide.at[rows, pl.ds(j * 512, 512)]
                copies.append(pltpu.make_async_copy(source, to, sem.at[len(copies)]))
    for copy in copies:
        copy.start()
    for copy in copies:
        copy.wait()


def allowed_block(i, seg_col, seg_row):
    rows, cols = 256, (i + 1) * 256
    same = seg_col[i * 256 : (i + 1) * 256, :] == seg_row[:, :cols]
    row = i * 256 + lax.broadcasted_iota(jnp.int32, (rows, cols), 0)
    return same & (row >= lax.broadcasted_iota(jnp.int32, (rows, cols), 1))


def forward_body(at, *refs):
    x, cosine, sine, seg_row, seg_col = refs[:5]
    a_refs, b_refs = refs[5:9], refs[9:13]
    a1, r1, x_mine, qr, kr, v, o, lse, peak, gains, give, keep = refs[13:25]
    w_qkv, w_o, gain_rows, sem, gain_sem = refs[25:]
    gain_copies = []
    for dy in range(4):
        for i in range(4):
            source = b_refs[i].at[pl.ds(dy * 144 + 128, 16), pl.ds(0, 128)]
            to = gain_rows.at[:, pl.ds((dy * 4 + i) * 128, 128)]
            gain_copies.append(pltpu.make_async_copy(source, to, gain_sem.at[len(gain_copies)]))
            gain_copies[-1].start()
    copies = attention_weights(a_refs, b_refs, w_qkv, w_o, sem)
    for copy in gain_copies:
        copy.wait()
    gains[...] = gain_rows[...].astype(f32)[:8]
    own = at[3] * 4 + at[4]
    for r in range(16):
        rows = pl.ds(pl.multiple_of((r // 2) * LEN + own * OWN, OWN), OWN)
        x_mine[:, lanes(position(r, at), 128)] = x[rows, (r % 2) * 128 : (r % 2 + 1) * 128]

    def norm(step, carry):
        rows = pl.ds(pl.multiple_of(step * 128, 128), 128)
        total = jnp.zeros((128, 1), f32)
        for m in range(8):
            value = x[pl.ds(pl.multiple_of(m * LEN + step * 128, 128), 128), :].astype(f32)
            total = total + jnp.sum(value * value, axis=1, keepdims=True)
        factor = lax.rsqrt(total / WIDTH + norm_epsilon)
        r1[rows, :] = factor
        for r in range(16):
            at_lanes = lanes(position(r, at), 128)
            from_rows = pl.ds(pl.multiple_of((r // 2) * LEN + step * 128, 128), 128)
            value = x[from_rows, (r % 2) * 128 : (r % 2 + 1) * 128].astype(f32)
            a1[rows, at_lanes] = (value * factor * gains[0:1, at_lanes]).astype(bf16)
        return carry

    lax.fori_loop(0, 6, norm, 0)
    for copy in copies:
        copy.wait()
    for i in range(3):
        rows = slice(i * 256, (i + 1) * 256)
        qk = kdot(a1[rows, :], w_qkv[:, :512])
        cos_i, sin_i = cosine[rows, :], sine[rows, :]
        for ref, at_col in ((qr, 0), (kr, 256)):
            one, two = turn(qk[:, at_col : at_col + 256], cos_i, sin_i)
            ref[rows, :128] = one.astype(bf16)
            ref[rows, 128:] = two.astype(bf16)
        v[rows, :] = kdot(a1[rows, :], w_qkv[:, 512:]).astype(bf16)
    largest = jnp.zeros((1, 1), f32)
    for i in range(3):
        rows, cols = slice(i * 256, (i + 1) * 256), (i + 1) * 256
        allowed = allowed_block(i, seg_col, seg_row)
        scores = kdot(qr[rows, :], kr[:cols, :], nt) * SCALE
        masked = jnp.where(allowed, scores, masked_value)
        size = jnp.where(allowed, jnp.abs(scores), 0.0)
        largest = jnp.maximum(largest, jnp.max(jnp.max(size, axis=1, keepdims=True), axis=0, keepdims=True))
        top = jnp.max(masked, axis=1, keepdims=True)
        log_total = top + jnp.log(jnp.sum(jnp.exp(masked - top), axis=1, keepdims=True))
        lse[rows, :] = log_total
        probs = jnp.exp(masked - log_total).astype(bf16)
        o[rows, :] = kdot(probs, v[:cols, :]).astype(bf16)
    peak[...] = jnp.broadcast_to(largest, (8, 128))
    for ref, c in ((give, 1 - at[3]), (keep, at[3])):
        rows = pl.ds(pl.multiple_of(c * 384, 384), 384)
        for half in range(2):
            cols = slice(half * 1024, (half + 1) * 1024)
            ref[:, cols] = kdot(o[rows, :], w_o[cols, :], nt).astype(bf16)


def reorder_body(at, whole, out):
    for r in range(16):
        rows = slice((r // 2) * LEN, (r // 2 + 1) * LEN)
        out[:, lanes(position(r, at), 128)] = whole[rows, (r % 2) * 128 : (r % 2 + 1) * 128]


def start_either(at, own, got, to, sem):
    mine = at[2] == at[3]

    @pl.when(mine)
    def _():
        pltpu.make_async_copy(own, to, sem).start()

    @pl.when(jnp.logical_not(mine))
    def _():
        pltpu.make_async_copy(got, to, sem).start()

    return pltpu.make_async_copy(got, to, sem)


def rows_a(refs, to_ref, cols, sem, copies):
    row = 0
    for ref in refs:
        to = to_ref.at[pl.ds(row, ref.shape[0]), cols]
        row += ref.shape[0]
        copies.append(pltpu.make_async_copy(ref, to, sem.at[len(copies)]))
        copies[-1].start()


def rows_b(at, own, refs, to_ref, cols, sem, copies):
    for i, ref in enumerate(refs):
        for j in range(4):
            to = to_ref.at[pl.ds((j * 4 + i) * 128, 128), cols]
            rows = pl.ds(j * 128, 128)
            if i == 0:
                copies.append(start_either(at, own.at[rows], ref.at[rows], to, sem.at[len(copies)]))
            else:
                copies.append(pltpu.make_async_copy(ref.at[rows], to, sem.at[len(copies)]))
                copies[-1].start()


def ffn_body(at, *refs):
    gains, h_in, dy_in = refs[:3]
    wide_a, (down_a, wide_b, down_b) = refs[3:8], [refs[8 + 4 * i : 12 + 4 * i] for i in range(3)]
    own_wide, own_down = refs[20:22]
    h_cols, a2_out, hid_out, dgate_out, dup_out, give_out, keep_out = refs[22:29]
    up_outs, gate_outs = refs[29:31], refs[31:33]
    h, dy, a2, hid, dgate, dup, give, keep, up_0, up_1, gate_0, gate_1 = refs[33:45]
    w_gate, w_up, w_down, sem, out_sem = refs[45:]
    h_copy = pltpu.make_async_copy(h_in, h, out_sem.at[14])
    h_copy.start()
    copies = []
    rows_a(wide_a, w_gate, pl.ds(0, FF), sem, copies)
    rows_b(at, own_wide, wide_b, w_up, pl.ds(0, FF), sem, copies)
    rows_a(down_a, w_down, pl.ds(0, 512), sem, copies)
    rows_b(at, own_down, down_b, w_down, pl.ds(512, 512), sem, copies)
    copies.append(pltpu.make_async_copy(dy_in, dy, out_sem.at[15]))
    copies[-1].start()
    sent = []

    def send(source, to):
        sent.append(pltpu.make_async_copy(source, to, out_sem.at[len(sent)]))
        sent[-1].start()

    h_copy.wait()
    own = at[3] * 4 + at[4]
    for j in range(2):
        h_cols[:, j * 128 : (j + 1) * 128] = h[:, lanes(position(2 * own + j, at), 128)]
    for i in range(6):
        rows = slice(i * 128, (i + 1) * 128)
        value = h[rows, :].astype(f32)
        factor = lax.rsqrt(jnp.mean(value * value, axis=1, keepdims=True) + norm_epsilon)
        a2[rows, :] = (value * factor * gains[1:2, :]).astype(bf16)
    send(a2, a2_out)
    for copy in copies:
        copy.wait()
    for j in range(4):
        cols = slice(j * 256, (j + 1) * 256)
        gate = kdot(a2[...], w_gate[:, cols])
        up = kdot(a2[...], w_up[:, cols])
        grad = kdot(dy[...], w_down[:, cols])
        sig = 1.0 / (1.0 + jnp.exp(-gate))
        act = gate * sig
        hid[:, cols] = (act * up).astype(bf16)
        dgate[:, cols] = (grad * up * sig * (1.0 + gate * (1.0 - sig))).astype(bf16)
        dup[:, cols] = (grad * act).astype(bf16)
    for source, to in ((hid, hid_out), (dgate, dgate_out), (dup, dup_out)):
        send(source, to)
    for ref, to, c in ((give, give_out, 1 - at[3]), (keep, keep_out, at[3])):
        rows = pl.ds(pl.multiple_of(c * 384, 384), 384)
        for j in range(4):
            cols = slice(j * 512, (j + 1) * 512)
            ref[:, cols] = (
                kdot(dgate[rows, :], w_gate[cols, :], nt) + kdot(dup[rows, :], w_up[cols, :], nt)
            ).astype(bf16)
        send(ref, to)
    for i, ref, to in ((1, gate_0, gate_outs[0]), (3, gate_1, gate_outs[1])):
        for j in range(2):
            n = slice(j * 512, (j + 1) * 512)
            ref[:, n] = kdot(a2[:, i * 512 : (i + 1) * 512], dgate[:, n], tn).astype(bf16)
        send(ref, to)
    for i in range(4):
        cols = slice((i * 4 + 2) * 128, (i * 4 + 4) * 128)
        for j in range(2):
            n = slice(j * 512, (j + 1) * 512)
            value = kdot(a2[:, cols], dup[:, n], tn).astype(bf16)
            up_0[i * 128 : (i + 1) * 128, n] = value[:128]
            up_1[i * 128 : (i + 1) * 128, n] = value[128:]
    send(up_0, up_outs[0])
    send(up_1, up_outs[1])
    for copy in sent:
        copy.wait()


def ffn_out_body(at, hid, *refs):
    down_a, down_b, own_down = refs[:4], refs[4:8], refs[8]
    give, keep, w_down, sem = refs[9:]
    copies = []
    rows_a(down_a, w_down, pl.ds(0, 512), sem, copies)
    rows_b(at, own_down, down_b, w_down, pl.ds(512, 512), sem, copies)
    for copy in copies:
        copy.wait()
    for ref, c in ((give, 1 - at[3]), (keep, at[3])):
        for dz in range(4):
            m = c * 4 + dz
            pair = pl.ds(pl.multiple_of((position(2 * m, at) >> 1) * 256, 256), 256)
            value = kdot(hid[...], w_down[pair, :], nt)
            rows = slice(dz * LEN, (dz + 1) * LEN)
            for j in range(2):
                ref[rows, lanes(at[2] ^ j, 128)] = value[:, j * 128 : (j + 1) * 128].astype(bf16)


def weight_rest_body(at, a2, dy, dgate, dup, hid, *outs):
    a_wide, b_wide, a_down, b_down = outs[:2], outs[2:4], outs[4:8], outs[8:]
    for i in range(4):
        cols, rows = slice(i * 512, (i + 1) * 512), slice(i * 128, (i + 1) * 128)
        for j in range(2):
            n = slice(j * 512, (j + 1) * 512)
            value = kdot(a2[:, i * 512 : i * 512 + 256], dup[:, n], tn).astype(bf16)
            for k in range(2):
                b_wide[k][rows, n] = value[k * 128 : (k + 1) * 128]
            if i % 2 == 0:
                a_wide[i // 2][:, n] = kdot(a2[:, cols], dgate[:, n], tn).astype(bf16)
        a_down[i][...] = kdot(dy[:, cols], hid[:, :512], tn).astype(bf16)
        value = kdot(dy[:, cols], hid[:, 512:], tn).astype(bf16)
        for k in range(4):
            b_down[k][rows, :] = value[k * 128 : (k + 1) * 128]


def backward_body(at, *refs):
    db, cosine, sine, seg_row, seg_col, qr, kr, v, lse, a1, gains = refs[:11]
    a_refs, b_refs = refs[11:15], refs[15:19]
    db_cols, dqkv, row_part, gain_part, give, keep = refs[19:25]
    w_qkv, w_o, d_o, dk_sum, dv_sum, sem = refs[25:]
    copies = attention_weights(a_refs, b_refs, w_qkv, w_o, sem)
    own = at[3] * 4 + at[4]
    for j in range(2):
        db_cols[:, j * 128 : (j + 1) * 128] = db[:, lanes(position(2 * own + j, at), 128)]
    for copy in copies:
        copy.wait()
    for i in range(3):
        rows = slice(i * 256, (i + 1) * 256)
        d_o[rows, :] = kdot(db[rows, :], w_o[...]).astype(bf16)
    for i in (2, 1, 0):
        rows, cols = slice(i * 256, (i + 1) * 256), (i + 1) * 256
        allowed = allowed_block(i, seg_col, seg_row)
        scores = kdot(qr[rows, :], kr[:cols, :], nt) * SCALE
        probs = jnp.exp(jnp.where(allowed, scores, masked_value) - lse[rows, :])
        low = probs.astype(bf16)
        dp = kdot(d_o[rows, :], v[:cols, :], nt)
        delta = jnp.sum(dp * probs, axis=1, keepdims=True)
        ds = (probs * (dp - delta)).astype(bf16)
        dq = kdot(ds, kr[:cols, :]) * SCALE
        row_part[rows, :] = jnp.sum(dq * qr[rows, :].astype(f32), axis=1, keepdims=True)
        one, two = turn(dq, cosine[rows, :], -sine[rows, :])
        dqkv[rows, :128] = one.astype(bf16)
        dqkv[rows, 128:256] = two.astype(bf16)
        dk_new = kdot(ds, qr[rows, :], tn)
        dv_new = kdot(low, d_o[rows, :], tn)
        if i == 2:
            dk_sum[...] = dk_new
            dv_sum[...] = dv_new
        else:
            dk_sum[:cols, :] = dk_sum[:cols, :] + dk_new
            dv_sum[:cols, :] = dv_sum[:cols, :] + dv_new
    for i in range(3):
        rows = slice(i * 256, (i + 1) * 256)
        dk = dk_sum[rows, :] * SCALE
        dv_i = dv_sum[rows, :]
        row_part[rows, :] = (
            row_part[rows, :]
            + jnp.sum(dk * kr[rows, :].astype(f32), axis=1, keepdims=True)
            + jnp.sum(dv_i * v[rows, :].astype(f32), axis=1, keepdims=True)
        )
        one, two = turn(dk, cosine[rows, :], -sine[rows, :])
        dqkv[rows, 256:384] = one.astype(bf16)
        dqkv[rows, 384:512] = two.astype(bf16)
        dqkv[rows, 512:] = dv_i.astype(bf16)
    for m, ref in [(j, give) for j in range(4)] + [(j, keep) for j in range(4)]:
        half = 1 - at[3] if ref is give else at[3]
        pair = lanes(position(2 * (half * 4 + m), at) >> 1, 256)
        value = kdot(dqkv[...], w_qkv[pair, :], nt)
        gain_part[:, pair] = jnp.sum(value * a1[:, pair].astype(f32), axis=0, keepdims=True) / gains[0:1, pair]
        rows = slice(m * LEN, (m + 1) * LEN)
        for j in range(2):
            ref[rows, lanes(at[2] ^ j, 128)] = value[:, j * 128 : (j + 1) * 128].astype(bf16)


def wide_sums(at, a, b, own, values):
    for i in range(4):
        rows = slice(i * 128, (i + 1) * 128)
        head = jnp.where(at[2] == at[3], own[rows, :], b[0][rows, :])
        of_b = head.astype(f32) + b[1][rows, :].astype(f32) + b[2][rows, :].astype(f32) + b[3][rows, :].astype(f32)
        of_a = a[0][rows, :].astype(f32) + a[1][rows, :].astype(f32) + a[2][rows, :].astype(f32) + a[3][rows, :].astype(f32)
        for value, total_ in ((values[i], of_b), (values[4 + i], of_a)):
            for j in range(2):
                value[j * 128 : (j + 1) * 128, :] = total_[:, j * 512 : (j + 1) * 512].astype(bf16)


def attention_weight_body(at, a1, dqkv, db, o, *refs):
    pieces, outs, values, sums = refs[:9], refs[9:17], refs[17:25], refs[25:33]
    held, sem, out_sem = refs[33:42], refs[42], refs[43]
    arriving = [pltpu.make_async_copy(x, v, sem.at[i]) for i, (x, v) in enumerate(zip(pieces, held))]
    for copy in arriving:
        copy.start()
    sent = []

    def send(source, to):
        sent.append(pltpu.make_async_copy(source, to, out_sem.at[len(sent)]))
        sent[-1].start()

    for i in range(4):
        cols, rows = slice(i * 512, (i + 1) * 512), slice(i * 128, (i + 1) * 128)
        values[i][...] = kdot(a1[:, cols], dqkv[:, 256:], tn).astype(bf16)
        send(values[i], outs[i].at[pl.ds(0, 512)])
        for n, left, right in ((slice(0, 256), a1, dqkv.at[:, :256]), (slice(256, 512), db, o)):
            value = kdot(left[:, cols], right[...], tn).astype(bf16)
            for k in range(4):
                values[4 + k][rows, n] = value[k * 128 : (k + 1) * 128]
    for i in range(4, 8):
        send(values[i], outs[i].at[pl.ds(0, 512)])
    for copy in arriving:
        copy.wait()
    wide_sums(at, held[:4], held[4:8], held[8], sums)
    for i in range(8):
        send(sums[i], outs[i].at[pl.ds(512, 256)])
    for copy in sent:
        copy.wait()


def ffn_sum_body(row, at, *refs):
    a, b, own, outs, values, sem = refs[:4], refs[4:8], refs[8], refs[17:25], refs[25:33], refs[33]
    mine = at[2] == at[3]
    copies = []
    for i in range(4):
        rows = slice(i * 128, (i + 1) * 128)
        head = jnp.where(mine, own[rows, :], b[0][rows, :])
        for value, terms in ((values[i], [b[k][rows, :] for k in (1, 2, 3)]), (values[4 + i], [a[k][rows, :] for k in (1, 2, 3)])):
            first = head if value is values[i] else a[0][rows, :]
            total = first.astype(f32) + terms[0].astype(f32) + terms[1].astype(f32) + terms[2].astype(f32)
            for j in range(total.shape[1] // 512):
                value[j * 128 : (j + 1) * 128, :] = total[:, j * 512 : (j + 1) * 512].astype(bf16)
    for i in range(8):
        to = outs[i].at[pl.ds(row, values[i].shape[0])]
        copies.append(pltpu.make_async_copy(values[i], to, sem.at[i]))
        copies[-1].start()
    for copy in copies:
        copy.wait()


def join_body(at, *refs):
    a, b, own, outs = refs[:4], refs[4:8], refs[8], refs[9:13]
    kv_give, kv_keep, va, vb, v_own, sem = refs[13], refs[14], refs[15:19], refs[19:23], refs[23], refs[24]
    pairs = list(zip([*a, *b, own], [*va, *vb, v_own]))
    copies = [pltpu.make_async_copy(x.at[pl.ds(0, 512)], v, sem.at[i]) for i, (x, v) in enumerate(pairs)]
    for copy in copies:
        copy.start()
    for copy in copies:
        copy.wait()
    odd = (at[4] & 1) == 1
    for i in range(4):
        rows = slice(i * 128, (i + 1) * 128)
        head = jnp.where(at[2] == at[3], v_own[rows, :], vb[0][rows, :])
        value = head.astype(f32) + vb[1][rows, :].astype(f32) + vb[2][rows, :].astype(f32) + vb[3][rows, :].astype(f32)
        outs[i][...] = value.astype(bf16)
        value = va[0][rows, :].astype(f32) + va[1][rows, :].astype(f32) + va[2][rows, :].astype(f32) + va[3][rows, :].astype(f32)
        for half in range(2):
            one, two = value[:, half * 256 : half * 256 + 128], value[:, half * 256 + 128 : (half + 1) * 256]
            n = slice(half * 128, (half + 1) * 128)
            kv_keep[rows, n] = jnp.where(odd, two, one)
            kv_give[rows, n] = jnp.where(odd, one, two).astype(bf16)


def finish_body(at, *refs):
    a, b, own = refs[:4], refs[4:8], refs[8]
    gate, up, down, va, vb, v_own, sem = refs[9], refs[10], refs[11], refs[12:16], refs[16:20], refs[20], refs[21]
    pairs = list(zip([*a, *b, own], [*va, *vb, v_own]))
    copies = [pltpu.make_async_copy(x.at[pl.ds(512, 384)], v, sem.at[i]) for i, (x, v) in enumerate(pairs)]
    for copy in copies:
        copy.start()
    for copy in copies:
        copy.wait()
    mine = at[2] == at[3]
    for j in range(3):
        rows = slice(j * 128, (j + 1) * 128)
        head = jnp.where(mine, v_own[rows, :], vb[0][rows, :])
        of_a = head.astype(f32) + vb[1][rows, :].astype(f32) + vb[2][rows, :].astype(f32) + vb[3][rows, :].astype(f32)
        of_b = va[0][rows, :].astype(f32) + va[1][rows, :].astype(f32) + va[2][rows, :].astype(f32) + va[3][rows, :].astype(f32)
        if j < 2:
            gate[:, j * 512 : (j + 1) * 512] = of_a
            up[:, j * 512 : (j + 1) * 512] = of_b
        else:
            down[:, :512] = of_a
            down[:, 512:] = of_b


def last_body(at, *refs):
    own, a, b, w_query, w_key = refs[0], refs[1:5], refs[5:9], refs[9], refs[10]
    query, output, key, value, gain_one, gain_two, clipped_query, clipped_key, small = refs[11:]
    a = [jnp.where(at[2] == at[3], own[...], a[0][...]), a[1][...], a[2][...], a[3][...]]
    kv = a[0][:128].astype(f32) + a[1][:128].astype(f32) + a[2][:128].astype(f32) + a[3][:128].astype(f32)
    key[...] = kv[:, :128]
    value[...] = kv[:, 128:]
    parts = [piece[128:, :128].astype(f32) + piece[128:, 128:].astype(f32) for piece in a]
    added = parts[0] + parts[1] + parts[2] + parts[3]
    most = jnp.maximum(jnp.maximum(parts[0], parts[1]), jnp.maximum(parts[2], parts[3]))
    small[...] = jnp.where(lax.broadcasted_iota(jnp.int32, (48, 128), 0) >= 32, most, added)
    tok, head = at[0] * 4 + at[1] * 2 + at[3], at[2] * 4 + at[4]
    gain_one[...] = small[pl.ds(tok, 1), :]
    gain_two[...] = small[pl.ds(16 + tok, 1), :]
    peak = small[pl.ds(32 + head, 1), :]
    pair = jnp.maximum(peak, small[pl.ds(32 + (head ^ 1), 1), :])
    scale = jnp.sqrt(logit_ceiling / (peak + peak_floor_epsilon))
    for j in range(2):
        cols = slice(j * 128, (j + 1) * 128)
        clipped_query[:, cols] = (w_query[:, cols].astype(f32) * scale).astype(bf16)
    scale = jnp.sqrt(logit_ceiling / (pair + peak_floor_epsilon))
    clipped_key[...] = (w_key[...].astype(f32) * scale).astype(bf16)
    total_b = b[0][...].astype(f32) + b[1][...].astype(f32) + b[2][...].astype(f32) + b[3][...].astype(f32)
    query[...] = total_b[:, :256]
    output[...] = total_b[:, 256:]


def on_device(
    tokens,
    segments,
    gain_attn,
    w_query,
    w_key,
    w_value,
    w_output,
    gain_ffn,
    w_gate,
    w_up,
    w_down,
    cotangent,
):
    y, lo, core = lax.axis_index(Y), lax.axis_index(XLO), lax.axis_index(CORE)
    hi, z = lax.axis_index(XHI), lax.axis_index(Z)
    at = jnp.stack([y, lo, hi, core, z]).astype(jnp.int32)
    mine = core * 4 + z

    riders = jnp.zeros((16, HEAD), bf16).at[:3].set(segments.reshape(3, HEAD).astype(bf16))
    hf = FF // 2
    odd = z % 2 == 1
    half = HEAD // 2
    kv_other = kv_partner(jnp.concatenate([w_key, w_value], 1))
    y_rows, mixed = call(
        along_y_body,
        "lay_out_y",
        [
            at,
            riders,
            gain_attn.astype(f32).reshape(1, 128),
            gain_ffn.astype(f32).reshape(1, 128),
            tokens,
            cotangent,
            w_query,
            w_output,
            w_up,
            w_down,
        ],
        [((528, 2 * HEAD), bf16), ((1552, HEAD), bf16)],
        [pltpu.SemaphoreType.DMA((7,))],
        0,
        anywhere=6,
    )
    (x_rows,) = call(
        along_x_body,
        "lay_out_x",
        [at, w_key, w_value, kv_other, w_gate, w_down],
        [((512, 2 * HEAD), bf16)],
        [pltpu.SemaphoreType.DMA((3,))],
        0,
        anywhere=2,
    )
    got = swap(mixed)
    along_y = [shift(y_rows, Y, -1), shift(y_rows, Y, 1)]
    along_x = [x_in(x_rows, *flip) for flip in FLIPS[2:]]
    got, late_y, late_x, *rest = lax.optimization_barrier((got, y_rows, x_rows, *along_y, *along_x))
    along_y = [y_rows, rest[0], shift(late_y, Y, 2), rest[1]]
    along_x = [own_or(x_in(late_x, 0, 0), x_rows), x_in(late_x, *FLIPS[1]), *rest[2:]]
    rest = lax.optimization_barrier((*along_x, *along_y))
    to_y, to_x = call(
        pack_body,
        "pack",
        [at, *rest],
        [((512, 2 * HEAD), bf16), ((576, 2 * HEAD), bf16)],
        [pltpu.SemaphoreType.DMA((8,))],
        0,
        anywhere=8,
    )
    a_wide, b_wide, a_down, b_down = call(
        riders_body,
        "riders",
        [at, *rest],
        [((512, FF), bf16)] * 2 + [((512, hf), bf16)] * 2,
        [pltpu.SemaphoreType.DMA((24,))],
        0,
        anywhere=8,
    )
    x_own = got[:LEN]
    x_all = team_gather(x_own)
    upstream = team_gather(after(got[784:1552], to_x))
    segment_row = got[LEN : LEN + 3].astype(f32).reshape(1, LEN)
    segment_col = segment_row.reshape(LEN, 1)
    cosine, sine = rope_tables(segment_row[0])
    first = [shift(to_y, Y, -1), shift(to_y, Y, 1)]
    second = [x_in(to_x, *flip) for flip in FLIPS[2:]]
    late_y, late_x, *rest = lax.optimization_barrier((to_y, to_x, *first, *second))
    first, second = rest[:2], rest[2:]
    first = [to_y, first[0], shift(late_y, Y, 2), first[1]]
    second = [own_or(x_in(late_x, 0, 0), to_x), x_in(late_x, *FLIPS[1])] + second
    x_all, cosine, sine, segment_row, segment_col, *rest = lax.optimization_barrier(
        (x_all, cosine, sine, segment_row, segment_col, *first, *second, a_wide, b_wide, a_down, b_down)
    )
    first, second, (a_wide, b_wide, a_down, b_down) = rest[:4], rest[4:8], rest[8:]
    wide_a = [shift(a_wide, Y, -1), shift(a_wide, Y, 1)]
    wide_b = [x_in(b_wide, *flip) for flip in FLIPS[2:]]

    part = ((LEN // 2, WIDTH), bf16)
    act, low, col = ((LEN, WIDTH), bf16), ((LEN, HEAD), bf16), ((LEN, 1), f32)
    a1, r1, x_mine, qr, kr, v, o, lse, peak, gain_rows, give, keep = call(
        forward_body,
        "attention_forward",
        [at, x_all, cosine, sine, segment_row, segment_col, *first, *second],
        [act, col, ((OWN, WIDTH), bf16), low, low, low, low, col, ((8, 128), f32), ((8, WIDTH), f32), part, part],
        [
            pltpu.VMEM((WIDTH, 3 * HEAD), bf16),
            pltpu.VMEM((WIDTH, HEAD), bf16),
            pltpu.VMEM((16, WIDTH), bf16),
            pltpu.SemaphoreType.DMA((48,)),
            pltpu.SemaphoreType.DMA((16,)),
        ],
        2 * LEN * WIDTH * 1024,
        anywhere=8,
    )
    give, keep, upstream, *done = lax.optimization_barrier(
        (give, keep, upstream, *wide_a, *wide_b, a_wide, b_wide, a_down, b_down)
    )
    wide_a, wide_b, (a_wide, b_wide, a_down, b_down) = done[:2], done[2:4], done[4:]
    attn_own = team_scatter(other_core(give), keep)
    halves = [shift(wide_a[0][:256], Y, -1), shift(wide_a[1][256:], Y, 1)]
    wide_a = [a_wide, wide_a[0], *halves, wide_a[1]]
    wide_b = [x_in(b_wide, *flip) for flip in FLIPS[:2]] + wide_b
    down_a = [shift(a_down, Y, -1), shift(a_down, Y, 1)]
    (dy,) = call(reorder_body, "order_upstream", [at, upstream], [((LEN, WIDTH), bf16)], [], 0)


    attn_own, dy, *done = lax.optimization_barrier((attn_own, dy, *wide_a, *wide_b, *down_a, b_wide, a_down, b_down))
    wide_a, wide_b, down_a, (b_wide, a_down, b_down) = done[:5], done[5:9], done[9:11], done[11:]
    down_b = [x_in(b_down, *flip) for flip in FLIPS]
    down_a = [a_down, down_a[0], shift(a_down, Y, 2), down_a[1]]
    hidden_own = x_mine.astype(f32) + attn_own
    hidden = team_gather(hidden_own.astype(bf16))
    wide = ((LEN, FF), bf16)
    block = ((512, FF), bf16)
    h_cols, a2, hid, dgate, dup, give, keep, up_2, up_3, gate_1, gate_3 = call(
        ffn_body,
        "feed_forward",
        [at, gain_rows, hidden, dy, *wide_a, *down_a, *wide_b, *down_b, b_wide, b_down],
        [low, act, wide, wide, wide, part, part, block, block, block, block],
        [
            *[pltpu.VMEM(*v) for v in (act, act, act, wide, wide, wide, part, part, block, block, block, block)],
            pltpu.VMEM((WIDTH, FF), bf16),
            pltpu.VMEM((WIDTH, FF), bf16),
            pltpu.VMEM((WIDTH, FF), bf16),
            pltpu.SemaphoreType.DMA((44,)),
            pltpu.SemaphoreType.DMA((16,)),
        ],
        14 * LEN * WIDTH * FF,
        anywhere=21,
        outs_anywhere=10,
    )
    other = other_core(give)
    wide_out, stack = ((512, FF), bf16), ((4 * LEN, HEAD), bf16)
    work = 2 * LEN * WIDTH * FF
    both = (keep.astype(f32) + other.astype(f32)).astype(bf16)
    normed_grad = lax.psum_scatter(both, Z, scatter_dimension=0, tiled=True).astype(f32)
    dgate, dup, hid = lax.optimization_barrier((dgate, dup, hid, both))[:3]
    got_up = [x_out(up_2, *FLIPS[2]), x_out(up_3, *FLIPS[3])]
    got_gate = [shift(gate_1, Y, 1), shift(gate_3, Y, 3)]
    rest = call(
        weight_rest_body,
        "weight_rest",
        [at, a2, dy, dgate, dup, hid],
        [wide_out] * 4 + [((512, hf), bf16)] * 8,
        [],
        work * 2,
    )
    out_give, out_keep = call(
        ffn_out_body,
        "feed_forward_out",
        [at, after(hid, rest[0]), *down_a, *down_b, b_down],
        [stack, stack],
        [pltpu.VMEM((WIDTH, FF), bf16), pltpu.SemaphoreType.DMA((20,))],
        work,
        anywhere=9,
    )
    normed_grad, out_give, out_keep, *got = lax.optimization_barrier(
        (normed_grad, out_give, out_keep, *got_up, *got_gate, *rest)
    )
    got_up, got_gate, gate_b, up_b = [got[2 * i : 2 * i + 2] for i in range(4)]
    down_g = got[8:]

    gain_two = gain_rows[1:2]
    factor_own = lax.rsqrt(jnp.mean(hidden_own * hidden_own, axis=1, keepdims=True) + norm_epsilon)
    grad_gain_two = jnp.sum(normed_grad * hidden_own * factor_own, axis=0)
    scaled = normed_grad * gain_two
    grad_res = (
        lax.dynamic_slice_in_dim(dy, mine * OWN, OWN, 0).astype(f32)
        + factor_own * scaled
        - hidden_own * factor_own**3 * jnp.mean(scaled * hidden_own, axis=1, keepdims=True)
    )
    grad_low = grad_res.astype(bf16)
    db = team_gather(grad_low)
    got_gate = [gate_b[0], shift(gate_b[1], Y, 2)] + got_gate
    got_up = [x_out(up_b[0], 0, 0), x_out(up_b[1], *FLIPS[1])] + got_up
    out_both = (out_keep.astype(f32) + other_core(out_give).astype(f32)).astype(bf16)
    db, out_both, *got = lax.optimization_barrier((db, out_both, *got_gate, *got_up, *down_g))
    got_gate, got_up, down_g = got[:4], got[4:8], got[8:]
    got_down_a = [shift(down_g[1], Y, 1), shift(down_g[3], Y, 3)]
    got_down_b = [x_out(block, *flip) for block, flip in zip(down_g[6:], FLIPS[2:])]

    db_cols, dqkv, row_part, gain_part, part_give, part_keep = call(
        backward_body,
        "attention_backward",
        [at, db, cosine, sine, segment_row, segment_col, qr, kr, v, lse, a1, gain_rows, *first, *second],
        [low, ((LEN, 3 * HEAD), bf16), col, ((1, WIDTH), f32), stack, stack],
        [
            pltpu.VMEM((WIDTH, 3 * HEAD), bf16),
            pltpu.VMEM((WIDTH, HEAD), bf16),
            pltpu.VMEM((LEN, HEAD), bf16),
            pltpu.VMEM((LEN, HEAD), f32),
            pltpu.VMEM((LEN, HEAD), f32),
            pltpu.SemaphoreType.DMA((48,)),
        ],
        2 * LEN * WIDTH * 1024,
        anywhere=8,
    )
    part_give, part_keep, dqkv, down_y, down_0, down_1, *got = lax.optimization_barrier(
        (part_give, part_keep, dqkv, down_g[2], down_g[4], down_g[5], *got_down_a, *got_down_b)
    )
    got_down_a = [down_g[0], shift(down_y, Y, 2), *got[:2]]
    got_down_b = [x_out(down_0, 0, 0), x_out(down_1, *FLIPS[1]), *got[2:]]
    part_other = other_core(part_give)
    message = ((896, 512), bf16)
    blocks = call(
        attention_weight_body,
        "attention_weights",
        [at, a1, dqkv, db, o, *got_gate, *got_up, up_b[0]],
        [message] * 8,
        [
            *[pltpu.VMEM((512, 512), bf16)] * 8,
            *[pltpu.VMEM((256, 512), bf16)] * 8,
            *[pltpu.VMEM((512, FF), bf16)] * 9,
            pltpu.SemaphoreType.DMA((9,)),
            pltpu.SemaphoreType.DMA((16,)),
        ],
        2 * LEN * WIDTH * 1024,
        anywhere=9,
        outs_anywhere=8,
    )
    part_keep, part_other, *got = lax.optimization_barrier((part_keep, part_other, *blocks, *got_down_a, *got_down_b))
    blocks, got_down_a, got_down_b = got[:8], got[8:12], got[12:]
    blocks = call(
        functools.partial(ffn_sum_body, 768),
        "feed_forward_sums_down",
        [at, *got_down_a, *got_down_b, down_0, *blocks],
        [message] * 8,
        [pltpu.VMEM((128, 512), bf16)] * 8 + [pltpu.SemaphoreType.DMA((8,))],
        0,
        anywhere=8,
        outs_anywhere=8,
        alias=8,
    )
    part_both = (part_keep.astype(f32) + part_other.astype(f32)).astype(bf16)
    attn_grad = lax.psum_scatter(part_both, Z, scatter_dimension=0, tiled=True).astype(f32)
    got_attn_a = [shift(blocks[1], Y, 1), shift(blocks[3], Y, 3)]
    got_attn_b = [x_out(blocks[4 + i], *FLIPS[i]) for i in (2, 3)]
    row_part = after(row_part, part_both)

    block_at = jnp.stack([((r // 4 - y) % 4) * 4 + ((r // 2 % 2) ^ lo) * 2 + ((r % 2) ^ hi) for r in range(16)])
    pick = (block_at[:, None] == jnp.arange(16)[None, :]).astype(f32)
    gain_parts = jnp.concatenate([gain_part.reshape(16, 128), grad_gain_two.reshape(16, 128)], 1)
    gain_parts = jnp.dot(pick, gain_parts, precision=lax.Precision.HIGHEST)
    peaks = jnp.where((jnp.arange(QUERY_HEADS) == mine)[:, None], peak, 0.0)
    small = jnp.concatenate([row_part.reshape(6, 128), gain_parts[:, :128], gain_parts[:, 128:], peaks], 0)
    is_peak = (jnp.arange(46) >= 38)[:, None]

    def join(values):
        total, most = values[0], values[0]
        for value in values[1:]:
            total, most = total + value, jnp.maximum(most, value)
        return jnp.where(is_peak[-total.shape[0] :], most, total)

    small = join([small, other_core(small)])
    small = join([small, z_other(small, 1)])

    rest = lax.optimization_barrier((blocks[2], blocks[4], blocks[5], small, *got_attn_a, *got_attn_b))
    (block_y, block_0, block_1, small), got_attn_a, got_attn_b = rest[:4], rest[4:6], rest[6:]
    got_attn_a = [blocks[0], shift(block_y, Y, 2), *got_attn_a]
    got_attn_b = [x_out(block_0, 0, 0), x_out(block_1, *FLIPS[1]), *got_attn_b]
    out_late = after(out_both, part_both)
    small = join([small, z_other(small, 2)])
    row_sum = small[:6].reshape(LEN, 1)
    small = small[6:]
    small = join([small, y_other(small, 1)])
    got_attn_a, got_attn_b, small, attn_grad = lax.optimization_barrier((got_attn_a, got_attn_b, small, attn_grad))
    ffn_own = lax.psum_scatter(out_late, Z, scatter_dimension=0, tiled=True).astype(f32)

    gain_pair = jnp.dot(pick, gain_rows[0].reshape(16, 128), precision=lax.Precision.HIGHEST)
    gain_cols = lax.dynamic_slice(gain_pair, (mine * 2, 0), (2, 128)).reshape(1, HEAD)
    grad_inputs = (
        db_cols.astype(f32) + r1 * attn_grad * gain_cols - x_own.astype(f32) * r1**2 * (row_sum / WIDTH)
    )
    home = [(h_cols.astype(f32) + ffn_own).astype(bf16), grad_inputs.astype(bf16)]
    home = swap(jnp.concatenate(home, 0))
    *sum_b, kv_give, kv_keep = call(
        join_body,
        "join_sums",
        [at, *got_attn_a, *got_attn_b, block_0],
        [((128, 512), bf16)] * 4 + [((512, HEAD), bf16), ((512, HEAD), f32)],
        [pltpu.VMEM((512, 512), bf16)] * 9 + [pltpu.SemaphoreType.DMA((9,))],
        0,
        anywhere=9,
    )
    kv_sum = (kv_keep + kv_partner(kv_give).astype(f32)).astype(bf16)
    sum_b = [sum_b[0]] + [shift(sum_b[i], Y, i) for i in (1, 2, 3)]
    first_y = sum_b[1]
    small = join([small, y_other(small, 2)])
    kv_sum, home, small, *sum_b = lax.optimization_barrier((kv_sum, home, small, *sum_b))
    high = lax.reduce_precision(small, 8, 7)
    rider = jnp.concatenate([high.astype(bf16), (small - high).astype(bf16)], 1)
    rider = jnp.pad(rider, ((0, 8), (0, 0)))
    rider = jnp.broadcast_to(rider[None], (4, 48, HEAD))
    last = jnp.concatenate([kv_sum.reshape(4, 128, HEAD), rider], 1).reshape(4 * 176, HEAD)
    sum_a = [x_out(last[i * 176 : (i + 1) * 176], *flip) for i, flip in enumerate(FLIPS)]
    grads = call(
        finish_body,
        "finish",
        [at, *got_attn_a, *got_attn_b, after(block_0, first_y)],
        [((128, FF), f32)] * 3,
        [pltpu.VMEM((384, 512), bf16)] * 9 + [pltpu.SemaphoreType.DMA((9,))],
        0,
        anywhere=9,
    )
    query, output, key, value, gain_one, gain_two, clipped_query, clipped_key = call(
        last_body,
        "last",
        [at, last[:176], *sum_a, *sum_b, w_query, w_key],
        [
            ((128, HEAD), f32),
            ((128, HEAD), f32),
            ((128, 128), f32),
            ((128, 128), f32),
            ((1, 128), f32),
            ((1, 128), f32),
            ((128, HEAD), bf16),
            ((128, 128), bf16),
        ],
        [pltpu.VMEM((48, 128), f32)],
        0,
    )
    return (
        home[:LEN],
        home[LEN:].astype(f32),
        gain_one.reshape(128),
        query,
        key,
        value,
        output,
        gain_two.reshape(128),
        grads[0],
        grads[1],
        grads[2],
        clipped_query,
        clipped_key,
    )


def solution(mesh):
    torus = Mesh(mesh.devices.reshape(4, 2, 2, 2, 4), (Y, XLO, CORE, XHI, Z))
    both, rows = P(TOK, MDL), P(TOK)
    return jax.shard_map(
        on_device,
        mesh=torus,
        in_specs=(both, P(TOK, None), rows, both, both, both, both, rows, both, both, both, both),
        out_specs=(both, both, rows, both, both, both, both, rows, both, both, both, both, both),
        check_vma=False,
    )
```

```python
import functools
import math

import jax
import jax.numpy as jnp
from jax import lax
from jax.experimental import pallas as pl
from jax.experimental.pallas import tpu as pltpu
from jax.sharding import Mesh
from jax.sharding import PartitionSpec as P

QUERY_HEADS = 8
HEAD = 256
WIDTH = 2048
LEN = 768
OWN = 96
FF = 1024
Y, XLO, CORE, XHI, Z = "tok_0", "tok_1", "tok_2", "mdl_0", "mdl_1"
TOK = (Y, XLO, CORE)
MDL = (XHI, Z)

norm_epsilon = 1e-06
rope_base = 1000042.0
logit_ceiling = 4.0
masked_value = -1e30
peak_floor_epsilon = 1e-06
SCALE = HEAD ** (-0.5)
nt = (((1,), (1,)), ((), ()))
tn = (((0,), (0,)), ((), ()))
f32 = jnp.float32
bf16 = jnp.bfloat16


def dot(a, b, dims=(((1,), (0,)), ((), ()))):
    return lax.dot_general(a, b, dims, preferred_element_type=f32)


def swap(a):
    got = lax.ppermute(a, (CORE, XHI), [(1, 2), (2, 1)])
    return jnp.where(lax.axis_index(CORE) == lax.axis_index(XHI), a, got)


def other_core(a):
    return lax.ppermute(a, CORE, [(0, 1), (1, 0)])


def shift(a, axis, by):
    return lax.ppermute(a, axis, [(i, (i + by) % 4) for i in range(4)])


def z_other(a, mask):
    return lax.ppermute(a, Z, [(i, i ^ mask) for i in range(4)])


def y_other(a, mask):
    return lax.ppermute(a, Y, [(i, i ^ mask) for i in range(4)])


def kv_partner(a):
    return lax.ppermute(a, Z, [(0, 1), (1, 0), (2, 3), (3, 2)])


def plane_pairs(flip_lo, flip_core):
    pairs = []
    for lo in range(2):
        for core in range(2):
            for hi in range(2):
                pairs.append((lo * 4 + core * 2 + hi, (lo ^ flip_lo) * 4 + hi * 2 + (core ^ flip_core)))
    return pairs


def x_pairs(flip_lo, flip_core, back):
    pairs = plane_pairs(flip_lo, flip_core)
    return [(there, here) if back else (here, there) for here, there in pairs if here != there]


def x_in(a, flip_lo, flip_core):
    return lax.ppermute(a, (XLO, CORE, XHI), x_pairs(flip_lo, flip_core, False))


def x_out(a, flip_lo, flip_core):
    return lax.ppermute(a, (XLO, CORE, XHI), x_pairs(flip_lo, flip_core, True))


def own_or(got, own):
    return jnp.where(lax.axis_index(CORE) == lax.axis_index(XHI), own, got)


FLIPS = ((0, 0), (0, 1), (1, 0), (1, 1))


def from_y(a):
    return [a, shift(a, Y, -1), shift(a, Y, 2), shift(a, Y, 1)]


def from_z(a):
    return [a, shift(a, Z, -1), shift(a, Z, 2), shift(a, Z, 1)]


def x_ring(a, mask):
    return lax.ppermute(a, (XLO, XHI), [(i, i ^ mask) for i in range(4)])


def total(pieces, cols=slice(None)):
    return sum(piece[:, cols].astype(f32) for piece in pieces)


def team_gather(own):
    return lax.all_gather(own, (CORE, Z), axis=0, tiled=True)


def team_scatter(other, keep):
    both = (keep.astype(f32) + other.astype(f32)).astype(bf16)
    return lax.psum_scatter(both, Z, scatter_dimension=0, tiled=True).astype(f32)


def after(value, *others):
    return lax.optimization_barrier((value, *others))[0]


def rope_tables(segment_row):
    earlier = jnp.sum((segment_row[None, :] < segment_row[:, None]).astype(jnp.int32), axis=1)
    places = jnp.arange(LEN, dtype=jnp.int32) - earlier
    half = HEAD // 2
    inverse = jnp.exp(jnp.arange(half, dtype=f32) * (-2.0 * math.log(rope_base) / HEAD))
    angles = places.astype(f32)[:, None] * inverse[None, :]
    return jnp.cos(angles), jnp.sin(angles)


def position(r, at):
    return (((r >> 2) - at[0]) & 3) * 4 + (((r >> 1) & 1) ^ at[1]) * 2 + ((r & 1) ^ at[2])


def lanes(index, size):
    return pl.ds(pl.multiple_of(index * size, size), size)


def owner(at, there, dz):
    return (at[3] ^ there) * 4 + ((at[4] + dz) & 3)


def kdot(a, b, dims=(((1,), (0,)), ((), ()))):
    return lax.dot_general(a, b, dims, preferred_element_type=f32)


def in_vmem(n):
    return [pl.BlockSpec(memory_space=pltpu.VMEM)] * n


def call(body, name, inputs, outs, scratch, flops, megabytes=56, anywhere=0, outs_anywhere=0, alias=0):
    moved = sum(v.size * v.dtype.itemsize for v in inputs[1:])
    moved += sum(math.prod(s) * jnp.dtype(d).itemsize for s, d in outs)
    specs = [pl.BlockSpec(memory_space=pltpu.SMEM)] + in_vmem(len(inputs) - 1 - anywhere)
    specs += [pl.BlockSpec(memory_space=pl.ANY)] * anywhere
    return list(pl.pallas_call(
        body,
        name=name,
        out_shape=[jax.ShapeDtypeStruct(s, d) for s, d in outs],
        in_specs=specs,
        out_specs=in_vmem(len(outs) - outs_anywhere) + [pl.BlockSpec(memory_space=pl.ANY)] * outs_anywhere,
        scratch_shapes=scratch,
        input_output_aliases={len(inputs) - alias + i: i for i in range(alias)},
        cost_estimate=pl.CostEstimate(flops=int(flops), bytes_accessed=int(moved), transcendentals=0),
        compiler_params=pltpu.CompilerParams(vmem_limit_bytes=megabytes * 2**20),
    )(*inputs))


def turn(values, cosine, sine):
    first, second = values[:, :128], values[:, 128:]
    return first * cosine - second * sine, second * cosine + first * sine


def attention_weights(a_refs, b_refs, w_qkv, w_o, sem):
    copies = []

    def move(source, to):
        copies.append(pltpu.make_async_copy(source, to, sem.at[len(copies)]))
        copies[-1].start()

    for i in range(4):
        for dy in range(4):
            rows = pl.ds((dy * 4 + i) * 128, 128)
            move(b_refs[i].at[pl.ds(dy * 144, 128), pl.ds(256, 256)], w_o.at[rows])
    for dy in range(4):
        for i in range(4):
            rows = pl.ds((dy * 4 + i) * 128, 128)
            move(b_refs[i].at[pl.ds(dy * 144, 128), pl.ds(0, 256)], w_qkv.at[rows, pl.ds(0, 256)])
            move(a_refs[dy].at[pl.ds(i * 128, 128)], w_qkv.at[rows, pl.ds(256, 512)])
    return copies


def along_y_body(at, *refs):
    gain_one, gain_two = refs[:2]
    w_query, w_output, w_up, w_down, out, sem = refs[2:]
    pairs = [
        (w_query, out.at[pl.ds(0, 128), pl.ds(0, 256)]),
        (w_output, out.at[pl.ds(0, 128), pl.ds(256, 256)]),
        (w_up.at[:, pl.ds(0, 512)], out.at[pl.ds(144, 128)]),
        (w_up.at[:, pl.ds(512, 512)], out.at[pl.ds(272, 128)]),
        (w_down.at[:, pl.ds(512, 512)], out.at[pl.ds(400, 128)]),
    ]
    copies = [pltpu.make_async_copy(a, b, sem.at[i]) for i, (a, b) in enumerate(pairs)]
    for copy in copies:
        copy.start()
    row = lax.broadcasted_iota(jnp.int32, (16, 128), 0)
    gains = jnp.where(row == 0, gain_one[...], jnp.where(row == 1, gain_two[...], 0.0))
    out[128:144, :128] = gains.astype(bf16)
    out[128:144, 128:] = jnp.zeros((16, 384), bf16)
    for copy in copies:
        copy.wait()


def along_x_body(at, *refs):
    riders, key, value, other, w_gate, w_down, out, sem = refs
    out[512:528, :256] = riders[...]
    out[512:528, 256:] = jnp.zeros((16, 256), bf16)
    pairs = [
        (w_gate.at[:, pl.ds(0, 512)], out.at[pl.ds(128, 128)]),
        (w_gate.at[:, pl.ds(512, 512)], out.at[pl.ds(256, 128)]),
        (w_down.at[:, pl.ds(0, 512)], out.at[pl.ds(384, 128)]),
    ]
    copies = [pltpu.make_async_copy(a, b, sem.at[i]) for i, (a, b) in enumerate(pairs)]
    for copy in copies:
        copy.start()
    odd = at[4] & 1
    out[:128, lanes(odd, 128)] = key[...]
    out[:128, lanes(1 - odd, 128)] = other[:, :128]
    out[:128, lanes(2 + odd, 128)] = value[...]
    out[:128, lanes(3 - odd, 128)] = other[:, 128:]
    for copy in copies:
        copy.wait()


def pack_body(at, *refs):
    xs, ys, to_y, to_x, sem = refs[:4], refs[4:8], refs[8], refs[9], refs[10]
    pairs = [(ref.at[pl.ds(0, 128)], to_y.at[pl.ds(128 * i, 128)]) for i, ref in enumerate(xs)]
    pairs += [(ref.at[pl.ds(0, 144)], to_x.at[pl.ds(144 * i, 144)]) for i, ref in enumerate(ys)]
    copies = [pltpu.make_async_copy(a, b, sem.at[i]) for i, (a, b) in enumerate(pairs)]
    for copy in copies:
        copy.start()
    for copy in copies:
        copy.wait()


def riders_body(at, *refs):
    xs, ys = refs[:4], refs[4:8]
    a_wide, b_wide, a_down, b_down, sem = refs[8:]
    copies = []
    for ref, row, wide, down in [(xs, 128, a_wide, a_down), (ys, 144, b_wide, b_down)]:
        for i in range(4):
            for j in range(3):
                source = ref[i].at[pl.ds(row + j * 128, 128)]
                rows = pl.ds(i * 128, 128)
                to = down.at[rows] if j == 2 else wide.at[rows, pl.ds(j * 512, 512)]
                copies.append(pltpu.make_async_copy(source, to, sem.at[len(copies)]))
    for copy in copies:
        copy.start()
    for copy in copies:
        copy.wait()


def allowed_block(i, seg_col, seg_row):
    rows, cols = 256, (i + 1) * 256
    same = seg_col[i * 256 : (i + 1) * 256, :] == seg_row[:, :cols]
    row = i * 256 + lax.broadcasted_iota(jnp.int32, (rows, cols), 0)
    return same & (row >= lax.broadcasted_iota(jnp.int32, (rows, cols), 1))


def forward_body(at, *refs):
    x, cosine, sine, seg_row, seg_col = refs[:5]
    a_refs, b_refs = refs[5:9], refs[9:13]
    a1, r1, x_mine, qr, kr, v, o, lse, peak, gains, give, keep = refs[13:25]
    w_qkv, w_o, gain_rows, sem, gain_sem = refs[25:]
    gain_copies = []
    for dy in range(4):
        for i in range(4):
            source = b_refs[i].at[pl.ds(dy * 144 + 128, 16), pl.ds(0, 128)]
            to = gain_rows.at[:, pl.ds((dy * 4 + i) * 128, 128)]
            gain_copies.append(pltpu.make_async_copy(source, to, gain_sem.at[len(gain_copies)]))
            gain_copies[-1].start()
    copies = attention_weights(a_refs, b_refs, w_qkv, w_o, sem)
    for copy in gain_copies:
        copy.wait()
    gains[...] = gain_rows[...].astype(f32)[:8]
    own = at[3] * 4 + at[4]
    for r in range(16):
        rows = pl.ds(pl.multiple_of((r // 2) * LEN + own * OWN, OWN), OWN)
        x_mine[:, lanes(position(r, at), 128)] = x[rows, (r % 2) * 128 : (r % 2 + 1) * 128]

    def norm(step, carry):
        rows = pl.ds(pl.multiple_of(step * 128, 128), 128)
        total = jnp.zeros((128, 1), f32)
        for m in range(8):
            value = x[pl.ds(pl.multiple_of(m * LEN + step * 128, 128), 128), :].astype(f32)
            total = total + jnp.sum(value * value, axis=1, keepdims=True)
        factor = lax.rsqrt(total / WIDTH + norm_epsilon)
        r1[rows, :] = factor
        for r in range(16):
            at_lanes = lanes(position(r, at), 128)
            from_rows = pl.ds(pl.multiple_of((r // 2) * LEN + step * 128, 128), 128)
            value = x[from_rows, (r % 2) * 128 : (r % 2 + 1) * 128].astype(f32)
            a1[rows, at_lanes] = (value * factor * gains[0:1, at_lanes]).astype(bf16)
        return carry

    lax.fori_loop(0, 6, norm, 0)
    for copy in copies:
        copy.wait()
    for i in range(3):
        rows = slice(i * 256, (i + 1) * 256)
        qk = kdot(a1[rows, :], w_qkv[:, :512])
        cos_i, sin_i = cosine[rows, :], sine[rows, :]
        for ref, at_col in ((qr, 0), (kr, 256)):
            one, two = turn(qk[:, at_col : at_col + 256], cos_i, sin_i)
            ref[rows, :128] = one.astype(bf16)
            ref[rows, 128:] = two.astype(bf16)
        v[rows, :] = kdot(a1[rows, :], w_qkv[:, 512:]).astype(bf16)
    largest = jnp.zeros((1, 1), f32)
    for i in range(3):
        rows, cols = slice(i * 256, (i + 1) * 256), (i + 1) * 256
        allowed = allowed_block(i, seg_col, seg_row)
        scores = kdot(qr[rows, :], kr[:cols, :], nt) * SCALE
        masked = jnp.where(allowed, scores, masked_value)
        size = jnp.where(allowed, jnp.abs(scores), 0.0)
        largest = jnp.maximum(largest, jnp.max(jnp.max(size, axis=1, keepdims=True), axis=0, keepdims=True))
        top = jnp.max(masked, axis=1, keepdims=True)
        log_total = top + jnp.log(jnp.sum(jnp.exp(masked - top), axis=1, keepdims=True))
        lse[rows, :] = log_total
        probs = jnp.exp(masked - log_total).astype(bf16)
        o[rows, :] = kdot(probs, v[:cols, :]).astype(bf16)
    peak[...] = jnp.broadcast_to(largest, (8, 128))
    for ref, c in ((give, 1 - at[3]), (keep, at[3])):
        rows = pl.ds(pl.multiple_of(c * 384, 384), 384)
        for half in range(2):
            cols = slice(half * 1024, (half + 1) * 1024)
            ref[:, cols] = kdot(o[rows, :], w_o[cols, :], nt).astype(bf16)


def reorder_body(at, whole, out):
    for r in range(16):
        rows = slice((r // 2) * LEN, (r // 2 + 1) * LEN)
        out[:, lanes(position(r, at), 128)] = whole[rows, (r % 2) * 128 : (r % 2 + 1) * 128]


def start_either(at, own, got, to, sem):
    mine = at[2] == at[3]

    @pl.when(mine)
    def _():
        pltpu.make_async_copy(own, to, sem).start()

    @pl.when(jnp.logical_not(mine))
    def _():
        pltpu.make_async_copy(got, to, sem).start()

    return pltpu.make_async_copy(got, to, sem)


def rows_a(refs, to_ref, cols, sem, copies):
    row = 0
    for ref in refs:
        to = to_ref.at[pl.ds(row, ref.shape[0]), cols]
        row += ref.shape[0]
        copies.append(pltpu.make_async_copy(ref, to, sem.at[len(copies)]))
        copies[-1].start()


def rows_b(at, own, refs, to_ref, cols, sem, copies):
    for i, ref in enumerate(refs):
        for j in range(4):
            to = to_ref.at[pl.ds((j * 4 + i) * 128, 128), cols]
            rows = pl.ds(j * 128, 128)
            if i == 0:
                copies.append(start_either(at, own.at[rows], ref.at[rows], to, sem.at[len(copies)]))
            else:
                copies.append(pltpu.make_async_copy(ref.at[rows], to, sem.at[len(copies)]))
                copies[-1].start()


def ffn_body(at, *refs):
    gains, h_in, dy_in = refs[:3]
    wide_a, (down_a, wide_b, down_b) = refs[3:8], [refs[8 + 4 * i : 12 + 4 * i] for i in range(3)]
    own_wide, own_down = refs[20:22]
    h_cols, a2_out, hid_out, dgate_out, dup_out, give_out, keep_out = refs[22:29]
    up_outs, gate_outs = refs[29:31], refs[31:33]
    h, dy, a2, hid, dgate, dup, give, keep, up_0, up_1, gate_0, gate_1 = refs[33:45]
    w_gate, w_up, w_down, sem, out_sem = refs[45:]
    h_copy = pltpu.make_async_copy(h_in, h, out_sem.at[14])
    h_copy.start()
    copies = []
    rows_a(wide_a, w_gate, pl.ds(0, FF), sem, copies)
    rows_b(at, own_wide, wide_b, w_up, pl.ds(0, FF), sem, copies)
    rows_a(down_a, w_down, pl.ds(0, 512), sem, copies)
    rows_b(at, own_down, down_b, w_down, pl.ds(512, 512), sem, copies)
    copies.append(pltpu.make_async_copy(dy_in, dy, out_sem.at[15]))
    copies[-1].start()
    sent = []

    def send(source, to):
        sent.append(pltpu.make_async_copy(source, to, out_sem.at[len(sent)]))
        sent[-1].start()

    h_copy.wait()
    own = at[3] * 4 + at[4]
    for j in range(2):
        h_cols[:, j * 128 : (j + 1) * 128] = h[:, lanes(position(2 * own + j, at), 128)]
    for i in range(6):
        rows = slice(i * 128, (i + 1) * 128)
        value = h[rows, :].astype(f32)
        factor = lax.rsqrt(jnp.mean(value * value, axis=1, keepdims=True) + norm_epsilon)
        a2[rows, :] = (value * factor * gains[1:2, :]).astype(bf16)
    send(a2, a2_out)
    for copy in copies:
        copy.wait()
    for j in range(4):
        cols = slice(j * 256, (j + 1) * 256)
        gate = kdot(a2[...], w_gate[:, cols])
        up = kdot(a2[...], w_up[:, cols])
        grad = kdot(dy[...], w_down[:, cols])
        sig = 1.0 / (1.0 + jnp.exp(-gate))
        act = gate * sig
        hid[:, cols] = (act * up).astype(bf16)
        dgate[:, cols] = (grad * up * sig * (1.0 + gate * (1.0 - sig))).astype(bf16)
        dup[:, cols] = (grad * act).astype(bf16)
    for source, to in ((hid, hid_out), (dgate, dgate_out), (dup, dup_out)):
        send(source, to)
    for ref, to, c in ((give, give_out, 1 - at[3]), (keep, keep_out, at[3])):
        rows = pl.ds(pl.multiple_of(c * 384, 384), 384)
        for j in range(4):
            cols = slice(j * 512, (j + 1) * 512)
            ref[:, cols] = (
                kdot(dgate[rows, :], w_gate[cols, :], nt) + kdot(dup[rows, :], w_up[cols, :], nt)
            ).astype(bf16)
        send(ref, to)
    for i, ref, to in ((1, gate_0, gate_outs[0]), (3, gate_1, gate_outs[1])):
        for j in range(2):
            n = slice(j * 512, (j + 1) * 512)
            ref[:, n] = kdot(a2[:, i * 512 : (i + 1) * 512], dgate[:, n], tn).astype(bf16)
        send(ref, to)
    for i in range(4):
        cols = slice((i * 4 + 2) * 128, (i * 4 + 4) * 128)
        for j in range(2):
            n = slice(j * 512, (j + 1) * 512)
            value = kdot(a2[:, cols], dup[:, n], tn).astype(bf16)
            up_0[i * 128 : (i + 1) * 128, n] = value[:128]
            up_1[i * 128 : (i + 1) * 128, n] = value[128:]
    send(up_0, up_outs[0])
    send(up_1, up_outs[1])
    for copy in sent:
        copy.wait()


def ffn_out_body(at, hid, *refs):
    down_a, down_b, own_down = refs[:4], refs[4:8], refs[8]
    give, keep, w_down, sem = refs[9:]
    copies = []
    rows_a(down_a, w_down, pl.ds(0, 512), sem, copies)
    rows_b(at, own_down, down_b, w_down, pl.ds(512, 512), sem, copies)
    for copy in copies:
        copy.wait()
    for ref, c in ((give, 1 - at[3]), (keep, at[3])):
        for dz in range(4):
            m = c * 4 + dz
            pair = pl.ds(pl.multiple_of((position(2 * m, at) >> 1) * 256, 256), 256)
            value = kdot(hid[...], w_down[pair, :], nt)
            rows = slice(dz * LEN, (dz + 1) * LEN)
            for j in range(2):
                ref[rows, lanes(at[2] ^ j, 128)] = value[:, j * 128 : (j + 1) * 128].astype(bf16)


def weight_rest_body(at, a2, dy, dgate, dup, hid, *outs):
    a_wide, b_wide, a_down, b_down = outs[:2], outs[2:4], outs[4:8], outs[8:]
    for i in range(4):
        cols, rows = slice(i * 512, (i + 1) * 512), slice(i * 128, (i + 1) * 128)
        for j in range(2):
            n = slice(j * 512, (j + 1) * 512)
            value = kdot(a2[:, i * 512 : i * 512 + 256], dup[:, n], tn).astype(bf16)
            for k in range(2):
                b_wide[k][rows, n] = value[k * 128 : (k + 1) * 128]
            if i % 2 == 0:
                a_wide[i // 2][:, n] = kdot(a2[:, cols], dgate[:, n], tn).astype(bf16)
        a_down[i][...] = kdot(dy[:, cols], hid[:, :512], tn).astype(bf16)
        value = kdot(dy[:, cols], hid[:, 512:], tn).astype(bf16)
        for k in range(4):
            b_down[k][rows, :] = value[k * 128 : (k + 1) * 128]


def backward_body(at, *refs):
    db, cosine, sine, seg_row, seg_col, qr, kr, v, lse, a1, gains = refs[:11]
    a_refs, b_refs = refs[11:15], refs[15:19]
    db_cols, dqkv, row_part, gain_part, give, keep = refs[19:25]
    w_qkv, w_o, d_o, dk_sum, dv_sum, sem = refs[25:]
    copies = attention_weights(a_refs, b_refs, w_qkv, w_o, sem)
    own = at[3] * 4 + at[4]
    for j in range(2):
        db_cols[:, j * 128 : (j + 1) * 128] = db[:, lanes(position(2 * own + j, at), 128)]
    for copy in copies:
        copy.wait()
    for i in range(3):
        rows = slice(i * 256, (i + 1) * 256)
        d_o[rows, :] = kdot(db[rows, :], w_o[...]).astype(bf16)
    for i in (2, 1, 0):
        rows, cols = slice(i * 256, (i + 1) * 256), (i + 1) * 256
        allowed = allowed_block(i, seg_col, seg_row)
        scores = kdot(qr[rows, :], kr[:cols, :], nt) * SCALE
        probs = jnp.exp(jnp.where(allowed, scores, masked_value) - lse[rows, :])
        low = probs.astype(bf16)
        dp = kdot(d_o[rows, :], v[:cols, :], nt)
        delta = jnp.sum(dp * probs, axis=1, keepdims=True)
        ds = (probs * (dp - delta)).astype(bf16)
        dq = kdot(ds, kr[:cols, :]) * SCALE
        row_part[rows, :] = jnp.sum(dq * qr[rows, :].astype(f32), axis=1, keepdims=True)
        one, two = turn(dq, cosine[rows, :], -sine[rows, :])
        dqkv[rows, :128] = one.astype(bf16)
        dqkv[rows, 128:256] = two.astype(bf16)
        dk_new = kdot(ds, qr[rows, :], tn)
        dv_new = kdot(low, d_o[rows, :], tn)
        if i == 2:
            dk_sum[...] = dk_new
            dv_sum[...] = dv_new
        else:
            dk_sum[:cols, :] = dk_sum[:cols, :] + dk_new
            dv_sum[:cols, :] = dv_sum[:cols, :] + dv_new
    for i in range(3):
        rows = slice(i * 256, (i + 1) * 256)
        dk = dk_sum[rows, :] * SCALE
        dv_i = dv_sum[rows, :]
        row_part[rows, :] = (
            row_part[rows, :]
            + jnp.sum(dk * kr[rows, :].astype(f32), axis=1, keepdims=True)
            + jnp.sum(dv_i * v[rows, :].astype(f32), axis=1, keepdims=True)
        )
        one, two = turn(dk, cosine[rows, :], -sine[rows, :])
        dqkv[rows, 256:384] = one.astype(bf16)
        dqkv[rows, 384:512] = two.astype(bf16)
        dqkv[rows, 512:] = dv_i.astype(bf16)
    for m, ref in [(j, give) for j in range(4)] + [(j, keep) for j in range(4)]:
        half = 1 - at[3] if ref is give else at[3]
        pair = lanes(position(2 * (half * 4 + m), at) >> 1, 256)
        value = kdot(dqkv[...], w_qkv[pair, :], nt)
        gain_part[:, pair] = jnp.sum(value * a1[:, pair].astype(f32), axis=0, keepdims=True) / gains[0:1, pair]
        rows = slice(m * LEN, (m + 1) * LEN)
        for j in range(2):
            ref[rows, lanes(at[2] ^ j, 128)] = value[:, j * 128 : (j + 1) * 128].astype(bf16)


def wide_sums(at, a, b, own, values):
    for i in range(4):
        rows = slice(i * 128, (i + 1) * 128)
        head = jnp.where(at[2] == at[3], own[rows, :], b[0][rows, :])
        of_b = head.astype(f32) + b[1][rows, :].astype(f32) + b[2][rows, :].astype(f32) + b[3][rows, :].astype(f32)
        of_a = a[0][rows, :].astype(f32) + a[1][rows, :].astype(f32) + a[2][rows, :].astype(f32) + a[3][rows, :].astype(f32)
        for value, total_ in ((values[i], of_b), (values[4 + i], of_a)):
            for j in range(2):
                value[j * 128 : (j + 1) * 128, :] = total_[:, j * 512 : (j + 1) * 512].astype(bf16)


def attention_weight_body(at, a1, dqkv, db, o, *refs):
    pieces, outs, values, sums = refs[:9], refs[9:17], refs[17:25], refs[25:33]
    held, sem, out_sem = refs[33:42], refs[42], refs[43]
    arriving = [pltpu.make_async_copy(x, v, sem.at[i]) for i, (x, v) in enumerate(zip(pieces, held))]
    for copy in arriving:
        copy.start()
    sent = []

    def send(source, to):
        sent.append(pltpu.make_async_copy(source, to, out_sem.at[len(sent)]))
        sent[-1].start()

    for i in range(4):
        cols, rows = slice(i * 512, (i + 1) * 512), slice(i * 128, (i + 1) * 128)
        values[i][...] = kdot(a1[:, cols], dqkv[:, 256:], tn).astype(bf16)
        send(values[i], outs[i].at[pl.ds(0, 512)])
        for n, left, right in ((slice(0, 256), a1, dqkv.at[:, :256]), (slice(256, 512), db, o)):
            value = kdot(left[:, cols], right[...], tn).astype(bf16)
            for k in range(4):
                values[4 + k][rows, n] = value[k * 128 : (k + 1) * 128]
    for i in range(4, 8):
        send(values[i], outs[i].at[pl.ds(0, 512)])
    for copy in arriving:
        copy.wait()
    wide_sums(at, held[:4], held[4:8], held[8], sums)
    for i in range(8):
        send(sums[i], outs[i].at[pl.ds(512, 256)])
    for copy in sent:
        copy.wait()


def ffn_sum_body(row, at, *refs):
    a, b, own, outs, values, sem = refs[:4], refs[4:8], refs[8], refs[17:25], refs[25:33], refs[33]
    mine = at[2] == at[3]
    copies = []
    for i in range(4):
        rows = slice(i * 128, (i + 1) * 128)
        head = jnp.where(mine, own[rows, :], b[0][rows, :])
        for value, terms in ((values[i], [b[k][rows, :] for k in (1, 2, 3)]), (values[4 + i], [a[k][rows, :] for k in (1, 2, 3)])):
            first = head if value is values[i] else a[0][rows, :]
            total = first.astype(f32) + terms[0].astype(f32) + terms[1].astype(f32) + terms[2].astype(f32)
            for j in range(total.shape[1] // 512):
                value[j * 128 : (j + 1) * 128, :] = total[:, j * 512 : (j + 1) * 512].astype(bf16)
    for i in range(8):
        to = outs[i].at[pl.ds(row, values[i].shape[0])]
        copies.append(pltpu.make_async_copy(values[i], to, sem.at[i]))
        copies[-1].start()
    for copy in copies:
        copy.wait()


def join_body(at, *refs):
    a, b, own, outs = refs[:4], refs[4:8], refs[8], refs[9:13]
    kv_give, kv_keep, va, vb, v_own, sem = refs[13], refs[14], refs[15:19], refs[19:23], refs[23], refs[24]
    pairs = list(zip([*a, *b, own], [*va, *vb, v_own]))
    copies = [pltpu.make_async_copy(x.at[pl.ds(0, 512)], v, sem.at[i]) for i, (x, v) in enumerate(pairs)]
    for copy in copies:
        copy.start()
    for copy in copies:
        copy.wait()
    odd = (at[4] & 1) == 1
    for i in range(4):
        rows = slice(i * 128, (i + 1) * 128)
        head = jnp.where(at[2] == at[3], v_own[rows, :], vb[0][rows, :])
        value = head.astype(f32) + vb[1][rows, :].astype(f32) + vb[2][rows, :].astype(f32) + vb[3][rows, :].astype(f32)
        outs[i][...] = value.astype(bf16)
        value = va[0][rows, :].astype(f32) + va[1][rows, :].astype(f32) + va[2][rows, :].astype(f32) + va[3][rows, :].astype(f32)
        for half in range(2):
            one, two = value[:, half * 256 : half * 256 + 128], value[:, half * 256 + 128 : (half + 1) * 256]
            n = slice(half * 128, (half + 1) * 128)
            kv_keep[rows, n] = jnp.where(odd, two, one)
            kv_give[rows, n] = jnp.where(odd, one, two).astype(bf16)


def finish_body(at, *refs):
    a, b, own = refs[:4], refs[4:8], refs[8]
    gate, up, down, va, vb, v_own, sem = refs[9], refs[10], refs[11], refs[12:16], refs[16:20], refs[20], refs[21]
    pairs = list(zip([*a, *b, own], [*va, *vb, v_own]))
    copies = [pltpu.make_async_copy(x.at[pl.ds(512, 384)], v, sem.at[i]) for i, (x, v) in enumerate(pairs)]
    for copy in copies:
        copy.start()
    for copy in copies:
        copy.wait()
    mine = at[2] == at[3]
    for j in range(3):
        rows = slice(j * 128, (j + 1) * 128)
        head = jnp.where(mine, v_own[rows, :], vb[0][rows, :])
        of_a = head.astype(f32) + vb[1][rows, :].astype(f32) + vb[2][rows, :].astype(f32) + vb[3][rows, :].astype(f32)
        of_b = va[0][rows, :].astype(f32) + va[1][rows, :].astype(f32) + va[2][rows, :].astype(f32) + va[3][rows, :].astype(f32)
        if j < 2:
            gate[:, j * 512 : (j + 1) * 512] = of_a
            up[:, j * 512 : (j + 1) * 512] = of_b
        else:
            down[:, :512] = of_a
            down[:, 512:] = of_b


def last_body(at, *refs):
    own, a, b, w_query, w_key = refs[0], refs[1:5], refs[5:9], refs[9], refs[10]
    query, output, key, value, gain_one, gain_two, clipped_query, clipped_key, small = refs[11:]
    a = [jnp.where(at[2] == at[3], own[...], a[0][...]), a[1][...], a[2][...], a[3][...]]
    kv = a[0][:128].astype(f32) + a[1][:128].astype(f32) + a[2][:128].astype(f32) + a[3][:128].astype(f32)
    key[...] = kv[:, :128]
    value[...] = kv[:, 128:]
    parts = [piece[128:, :128].astype(f32) + piece[128:, 128:].astype(f32) for piece in a]
    added = parts[0] + parts[1] + parts[2] + parts[3]
    most = jnp.maximum(jnp.maximum(parts[0], parts[1]), jnp.maximum(parts[2], parts[3]))
    small[...] = jnp.where(lax.broadcasted_iota(jnp.int32, (48, 128), 0) >= 32, most, added)
    tok, head = at[0] * 4 + at[1] * 2 + at[3], at[2] * 4 + at[4]
    gain_one[...] = small[pl.ds(tok, 1), :]
    gain_two[...] = small[pl.ds(16 + tok, 1), :]
    peak = small[pl.ds(32 + head, 1), :]
    pair = jnp.maximum(peak, small[pl.ds(32 + (head ^ 1), 1), :])
    scale = jnp.sqrt(logit_ceiling / (peak + peak_floor_epsilon))
    for j in range(2):
        cols = slice(j * 128, (j + 1) * 128)
        clipped_query[:, cols] = (w_query[:, cols].astype(f32) * scale).astype(bf16)
    scale = jnp.sqrt(logit_ceiling / (pair + peak_floor_epsilon))
    clipped_key[...] = (w_key[...].astype(f32) * scale).astype(bf16)
    total_b = b[0][...].astype(f32) + b[1][...].astype(f32) + b[2][...].astype(f32) + b[3][...].astype(f32)
    query[...] = total_b[:, :256]
    output[...] = total_b[:, 256:]


def on_device(
    tokens,
    segments,
    gain_attn,
    w_query,
    w_key,
    w_value,
    w_output,
    gain_ffn,
    w_gate,
    w_up,
    w_down,
    cotangent,
):
    y, lo, core = lax.axis_index(Y), lax.axis_index(XLO), lax.axis_index(CORE)
    hi, z = lax.axis_index(XHI), lax.axis_index(Z)
    at = jnp.stack([y, lo, hi, core, z]).astype(jnp.int32)
    mine = core * 4 + z

    riders = jnp.zeros((16, HEAD), bf16).at[:3].set(segments.reshape(3, HEAD).astype(bf16))
    hf = FF // 2
    odd = z % 2 == 1
    half = HEAD // 2
    kv_other = kv_partner(jnp.concatenate([w_key, w_value], 1))
    (y_rows,) = call(
        along_y_body,
        "lay_out_y",
        [
            at,
            after(gain_attn.astype(f32).reshape(1, 128), kv_other),
            gain_ffn.astype(f32).reshape(1, 128),
            w_query,
            w_output,
            w_up,
            w_down,
        ],
        [((528, 2 * HEAD), bf16)],
        [pltpu.SemaphoreType.DMA((5,))],
        0,
        anywhere=4,
    )
    (x_rows,) = call(
        along_x_body,
        "lay_out_x",
        [at, riders, w_key, w_value, kv_other, w_gate, w_down],
        [((528, 2 * HEAD), bf16)],
        [pltpu.SemaphoreType.DMA((3,))],
        0,
        anywhere=2,
    )
    x_own, upstream_own = swap(tokens), swap(cotangent)
    along_y = [shift(y_rows, Y, -1), shift(y_rows, Y, 1)]
    along_x = [x_in(x_rows, *flip) for flip in FLIPS[2:]]
    x_own, upstream_own, late_y, late_x, *rest = lax.optimization_barrier(
        (x_own, upstream_own, y_rows, x_rows, *along_y, *along_x)
    )
    along_y = [y_rows, rest[0], shift(late_y, Y, 2), rest[1]]
    along_x = [own_or(x_in(late_x, 0, 0), x_rows), x_in(late_x, *FLIPS[1]), *rest[2:]]
    rest = lax.optimization_barrier((*along_x, *along_y))
    to_y, to_x = call(
        pack_body,
        "pack",
        [at, *rest],
        [((512, 2 * HEAD), bf16), ((576, 2 * HEAD), bf16)],
        [pltpu.SemaphoreType.DMA((8,))],
        0,
        anywhere=8,
    )
    a_wide, b_wide, a_down, b_down = call(
        riders_body,
        "riders",
        [at, *rest],
        [((512, FF), bf16)] * 2 + [((512, hf), bf16)] * 2,
        [pltpu.SemaphoreType.DMA((24,))],
        0,
        anywhere=8,
    )
    x_all = team_gather(x_own)
    upstream = team_gather(after(upstream_own, to_x))
    segment_row = rest[0][512:515, :HEAD].astype(f32).reshape(1, LEN)
    segment_col = segment_row.reshape(LEN, 1)
    cosine, sine = rope_tables(segment_row[0])
    first = [shift(to_y, Y, -1), shift(to_y, Y, 1)]
    second = [x_in(to_x, *flip) for flip in FLIPS[2:]]
    late_y, late_x, *rest = lax.optimization_barrier((to_y, to_x, *first, *second))
    first, second = rest[:2], rest[2:]
    first = [to_y, first[0], shift(late_y, Y, 2), first[1]]
    second = [own_or(x_in(late_x, 0, 0), to_x), x_in(late_x, *FLIPS[1])] + second
    x_all, cosine, sine, segment_row, segment_col, *rest = lax.optimization_barrier(
        (x_all, cosine, sine, segment_row, segment_col, *first, *second, a_wide, b_wide, a_down, b_down)
    )
    first, second, (a_wide, b_wide, a_down, b_down) = rest[:4], rest[4:8], rest[8:]
    wide_a = [shift(a_wide, Y, -1), shift(a_wide, Y, 1)]
    wide_b = [x_in(b_wide, *flip) for flip in FLIPS[2:]]

    part = ((LEN // 2, WIDTH), bf16)
    act, low, col = ((LEN, WIDTH), bf16), ((LEN, HEAD), bf16), ((LEN, 1), f32)
    a1, r1, x_mine, qr, kr, v, o, lse, peak, gain_rows, give, keep = call(
        forward_body,
        "attention_forward",
        [at, x_all, cosine, sine, segment_row, segment_col, *first, *second],
        [act, col, ((OWN, WIDTH), bf16), low, low, low, low, col, ((8, 128), f32), ((8, WIDTH), f32), part, part],
        [
            pltpu.VMEM((WIDTH, 3 * HEAD), bf16),
            pltpu.VMEM((WIDTH, HEAD), bf16),
            pltpu.VMEM((16, WIDTH), bf16),
            pltpu.SemaphoreType.DMA((48,)),
            pltpu.SemaphoreType.DMA((16,)),
        ],
        2 * LEN * WIDTH * 1024,
        anywhere=8,
    )
    give, keep, upstream, *done = lax.optimization_barrier(
        (give, keep, upstream, *wide_a, *wide_b, a_wide, b_wide, a_down, b_down)
    )
    wide_a, wide_b, (a_wide, b_wide, a_down, b_down) = done[:2], done[2:4], done[4:]
    attn_own = team_scatter(other_core(give), keep)
    halves = [shift(wide_a[0][:256], Y, -1), shift(wide_a[1][256:], Y, 1)]
    wide_a = [a_wide, wide_a[0], *halves, wide_a[1]]
    wide_b = [x_in(b_wide, *flip) for flip in FLIPS[:2]] + wide_b
    down_a = [shift(a_down, Y, -1), shift(a_down, Y, 1)]
    (dy,) = call(reorder_body, "order_upstream", [at, upstream], [((LEN, WIDTH), bf16)], [], 0)


    attn_own, dy, *done = lax.optimization_barrier((attn_own, dy, *wide_a, *wide_b, *down_a, b_wide, a_down, b_down))
    wide_a, wide_b, down_a, (b_wide, a_down, b_down) = done[:5], done[5:9], done[9:11], done[11:]
    down_b = [x_in(b_down, *flip) for flip in FLIPS]
    down_a = [a_down, down_a[0], shift(a_down, Y, 2), down_a[1]]
    hidden_own = x_mine.astype(f32) + attn_own
    hidden = team_gather(hidden_own.astype(bf16))
    wide = ((LEN, FF), bf16)
    block = ((512, FF), bf16)
    h_cols, a2, hid, dgate, dup, give, keep, up_2, up_3, gate_1, gate_3 = call(
        ffn_body,
        "feed_forward",
        [at, gain_rows, hidden, dy, *wide_a, *down_a, *wide_b, *down_b, b_wide, b_down],
        [low, act, wide, wide, wide, part, part, block, block, block, block],
        [
            *[pltpu.VMEM(*v) for v in (act, act, act, wide, wide, wide, part, part, block, block, block, block)],
            pltpu.VMEM((WIDTH, FF), bf16),
            pltpu.VMEM((WIDTH, FF), bf16),
            pltpu.VMEM((WIDTH, FF), bf16),
            pltpu.SemaphoreType.DMA((44,)),
            pltpu.SemaphoreType.DMA((16,)),
        ],
        14 * LEN * WIDTH * FF,
        anywhere=21,
        outs_anywhere=10,
    )
    other = other_core(give)
    wide_out, stack = ((512, FF), bf16), ((4 * LEN, HEAD), bf16)
    work = 2 * LEN * WIDTH * FF
    both = (keep.astype(f32) + other.astype(f32)).astype(bf16)
    normed_grad = lax.psum_scatter(both, Z, scatter_dimension=0, tiled=True).astype(f32)
    dgate, dup, hid = lax.optimization_barrier((dgate, dup, hid, both))[:3]
    got_up = [x_out(up_2, *FLIPS[2]), x_out(up_3, *FLIPS[3])]
    got_gate = [shift(gate_1, Y, 1), shift(gate_3, Y, 3)]
    rest = call(
        weight_rest_body,
        "weight_rest",
        [at, a2, dy, dgate, dup, hid],
        [wide_out] * 4 + [((512, hf), bf16)] * 8,
        [],
        work * 2,
    )
    out_give, out_keep = call(
        ffn_out_body,
        "feed_forward_out",
        [at, after(hid, rest[0]), *down_a, *down_b, b_down],
        [stack, stack],
        [pltpu.VMEM((WIDTH, FF), bf16), pltpu.SemaphoreType.DMA((20,))],
        work,
        anywhere=9,
    )
    normed_grad, out_give, out_keep, *got = lax.optimization_barrier(
        (normed_grad, out_give, out_keep, *got_up, *got_gate, *rest)
    )
    got_up, got_gate, gate_b, up_b = [got[2 * i : 2 * i + 2] for i in range(4)]
    down_g = got[8:]

    gain_two = gain_rows[1:2]
    factor_own = lax.rsqrt(jnp.mean(hidden_own * hidden_own, axis=1, keepdims=True) + norm_epsilon)
    grad_gain_two = jnp.sum(normed_grad * hidden_own * factor_own, axis=0)
    scaled = normed_grad * gain_two
    grad_res = (
        lax.dynamic_slice_in_dim(dy, mine * OWN, OWN, 0).astype(f32)
        + factor_own * scaled
        - hidden_own * factor_own**3 * jnp.mean(scaled * hidden_own, axis=1, keepdims=True)
    )
    grad_low = grad_res.astype(bf16)
    db = team_gather(grad_low)
    got_gate = [gate_b[0], shift(gate_b[1], Y, 2)] + got_gate
    got_up = [x_out(up_b[0], 0, 0), x_out(up_b[1], *FLIPS[1])] + got_up
    out_both = (out_keep.astype(f32) + other_core(out_give).astype(f32)).astype(bf16)
    db, out_both, *got = lax.optimization_barrier((db, out_both, *got_gate, *got_up, *down_g))
    got_gate, got_up, down_g = got[:4], got[4:8], got[8:]
    got_down_a = [shift(down_g[1], Y, 1), shift(down_g[3], Y, 3)]
    got_down_b = [x_out(block, *flip) for block, flip in zip(down_g[6:], FLIPS[2:])]

    db_cols, dqkv, row_part, gain_part, part_give, part_keep = call(
        backward_body,
        "attention_backward",
        [at, db, cosine, sine, segment_row, segment_col, qr, kr, v, lse, a1, gain_rows, *first, *second],
        [low, ((LEN, 3 * HEAD), bf16), col, ((1, WIDTH), f32), stack, stack],
        [
            pltpu.VMEM((WIDTH, 3 * HEAD), bf16),
            pltpu.VMEM((WIDTH, HEAD), bf16),
            pltpu.VMEM((LEN, HEAD), bf16),
            pltpu.VMEM((LEN, HEAD), f32),
            pltpu.VMEM((LEN, HEAD), f32),
            pltpu.SemaphoreType.DMA((48,)),
        ],
        2 * LEN * WIDTH * 1024,
        anywhere=8,
    )
    part_give, part_keep, dqkv, down_y, down_0, down_1, *got = lax.optimization_barrier(
        (part_give, part_keep, dqkv, down_g[2], down_g[4], down_g[5], *got_down_a, *got_down_b)
    )
    got_down_a = [down_g[0], shift(down_y, Y, 2), *got[:2]]
    got_down_b = [x_out(down_0, 0, 0), x_out(down_1, *FLIPS[1]), *got[2:]]
    part_other = other_core(part_give)
    message = ((896, 512), bf16)
    blocks = call(
        attention_weight_body,
        "attention_weights",
        [at, a1, dqkv, db, o, *got_gate, *got_up, up_b[0]],
        [message] * 8,
        [
            *[pltpu.VMEM((512, 512), bf16)] * 8,
            *[pltpu.VMEM((256, 512), bf16)] * 8,
            *[pltpu.VMEM((512, FF), bf16)] * 9,
            pltpu.SemaphoreType.DMA((9,)),
            pltpu.SemaphoreType.DMA((16,)),
        ],
        2 * LEN * WIDTH * 1024,
        anywhere=9,
        outs_anywhere=8,
    )
    part_keep, part_other, *got = lax.optimization_barrier((part_keep, part_other, *blocks, *got_down_a, *got_down_b))
    blocks, got_down_a, got_down_b = got[:8], got[8:12], got[12:]
    blocks = call(
        functools.partial(ffn_sum_body, 768),
        "feed_forward_sums_down",
        [at, *got_down_a, *got_down_b, down_0, *blocks],
        [message] * 8,
        [pltpu.VMEM((128, 512), bf16)] * 8 + [pltpu.SemaphoreType.DMA((8,))],
        0,
        anywhere=8,
        outs_anywhere=8,
        alias=8,
    )
    part_both = (part_keep.astype(f32) + part_other.astype(f32)).astype(bf16)
    attn_grad = lax.psum_scatter(part_both, Z, scatter_dimension=0, tiled=True).astype(f32)
    got_attn_a = [shift(blocks[1], Y, 1), shift(blocks[3], Y, 3)]
    got_attn_b = [x_out(blocks[4 + i], *FLIPS[i]) for i in (2, 3)]
    row_part = after(row_part, part_both)

    block_at = jnp.stack([((r // 4 - y) % 4) * 4 + ((r // 2 % 2) ^ lo) * 2 + ((r % 2) ^ hi) for r in range(16)])
    pick = (block_at[:, None] == jnp.arange(16)[None, :]).astype(f32)
    gain_parts = jnp.concatenate([gain_part.reshape(16, 128), grad_gain_two.reshape(16, 128)], 1)
    gain_parts = jnp.dot(pick, gain_parts, precision=lax.Precision.HIGHEST)
    peaks = jnp.where((jnp.arange(QUERY_HEADS) == mine)[:, None], peak, 0.0)
    small = jnp.concatenate([row_part.reshape(6, 128), gain_parts[:, :128], gain_parts[:, 128:], peaks], 0)
    is_peak = (jnp.arange(46) >= 38)[:, None]

    def join(values):
        total, most = values[0], values[0]
        for value in values[1:]:
            total, most = total + value, jnp.maximum(most, value)
        return jnp.where(is_peak[-total.shape[0] :], most, total)

    small = join([small, other_core(small)])
    small = join([small, z_other(small, 1)])

    rest = lax.optimization_barrier((blocks[2], blocks[4], blocks[5], small, *got_attn_a, *got_attn_b))
    (block_y, block_0, block_1, small), got_attn_a, got_attn_b = rest[:4], rest[4:6], rest[6:]
    got_attn_a = [blocks[0], shift(block_y, Y, 2), *got_attn_a]
    got_attn_b = [x_out(block_0, 0, 0), x_out(block_1, *FLIPS[1]), *got_attn_b]
    out_late = after(out_both, part_both)
    small = join([small, z_other(small, 2)])
    row_sum = small[:6].reshape(LEN, 1)
    small = small[6:]
    small = join([small, y_other(small, 1)])
    got_attn_a, got_attn_b, small, attn_grad = lax.optimization_barrier((got_attn_a, got_attn_b, small, attn_grad))
    ffn_own = lax.psum_scatter(out_late, Z, scatter_dimension=0, tiled=True).astype(f32)

    gain_pair = jnp.dot(pick, gain_rows[0].reshape(16, 128), precision=lax.Precision.HIGHEST)
    gain_cols = lax.dynamic_slice(gain_pair, (mine * 2, 0), (2, 128)).reshape(1, HEAD)
    grad_inputs = (
        db_cols.astype(f32) + r1 * attn_grad * gain_cols - x_own.astype(f32) * r1**2 * (row_sum / WIDTH)
    )
    home = [(h_cols.astype(f32) + ffn_own).astype(bf16), grad_inputs.astype(bf16)]
    home = swap(jnp.concatenate(home, 0))
    *sum_b, kv_give, kv_keep = call(
        join_body,
        "join_sums",
        [at, *got_attn_a, *got_attn_b, block_0],
        [((128, 512), bf16)] * 4 + [((512, HEAD), bf16), ((512, HEAD), f32)],
        [pltpu.VMEM((512, 512), bf16)] * 9 + [pltpu.SemaphoreType.DMA((9,))],
        0,
        anywhere=9,
    )
    kv_sum = (kv_keep + kv_partner(kv_give).astype(f32)).astype(bf16)
    sum_b = [sum_b[0]] + [shift(sum_b[i], Y, i) for i in (1, 2, 3)]
    first_y = sum_b[1]
    small = join([small, y_other(small, 2)])
    kv_sum, home, small, *sum_b = lax.optimization_barrier((kv_sum, home, small, *sum_b))
    high = lax.reduce_precision(small, 8, 7)
    rider = jnp.concatenate([high.astype(bf16), (small - high).astype(bf16)], 1)
    rider = jnp.pad(rider, ((0, 8), (0, 0)))
    rider = jnp.broadcast_to(rider[None], (4, 48, HEAD))
    last = jnp.concatenate([kv_sum.reshape(4, 128, HEAD), rider], 1).reshape(4 * 176, HEAD)
    sum_a = [x_out(last[i * 176 : (i + 1) * 176], *flip) for i, flip in enumerate(FLIPS)]
    grads = call(
        finish_body,
        "finish",
        [at, *got_attn_a, *got_attn_b, after(block_0, first_y)],
        [((128, FF), f32)] * 3,
        [pltpu.VMEM((384, 512), bf16)] * 9 + [pltpu.SemaphoreType.DMA((9,))],
        0,
        anywhere=9,
    )
    query, output, key, value, gain_one, gain_two, clipped_query, clipped_key = call(
        last_body,
        "last",
        [at, last[:176], *sum_a, *sum_b, w_query, w_key],
        [
            ((128, HEAD), f32),
            ((128, HEAD), f32),
            ((128, 128), f32),
            ((128, 128), f32),
            ((1, 128), f32),
            ((1, 128), f32),
            ((128, HEAD), bf16),
            ((128, 128), bf16),
        ],
        [pltpu.VMEM((48, 128), f32)],
        0,
    )
    return (
        home[:LEN],
        home[LEN:].astype(f32),
        gain_one.reshape(128),
        query,
        key,
        value,
        output,
        gain_two.reshape(128),
        grads[0],
        grads[1],
        grads[2],
        clipped_query,
        clipped_key,
    )


def solution(mesh):
    torus = Mesh(mesh.devices.reshape(4, 2, 2, 2, 4), (Y, XLO, CORE, XHI, Z))
    both, rows = P(TOK, MDL), P(TOK)
    return jax.shard_map(
        on_device,
        mesh=torus,
        in_specs=(both, P(TOK, None), rows, both, both, both, both, rows, both, both, both, both),
        out_specs=(both, both, rows, both, both, both, both, rows, both, both, both, both, both),
        check_vma=False,
    )
```

```python
import functools
import math

import jax
import jax.numpy as jnp
from jax import lax
from jax.experimental import pallas as pl
from jax.experimental.pallas import tpu as pltpu
from jax.sharding import Mesh
from jax.sharding import PartitionSpec as P

QUERY_HEADS = 8
HEAD = 256
WIDTH = 2048
LEN = 768
OWN = 96
FF = 1024
Y, XLO, CORE, XHI, Z = "tok_0", "tok_1", "tok_2", "mdl_0", "mdl_1"
TOK = (Y, XLO, CORE)
MDL = (XHI, Z)

norm_epsilon = 1e-06
rope_base = 1000042.0
logit_ceiling = 4.0
masked_value = -1e30
peak_floor_epsilon = 1e-06
SCALE = HEAD ** (-0.5)
nt = (((1,), (1,)), ((), ()))
tn = (((0,), (0,)), ((), ()))
f32 = jnp.float32
bf16 = jnp.bfloat16


def dot(a, b, dims=(((1,), (0,)), ((), ()))):
    return lax.dot_general(a, b, dims, preferred_element_type=f32)


def swap(a):
    got = lax.ppermute(a, (CORE, XHI), [(1, 2), (2, 1)])
    return jnp.where(lax.axis_index(CORE) == lax.axis_index(XHI), a, got)


def other_core(a):
    return lax.ppermute(a, CORE, [(0, 1), (1, 0)])


def shift(a, axis, by):
    return lax.ppermute(a, axis, [(i, (i + by) % 4) for i in range(4)])


def z_other(a, mask):
    return lax.ppermute(a, Z, [(i, i ^ mask) for i in range(4)])


def y_other(a, mask):
    return lax.ppermute(a, Y, [(i, i ^ mask) for i in range(4)])


def kv_partner(a):
    return lax.ppermute(a, Z, [(0, 1), (1, 0), (2, 3), (3, 2)])


def plane_pairs(flip_lo, flip_core):
    pairs = []
    for lo in range(2):
        for core in range(2):
            for hi in range(2):
                pairs.append((lo * 4 + core * 2 + hi, (lo ^ flip_lo) * 4 + hi * 2 + (core ^ flip_core)))
    return pairs


def x_pairs(flip_lo, flip_core, back):
    pairs = plane_pairs(flip_lo, flip_core)
    return [(there, here) if back else (here, there) for here, there in pairs if here != there]


def x_in(a, flip_lo, flip_core):
    return lax.ppermute(a, (XLO, CORE, XHI), x_pairs(flip_lo, flip_core, False))


def x_out(a, flip_lo, flip_core):
    return lax.ppermute(a, (XLO, CORE, XHI), x_pairs(flip_lo, flip_core, True))


def own_or(got, own):
    return jnp.where(lax.axis_index(CORE) == lax.axis_index(XHI), own, got)


FLIPS = ((0, 0), (0, 1), (1, 0), (1, 1))


def from_y(a):
    return [a, shift(a, Y, -1), shift(a, Y, 2), shift(a, Y, 1)]


def from_z(a):
    return [a, shift(a, Z, -1), shift(a, Z, 2), shift(a, Z, 1)]


def x_ring(a, mask):
    return lax.ppermute(a, (XLO, XHI), [(i, i ^ mask) for i in range(4)])


def total(pieces, cols=slice(None)):
    return sum(piece[:, cols].astype(f32) for piece in pieces)


def team_gather(own):
    return lax.all_gather(own, (CORE, Z), axis=0, tiled=True)


def team_scatter(other, keep):
    both = (keep.astype(f32) + other.astype(f32)).astype(bf16)
    return lax.psum_scatter(both, Z, scatter_dimension=0, tiled=True).astype(f32)


def after(value, *others):
    return lax.optimization_barrier((value, *others))[0]


def rope_tables(segment_row):
    earlier = jnp.sum((segment_row[None, :] < segment_row[:, None]).astype(jnp.int32), axis=1)
    places = jnp.arange(LEN, dtype=jnp.int32) - earlier
    half = HEAD // 2
    inverse = jnp.exp(jnp.arange(half, dtype=f32) * (-2.0 * math.log(rope_base) / HEAD))
    angles = places.astype(f32)[:, None] * inverse[None, :]
    return jnp.cos(angles), jnp.sin(angles)


def position(r, at):
    return (((r >> 2) - at[0]) & 3) * 4 + (((r >> 1) & 1) ^ at[1]) * 2 + ((r & 1) ^ at[2])


def lanes(index, size):
    return pl.ds(pl.multiple_of(index * size, size), size)


def owner(at, there, dz):
    return (at[3] ^ there) * 4 + ((at[4] + dz) & 3)


def kdot(a, b, dims=(((1,), (0,)), ((), ()))):
    return lax.dot_general(a, b, dims, preferred_element_type=f32)


def in_vmem(n):
    return [pl.BlockSpec(memory_space=pltpu.VMEM)] * n


def call(body, name, inputs, outs, scratch, flops, megabytes=56, anywhere=0, outs_anywhere=0, alias=0):
    moved = sum(v.size * v.dtype.itemsize for v in inputs[1:])
    moved += sum(math.prod(s) * jnp.dtype(d).itemsize for s, d in outs)
    specs = [pl.BlockSpec(memory_space=pltpu.SMEM)] + in_vmem(len(inputs) - 1 - anywhere)
    specs += [pl.BlockSpec(memory_space=pl.ANY)] * anywhere
    return list(pl.pallas_call(
        body,
        name=name,
        out_shape=[jax.ShapeDtypeStruct(s, d) for s, d in outs],
        in_specs=specs,
        out_specs=in_vmem(len(outs) - outs_anywhere) + [pl.BlockSpec(memory_space=pl.ANY)] * outs_anywhere,
        scratch_shapes=scratch,
        input_output_aliases={len(inputs) - alias + i: i for i in range(alias)},
        cost_estimate=pl.CostEstimate(flops=int(flops), bytes_accessed=int(moved), transcendentals=0),
        compiler_params=pltpu.CompilerParams(vmem_limit_bytes=megabytes * 2**20),
    )(*inputs))


def turn(values, cosine, sine):
    first, second = values[:, :128], values[:, 128:]
    return first * cosine - second * sine, second * cosine + first * sine


def attention_weights(a_refs, b_refs, w_qkv, w_o, sem):
    copies = []

    def move(source, to):
        copies.append(pltpu.make_async_copy(source, to, sem.at[len(copies)]))
        copies[-1].start()

    for i in range(4):
        for dy in range(4):
            rows = pl.ds((dy * 4 + i) * 128, 128)
            move(b_refs[i].at[pl.ds(dy * 144, 128), pl.ds(256, 256)], w_o.at[rows])
    for dy in range(4):
        for i in range(4):
            rows = pl.ds((dy * 4 + i) * 128, 128)
            move(b_refs[i].at[pl.ds(dy * 144, 128), pl.ds(0, 256)], w_qkv.at[rows, pl.ds(0, 256)])
            move(a_refs[dy].at[pl.ds(i * 128, 128)], w_qkv.at[rows, pl.ds(256, 512)])
    return copies


def along_y_body(at, *refs):
    riders, gain_one, gain_two = refs[:3]
    tokens, cotangent, w_query, w_output, w_up, w_down, out, mixed, sem = refs[3:]
    pairs = [
        (w_query, out.at[pl.ds(0, 128), pl.ds(0, 256)]),
        (w_output, out.at[pl.ds(0, 128), pl.ds(256, 256)]),
        (w_up.at[:, pl.ds(0, 512)], out.at[pl.ds(144, 128)]),
        (w_up.at[:, pl.ds(512, 512)], out.at[pl.ds(272, 128)]),
        (w_down.at[:, pl.ds(512, 512)], out.at[pl.ds(400, 128)]),
        (tokens, mixed.at[pl.ds(0, 768)]),
        (cotangent, mixed.at[pl.ds(784, 768)]),
    ]
    copies = [pltpu.make_async_copy(a, b, sem.at[i]) for i, (a, b) in enumerate(pairs)]
    for copy in copies:
        copy.start()
    row = lax.broadcasted_iota(jnp.int32, (16, 128), 0)
    gains = jnp.where(row == 0, gain_one[...], jnp.where(row == 1, gain_two[...], 0.0))
    out[128:144, :128] = gains.astype(bf16)
    out[128:144, 128:] = jnp.zeros((16, 384), bf16)
    mixed[768:784, :] = riders[...]
    for copy in copies:
        copy.wait()


def along_x_body(at, *refs):
    key, value, other, w_gate, w_down, out, sem = refs
    pairs = [
        (w_gate.at[:, pl.ds(0, 512)], out.at[pl.ds(128, 128)]),
        (w_gate.at[:, pl.ds(512, 512)], out.at[pl.ds(256, 128)]),
        (w_down.at[:, pl.ds(0, 512)], out.at[pl.ds(384, 128)]),
    ]
    copies = [pltpu.make_async_copy(a, b, sem.at[i]) for i, (a, b) in enumerate(pairs)]
    for copy in copies:
        copy.start()
    odd = at[4] & 1
    out[:128, lanes(odd, 128)] = key[...]
    out[:128, lanes(1 - odd, 128)] = other[:, :128]
    out[:128, lanes(2 + odd, 128)] = value[...]
    out[:128, lanes(3 - odd, 128)] = other[:, 128:]
    for copy in copies:
        copy.wait()


def pack_body(at, *refs):
    xs, ys, to_y, to_x, sem = refs[:4], refs[4:8], refs[8], refs[9], refs[10]
    pairs = [(ref.at[pl.ds(0, 128)], to_y.at[pl.ds(128 * i, 128)]) for i, ref in enumerate(xs)]
    pairs += [(ref.at[pl.ds(0, 144)], to_x.at[pl.ds(144 * i, 144)]) for i, ref in enumerate(ys)]
    copies = [pltpu.make_async_copy(a, b, sem.at[i]) for i, (a, b) in enumerate(pairs)]
    for copy in copies:
        copy.start()
    for copy in copies:
        copy.wait()


def riders_body(at, *refs):
    xs, ys = refs[:4], refs[4:8]
    a_wide, b_wide, a_down, b_down, sem = refs[8:]
    copies = []
    for ref, row, wide, down in [(xs, 128, a_wide, a_down), (ys, 144, b_wide, b_down)]:
        for i in range(4):
            for j in range(3):
                source = ref[i].at[pl.ds(row + j * 128, 128)]
                rows = pl.ds(i * 128, 128)
                to = down.at[rows] if j == 2 else wide.at[rows, pl.ds(j * 512, 512)]
                copies.append(pltpu.make_async_copy(source, to, sem.at[len(copies)]))
    for copy in copies:
        copy.start()
    for copy in copies:
        copy.wait()


def allowed_block(i, seg_col, seg_row):
    rows, cols = 256, (i + 1) * 256
    same = seg_col[i * 256 : (i + 1) * 256, :] == seg_row[:, :cols]
    row = i * 256 + lax.broadcasted_iota(jnp.int32, (rows, cols), 0)
    return same & (row >= lax.broadcasted_iota(jnp.int32, (rows, cols), 1))


def forward_body(at, *refs):
    x, cosine, sine, seg_row, seg_col = refs[:5]
    a_refs, b_refs = refs[5:9], refs[9:13]
    a1, r1, x_mine, qr, kr, v, o, lse, peak, gains, give, keep = refs[13:25]
    w_qkv, w_o, gain_rows, sem, gain_sem = refs[25:]
    gain_copies = []
    for dy in range(4):
        for i in range(4):
            source = b_refs[i].at[pl.ds(dy * 144 + 128, 16), pl.ds(0, 128)]
            to = gain_rows.at[:, pl.ds((dy * 4 + i) * 128, 128)]
            gain_copies.append(pltpu.make_async_copy(source, to, gain_sem.at[len(gain_copies)]))
            gain_copies[-1].start()
    copies = attention_weights(a_refs, b_refs, w_qkv, w_o, sem)
    for copy in gain_copies:
        copy.wait()
    gains[...] = gain_rows[...].astype(f32)[:8]
    own = at[3] * 4 + at[4]
    for r in range(16):
        rows = pl.ds(pl.multiple_of((r // 2) * LEN + own * OWN, OWN), OWN)
        x_mine[:, lanes(position(r, at), 128)] = x[rows, (r % 2) * 128 : (r % 2 + 1) * 128]

    def norm(step, carry):
        rows = pl.ds(pl.multiple_of(step * 128, 128), 128)
        total = jnp.zeros((128, 1), f32)
        for m in range(8):
            value = x[pl.ds(pl.multiple_of(m * LEN + step * 128, 128), 128), :].astype(f32)
            total = total + jnp.sum(value * value, axis=1, keepdims=True)
        factor = lax.rsqrt(total / WIDTH + norm_epsilon)
        r1[rows, :] = factor
        for r in range(16):
            at_lanes = lanes(position(r, at), 128)
            from_rows = pl.ds(pl.multiple_of((r // 2) * LEN + step * 128, 128), 128)
            value = x[from_rows, (r % 2) * 128 : (r % 2 + 1) * 128].astype(f32)
            a1[rows, at_lanes] = (value * factor * gains[0:1, at_lanes]).astype(bf16)
        return carry

    lax.fori_loop(0, 6, norm, 0)
    for copy in copies:
        copy.wait()
    for i in range(3):
        rows = slice(i * 256, (i + 1) * 256)
        qk = kdot(a1[rows, :], w_qkv[:, :512])
        cos_i, sin_i = cosine[rows, :], sine[rows, :]
        for ref, at_col in ((qr, 0), (kr, 256)):
            one, two = turn(qk[:, at_col : at_col + 256], cos_i, sin_i)
            ref[rows, :128] = one.astype(bf16)
            ref[rows, 128:] = two.astype(bf16)
        v[rows, :] = kdot(a1[rows, :], w_qkv[:, 512:]).astype(bf16)
    largest = jnp.zeros((1, 1), f32)
    for i in range(3):
        rows, cols = slice(i * 256, (i + 1) * 256), (i + 1) * 256
        allowed = allowed_block(i, seg_col, seg_row)
        scores = kdot(qr[rows, :], kr[:cols, :], nt) * SCALE
        masked = jnp.where(allowed, scores, masked_value)
        size = jnp.where(allowed, jnp.abs(scores), 0.0)
        largest = jnp.maximum(largest, jnp.max(jnp.max(size, axis=1, keepdims=True), axis=0, keepdims=True))
        top = jnp.max(masked, axis=1, keepdims=True)
        log_total = top + jnp.log(jnp.sum(jnp.exp(masked - top), axis=1, keepdims=True))
        lse[rows, :] = log_total
        probs = jnp.exp(masked - log_total).astype(bf16)
        o[rows, :] = kdot(probs, v[:cols, :]).astype(bf16)
    peak[...] = jnp.broadcast_to(largest, (8, 128))
    for ref, c in ((give, 1 - at[3]), (keep, at[3])):
        rows = pl.ds(pl.multiple_of(c * 384, 384), 384)
        for half in range(2):
            cols = slice(half * 1024, (half + 1) * 1024)
            ref[:, cols] = kdot(o[rows, :], w_o[cols, :], nt).astype(bf16)


def reorder_body(at, whole, out):
    for r in range(16):
        rows = slice((r // 2) * LEN, (r // 2 + 1) * LEN)
        out[:, lanes(position(r, at), 128)] = whole[rows, (r % 2) * 128 : (r % 2 + 1) * 128]


def start_either(at, own, got, to, sem):
    mine = at[2] == at[3]

    @pl.when(mine)
    def _():
        pltpu.make_async_copy(own, to, sem).start()

    @pl.when(jnp.logical_not(mine))
    def _():
        pltpu.make_async_copy(got, to, sem).start()

    return pltpu.make_async_copy(got, to, sem)


def rows_a(refs, to_ref, cols, sem, copies):
    row = 0
    for ref in refs:
        to = to_ref.at[pl.ds(row, ref.shape[0]), cols]
        row += ref.shape[0]
        copies.append(pltpu.make_async_copy(ref, to, sem.at[len(copies)]))
        copies[-1].start()


def rows_b(at, own, refs, to_ref, cols, sem, copies):
    for i, ref in enumerate(refs):
        for j in range(4):
            to = to_ref.at[pl.ds((j * 4 + i) * 128, 128), cols]
            rows = pl.ds(j * 128, 128)
            if i == 0:
                copies.append(start_either(at, own.at[rows], ref.at[rows], to, sem.at[len(copies)]))
            else:
                copies.append(pltpu.make_async_copy(ref.at[rows], to, sem.at[len(copies)]))
                copies[-1].start()


def ffn_body(at, *refs):
    gains, h_in, dy_in = refs[:3]
    wide_a, (down_a, wide_b, down_b) = refs[3:8], [refs[8 + 4 * i : 12 + 4 * i] for i in range(3)]
    own_wide, own_down = refs[20:22]
    h_cols, a2_out, hid_out, dgate_out, dup_out, give_out, keep_out = refs[22:29]
    up_outs, gate_outs = refs[29:31], refs[31:33]
    h, dy, a2, hid, dgate, dup, give, keep, up_0, up_1, gate_0, gate_1 = refs[33:45]
    w_gate, w_up, w_down, sem, out_sem = refs[45:]
    h_copy = pltpu.make_async_copy(h_in, h, out_sem.at[14])
    h_copy.start()
    copies = []
    rows_a(wide_a, w_gate, pl.ds(0, FF), sem, copies)
    rows_b(at, own_wide, wide_b, w_up, pl.ds(0, FF), sem, copies)
    rows_a(down_a, w_down, pl.ds(0, 512), sem, copies)
    rows_b(at, own_down, down_b, w_down, pl.ds(512, 512), sem, copies)
    copies.append(pltpu.make_async_copy(dy_in, dy, out_sem.at[15]))
    copies[-1].start()
    sent = []

    def send(source, to):
        sent.append(pltpu.make_async_copy(source, to, out_sem.at[len(sent)]))
        sent[-1].start()

    h_copy.wait()
    own = at[3] * 4 + at[4]
    for j in range(2):
        h_cols[:, j * 128 : (j + 1) * 128] = h[:, lanes(position(2 * own + j, at), 128)]
    for i in range(6):
        rows = slice(i * 128, (i + 1) * 128)
        value = h[rows, :].astype(f32)
        factor = lax.rsqrt(jnp.mean(value * value, axis=1, keepdims=True) + norm_epsilon)
        a2[rows, :] = (value * factor * gains[1:2, :]).astype(bf16)
    send(a2, a2_out)
    for copy in copies:
        copy.wait()
    for j in range(4):
        cols = slice(j * 256, (j + 1) * 256)
        gate = kdot(a2[...], w_gate[:, cols])
        up = kdot(a2[...], w_up[:, cols])
        grad = kdot(dy[...], w_down[:, cols])
        sig = 1.0 / (1.0 + jnp.exp(-gate))
        act = gate * sig
        hid[:, cols] = (act * up).astype(bf16)
        dgate[:, cols] = (grad * up * sig * (1.0 + gate * (1.0 - sig))).astype(bf16)
        dup[:, cols] = (grad * act).astype(bf16)
    for source, to in ((hid, hid_out), (dgate, dgate_out), (dup, dup_out)):
        send(source, to)
    for ref, to, c in ((give, give_out, 1 - at[3]), (keep, keep_out, at[3])):
        rows = pl.ds(pl.multiple_of(c * 384, 384), 384)
        for j in range(4):
            cols = slice(j * 512, (j + 1) * 512)
            ref[:, cols] = (
                kdot(dgate[rows, :], w_gate[cols, :], nt) + kdot(dup[rows, :], w_up[cols, :], nt)
            ).astype(bf16)
        send(ref, to)
    for i, ref, to in ((1, gate_0, gate_outs[0]), (3, gate_1, gate_outs[1])):
        for j in range(2):
            n = slice(j * 512, (j + 1) * 512)
            ref[:, n] = kdot(a2[:, i * 512 : (i + 1) * 512], dgate[:, n], tn).astype(bf16)
        send(ref, to)
    for i in range(4):
        cols = slice((i * 4 + 2) * 128, (i * 4 + 4) * 128)
        for j in range(2):
            n = slice(j * 512, (j + 1) * 512)
            value = kdot(a2[:, cols], dup[:, n], tn).astype(bf16)
            up_0[i * 128 : (i + 1) * 128, n] = value[:128]
            up_1[i * 128 : (i + 1) * 128, n] = value[128:]
    send(up_0, up_outs[0])
    send(up_1, up_outs[1])
    for copy in sent:
        copy.wait()


def ffn_out_body(at, hid, *refs):
    down_a, down_b, own_down = refs[:4], refs[4:8], refs[8]
    give, keep, w_down, sem = refs[9:]
    copies = []
    rows_a(down_a, w_down, pl.ds(0, 512), sem, copies)
    rows_b(at, own_down, down_b, w_down, pl.ds(512, 512), sem, copies)
    for copy in copies:
        copy.wait()
    for ref, c in ((give, 1 - at[3]), (keep, at[3])):
        for dz in range(4):
            m = c * 4 + dz
            pair = pl.ds(pl.multiple_of((position(2 * m, at) >> 1) * 256, 256), 256)
            value = kdot(hid[...], w_down[pair, :], nt)
            rows = slice(dz * LEN, (dz + 1) * LEN)
            for j in range(2):
                ref[rows, lanes(at[2] ^ j, 128)] = value[:, j * 128 : (j + 1) * 128].astype(bf16)


def weight_rest_body(at, a2, dy, dgate, dup, hid, *outs):
    a_wide, b_wide, a_down, b_down = outs[:2], outs[2:4], outs[4:8], outs[8:]
    for i in range(4):
        cols, rows = slice(i * 512, (i + 1) * 512), slice(i * 128, (i + 1) * 128)
        for j in range(2):
            n = slice(j * 512, (j + 1) * 512)
            value = kdot(a2[:, i * 512 : i * 512 + 256], dup[:, n], tn).astype(bf16)
            for k in range(2):
                b_wide[k][rows, n] = value[k * 128 : (k + 1) * 128]
            if i % 2 == 0:
                a_wide[i // 2][:, n] = kdot(a2[:, cols], dgate[:, n], tn).astype(bf16)
        a_down[i][...] = kdot(dy[:, cols], hid[:, :512], tn).astype(bf16)
        value = kdot(dy[:, cols], hid[:, 512:], tn).astype(bf16)
        for k in range(4):
            b_down[k][rows, :] = value[k * 128 : (k + 1) * 128]


def backward_body(at, *refs):
    db, cosine, sine, seg_row, seg_col, qr, kr, v, lse, a1, gains = refs[:11]
    a_refs, b_refs = refs[11:15], refs[15:19]
    db_cols, dqkv, row_part, gain_part, give, keep = refs[19:25]
    w_qkv, w_o, d_o, dk_sum, dv_sum, sem = refs[25:]
    copies = attention_weights(a_refs, b_refs, w_qkv, w_o, sem)
    own = at[3] * 4 + at[4]
    for j in range(2):
        db_cols[:, j * 128 : (j + 1) * 128] = db[:, lanes(position(2 * own + j, at), 128)]
    for copy in copies:
        copy.wait()
    for i in range(3):
        rows = slice(i * 256, (i + 1) * 256)
        d_o[rows, :] = kdot(db[rows, :], w_o[...]).astype(bf16)
    for i in (2, 1, 0):
        rows, cols = slice(i * 256, (i + 1) * 256), (i + 1) * 256
        allowed = allowed_block(i, seg_col, seg_row)
        scores = kdot(qr[rows, :], kr[:cols, :], nt) * SCALE
        probs = jnp.exp(jnp.where(allowed, scores, masked_value) - lse[rows, :])
        low = probs.astype(bf16)
        dp = kdot(d_o[rows, :], v[:cols, :], nt)
        delta = jnp.sum(dp * probs, axis=1, keepdims=True)
        ds = (probs * (dp - delta)).astype(bf16)
        dq = kdot(ds, kr[:cols, :]) * SCALE
        row_part[rows, :] = jnp.sum(dq * qr[rows, :].astype(f32), axis=1, keepdims=True)
        one, two = turn(dq, cosine[rows, :], -sine[rows, :])
        dqkv[rows, :128] = one.astype(bf16)
        dqkv[rows, 128:256] = two.astype(bf16)
        dk_new = kdot(ds, qr[rows, :], tn)
        dv_new = kdot(low, d_o[rows, :], tn)
        if i == 2:
            dk_sum[...] = dk_new
            dv_sum[...] = dv_new
        else:
            dk_sum[:cols, :] = dk_sum[:cols, :] + dk_new
            dv_sum[:cols, :] = dv_sum[:cols, :] + dv_new
    for i in range(3):
        rows = slice(i * 256, (i + 1) * 256)
        dk = dk_sum[rows, :] * SCALE
        dv_i = dv_sum[rows, :]
        row_part[rows, :] = (
            row_part[rows, :]
            + jnp.sum(dk * kr[rows, :].astype(f32), axis=1, keepdims=True)
            + jnp.sum(dv_i * v[rows, :].astype(f32), axis=1, keepdims=True)
        )
        one, two = turn(dk, cosine[rows, :], -sine[rows, :])
        dqkv[rows, 256:384] = one.astype(bf16)
        dqkv[rows, 384:512] = two.astype(bf16)
        dqkv[rows, 512:] = dv_i.astype(bf16)
    for m, ref in [(j, give) for j in range(4)] + [(j, keep) for j in range(4)]:
        half = 1 - at[3] if ref is give else at[3]
        pair = lanes(position(2 * (half * 4 + m), at) >> 1, 256)
        value = kdot(dqkv[...], w_qkv[pair, :], nt)
        gain_part[:, pair] = jnp.sum(value * a1[:, pair].astype(f32), axis=0, keepdims=True) / gains[0:1, pair]
        rows = slice(m * LEN, (m + 1) * LEN)
        for j in range(2):
            ref[rows, lanes(at[2] ^ j, 128)] = value[:, j * 128 : (j + 1) * 128].astype(bf16)


def wide_sums(at, a, b, own, values):
    for i in range(4):
        rows = slice(i * 128, (i + 1) * 128)
        head = jnp.where(at[2] == at[3], own[rows, :], b[0][rows, :])
        of_b = head.astype(f32) + b[1][rows, :].astype(f32) + b[2][rows, :].astype(f32) + b[3][rows, :].astype(f32)
        of_a = a[0][rows, :].astype(f32) + a[1][rows, :].astype(f32) + a[2][rows, :].astype(f32) + a[3][rows, :].astype(f32)
        for value, total_ in ((values[i], of_b), (values[4 + i], of_a)):
            for j in range(2):
                value[j * 128 : (j + 1) * 128, :] = total_[:, j * 512 : (j + 1) * 512].astype(bf16)


def attention_weight_body(at, a1, dqkv, db, o, *refs):
    pieces, outs, values, sums = refs[:9], refs[9:17], refs[17:25], refs[25:33]
    held, sem, out_sem = refs[33:42], refs[42], refs[43]
    arriving = [pltpu.make_async_copy(x, v, sem.at[i]) for i, (x, v) in enumerate(zip(pieces, held))]
    for copy in arriving:
        copy.start()
    sent = []

    def send(source, to):
        sent.append(pltpu.make_async_copy(source, to, out_sem.at[len(sent)]))
        sent[-1].start()

    for i in range(4):
        cols, rows = slice(i * 512, (i + 1) * 512), slice(i * 128, (i + 1) * 128)
        values[i][...] = kdot(a1[:, cols], dqkv[:, 256:], tn).astype(bf16)
        send(values[i], outs[i].at[pl.ds(0, 512)])
        for n, left, right in ((slice(0, 256), a1, dqkv.at[:, :256]), (slice(256, 512), db, o)):
            value = kdot(left[:, cols], right[...], tn).astype(bf16)
            for k in range(4):
                values[4 + k][rows, n] = value[k * 128 : (k + 1) * 128]
    for i in range(4, 8):
        send(values[i], outs[i].at[pl.ds(0, 512)])
    for copy in arriving:
        copy.wait()
    wide_sums(at, held[:4], held[4:8], held[8], sums)
    for i in range(8):
        send(sums[i], outs[i].at[pl.ds(512, 256)])
    for copy in sent:
        copy.wait()


def ffn_sum_body(row, at, *refs):
    a, b, own, outs, values, sem = refs[:4], refs[4:8], refs[8], refs[17:25], refs[25:33], refs[33]
    mine = at[2] == at[3]
    copies = []
    for i in range(4):
        rows = slice(i * 128, (i + 1) * 128)
        head = jnp.where(mine, own[rows, :], b[0][rows, :])
        for value, terms in ((values[i], [b[k][rows, :] for k in (1, 2, 3)]), (values[4 + i], [a[k][rows, :] for k in (1, 2, 3)])):
            first = head if value is values[i] else a[0][rows, :]
            total = first.astype(f32) + terms[0].astype(f32) + terms[1].astype(f32) + terms[2].astype(f32)
            for j in range(total.shape[1] // 512):
                value[j * 128 : (j + 1) * 128, :] = total[:, j * 512 : (j + 1) * 512].astype(bf16)
    for i in range(8):
        to = outs[i].at[pl.ds(row, values[i].shape[0])]
        copies.append(pltpu.make_async_copy(values[i], to, sem.at[i]))
        copies[-1].start()
    for copy in copies:
        copy.wait()


def join_body(at, *refs):
    a, b, own, outs = refs[:4], refs[4:8], refs[8], refs[9:13]
    kv_give, kv_keep, va, vb, v_own, sem = refs[13], refs[14], refs[15:19], refs[19:23], refs[23], refs[24]
    pairs = list(zip([*a, *b, own], [*va, *vb, v_own]))
    copies = [pltpu.make_async_copy(x.at[pl.ds(0, 512)], v, sem.at[i]) for i, (x, v) in enumerate(pairs)]
    for copy in copies:
        copy.start()
    for copy in copies:
        copy.wait()
    odd = (at[4] & 1) == 1
    for i in range(4):
        rows = slice(i * 128, (i + 1) * 128)
        head = jnp.where(at[2] == at[3], v_own[rows, :], vb[0][rows, :])
        value = head.astype(f32) + vb[1][rows, :].astype(f32) + vb[2][rows, :].astype(f32) + vb[3][rows, :].astype(f32)
        outs[i][...] = value.astype(bf16)
        value = va[0][rows, :].astype(f32) + va[1][rows, :].astype(f32) + va[2][rows, :].astype(f32) + va[3][rows, :].astype(f32)
        for half in range(2):
            one, two = value[:, half * 256 : half * 256 + 128], value[:, half * 256 + 128 : (half + 1) * 256]
            n = slice(half * 128, (half + 1) * 128)
            kv_keep[rows, n] = jnp.where(odd, two, one)
            kv_give[rows, n] = jnp.where(odd, one, two).astype(bf16)


def finish_body(at, *refs):
    a, b, own = refs[:4], refs[4:8], refs[8]
    gate, up, down, va, vb, v_own, sem = refs[9], refs[10], refs[11], refs[12:16], refs[16:20], refs[20], refs[21]
    pairs = list(zip([*a, *b, own], [*va, *vb, v_own]))
    copies = [pltpu.make_async_copy(x.at[pl.ds(512, 384)], v, sem.at[i]) for i, (x, v) in enumerate(pairs)]
    for copy in copies:
        copy.start()
    for copy in copies:
        copy.wait()
    mine = at[2] == at[3]
    for j in range(3):
        rows = slice(j * 128, (j + 1) * 128)
        head = jnp.where(mine, v_own[rows, :], vb[0][rows, :])
        of_a = head.astype(f32) + vb[1][rows, :].astype(f32) + vb[2][rows, :].astype(f32) + vb[3][rows, :].astype(f32)
        of_b = va[0][rows, :].astype(f32) + va[1][rows, :].astype(f32) + va[2][rows, :].astype(f32) + va[3][rows, :].astype(f32)
        if j < 2:
            gate[:, j * 512 : (j + 1) * 512] = of_a
            up[:, j * 512 : (j + 1) * 512] = of_b
        else:
            down[:, :512] = of_a
            down[:, 512:] = of_b


def last_body(at, *refs):
    own, a, b, w_query, w_key = refs[0], refs[1:5], refs[5:9], refs[9], refs[10]
    query, output, key, value, gain_one, gain_two, clipped_query, clipped_key, small = refs[11:]
    a = [jnp.where(at[2] == at[3], own[...], a[0][...]), a[1][...], a[2][...], a[3][...]]
    kv = a[0][:128].astype(f32) + a[1][:128].astype(f32) + a[2][:128].astype(f32) + a[3][:128].astype(f32)
    key[...] = kv[:, :128]
    value[...] = kv[:, 128:]
    parts = [piece[128:, :128].astype(f32) + piece[128:, 128:].astype(f32) for piece in a]
    added = parts[0] + parts[1] + parts[2] + parts[3]
    most = jnp.maximum(jnp.maximum(parts[0], parts[1]), jnp.maximum(parts[2], parts[3]))
    small[...] = jnp.where(lax.broadcasted_iota(jnp.int32, (48, 128), 0) >= 32, most, added)
    tok, head = at[0] * 4 + at[1] * 2 + at[3], at[2] * 4 + at[4]
    gain_one[...] = small[pl.ds(tok, 1), :]
    gain_two[...] = small[pl.ds(16 + tok, 1), :]
    peak = small[pl.ds(32 + head, 1), :]
    pair = jnp.maximum(peak, small[pl.ds(32 + (head ^ 1), 1), :])
    scale = jnp.sqrt(logit_ceiling / (peak + peak_floor_epsilon))
    for j in range(2):
        cols = slice(j * 128, (j + 1) * 128)
        clipped_query[:, cols] = (w_query[:, cols].astype(f32) * scale).astype(bf16)
    scale = jnp.sqrt(logit_ceiling / (pair + peak_floor_epsilon))
    clipped_key[...] = (w_key[...].astype(f32) * scale).astype(bf16)
    total_b = b[0][...].astype(f32) + b[1][...].astype(f32) + b[2][...].astype(f32) + b[3][...].astype(f32)
    query[...] = total_b[:, :256]
    output[...] = total_b[:, 256:]


def on_device(
    tokens,
    segments,
    gain_attn,
    w_query,
    w_key,
    w_value,
    w_output,
    gain_ffn,
    w_gate,
    w_up,
    w_down,
    cotangent,
):
    y, lo, core = lax.axis_index(Y), lax.axis_index(XLO), lax.axis_index(CORE)
    hi, z = lax.axis_index(XHI), lax.axis_index(Z)
    at = jnp.stack([y, lo, hi, core, z]).astype(jnp.int32)
    mine = core * 4 + z

    riders = jnp.zeros((16, HEAD), bf16).at[:3].set(segments.reshape(3, HEAD).astype(bf16))
    hf = FF // 2
    odd = z % 2 == 1
    half = HEAD // 2
    kv_other = kv_partner(jnp.concatenate([w_key, w_value], 1))
    y_rows, mixed = call(
        along_y_body,
        "lay_out_y",
        [
            at,
            riders,
            gain_attn.astype(f32).reshape(1, 128),
            gain_ffn.astype(f32).reshape(1, 128),
            tokens,
            cotangent,
            w_query,
            w_output,
            w_up,
            w_down,
        ],
        [((528, 2 * HEAD), bf16), ((1552, HEAD), bf16)],
        [pltpu.SemaphoreType.DMA((7,))],
        0,
        anywhere=6,
    )
    (x_rows,) = call(
        along_x_body,
        "lay_out_x",
        [at, w_key, w_value, kv_other, w_gate, w_down],
        [((512, 2 * HEAD), bf16)],
        [pltpu.SemaphoreType.DMA((3,))],
        0,
        anywhere=2,
    )
    got = swap(mixed)
    along_y = [shift(y_rows, Y, -1), shift(y_rows, Y, 1)]
    along_x = [x_in(x_rows, *flip) for flip in FLIPS[2:]]
    got, late_y, late_x, *rest = lax.optimization_barrier((got, y_rows, x_rows, *along_y, *along_x))
    along_y = [y_rows, rest[0], shift(late_y, Y, 2), rest[1]]
    along_x = [own_or(x_in(late_x, 0, 0), x_rows), x_in(late_x, *FLIPS[1]), *rest[2:]]
    rest = lax.optimization_barrier((*along_x, *along_y))
    to_y, to_x = call(
        pack_body,
        "pack",
        [at, *rest],
        [((512, 2 * HEAD), bf16), ((576, 2 * HEAD), bf16)],
        [pltpu.SemaphoreType.DMA((8,))],
        0,
        anywhere=8,
    )
    a_wide, b_wide, a_down, b_down = call(
        riders_body,
        "riders",
        [at, *rest],
        [((512, FF), bf16)] * 2 + [((512, hf), bf16)] * 2,
        [pltpu.SemaphoreType.DMA((24,))],
        0,
        anywhere=8,
    )
    x_own = got[:LEN]
    x_all = team_gather(x_own)
    upstream = team_gather(after(got[784:1552], to_x))
    segment_row = got[LEN : LEN + 3].astype(f32).reshape(1, LEN)
    segment_col = segment_row.reshape(LEN, 1)
    cosine, sine = rope_tables(segment_row[0])
    first = [shift(to_y, Y, -1), shift(to_y, Y, 1)]
    second = [x_in(to_x, *flip) for flip in FLIPS[2:]]
    late_y, late_x, *rest = lax.optimization_barrier((to_y, to_x, *first, *second))
    first, second = rest[:2], rest[2:]
    first = [to_y, first[0], shift(late_y, Y, 2), first[1]]
    second = [own_or(x_in(late_x, 0, 0), to_x), x_in(late_x, *FLIPS[1])] + second
    x_all, cosine, sine, segment_row, segment_col, *rest = lax.optimization_barrier(
        (x_all, cosine, sine, segment_row, segment_col, *first, *second, a_wide, b_wide, a_down, b_down)
    )
    first, second, (a_wide, b_wide, a_down, b_down) = rest[:4], rest[4:8], rest[8:]
    wide_a = [shift(a_wide, Y, -1), shift(a_wide, Y, 1)]
    wide_b = [x_in(b_wide, *flip) for flip in FLIPS[2:]]

    part = ((LEN // 2, WIDTH), bf16)
    act, low, col = ((LEN, WIDTH), bf16), ((LEN, HEAD), bf16), ((LEN, 1), f32)
    a1, r1, x_mine, qr, kr, v, o, lse, peak, gain_rows, give, keep = call(
        forward_body,
        "attention_forward",
        [at, x_all, cosine, sine, segment_row, segment_col, *first, *second],
        [act, col, ((OWN, WIDTH), bf16), low, low, low, low, col, ((8, 128), f32), ((8, WIDTH), f32), part, part],
        [
            pltpu.VMEM((WIDTH, 3 * HEAD), bf16),
            pltpu.VMEM((WIDTH, HEAD), bf16),
            pltpu.VMEM((16, WIDTH), bf16),
            pltpu.SemaphoreType.DMA((48,)),
            pltpu.SemaphoreType.DMA((16,)),
        ],
        2 * LEN * WIDTH * 1024,
        anywhere=8,
    )
    give, keep, upstream, *done = lax.optimization_barrier(
        (give, keep, upstream, *wide_a, *wide_b, a_wide, b_wide, a_down, b_down)
    )
    wide_a, wide_b, (a_wide, b_wide, a_down, b_down) = done[:2], done[2:4], done[4:]
    attn_own = team_scatter(other_core(give), keep)
    halves = [shift(wide_a[0][:256], Y, -1), shift(wide_a[1][256:], Y, 1)]
    wide_a = [a_wide, wide_a[0], *halves, wide_a[1]]
    wide_b = [x_in(b_wide, *flip) for flip in FLIPS[:2]] + wide_b
    down_a = [shift(a_down, Y, -1), shift(a_down, Y, 1)]
    (dy,) = call(reorder_body, "order_upstream", [at, upstream], [((LEN, WIDTH), bf16)], [], 0)


    attn_own, dy, *done = lax.optimization_barrier((attn_own, dy, *wide_a, *wide_b, *down_a, b_wide, a_down, b_down))
    wide_a, wide_b, down_a, (b_wide, a_down, b_down) = done[:5], done[5:9], done[9:11], done[11:]
    down_b = [x_in(b_down, *flip) for flip in FLIPS]
    down_a = [a_down, down_a[0], shift(a_down, Y, 2), down_a[1]]
    hidden_own = x_mine.astype(f32) + attn_own
    hidden = team_gather(hidden_own.astype(bf16))
    wide = ((LEN, FF), bf16)
    block = ((512, FF), bf16)
    h_cols, a2, hid, dgate, dup, give, keep, up_2, up_3, gate_1, gate_3 = call(
        ffn_body,
        "feed_forward",
        [at, gain_rows, hidden, dy, *wide_a, *down_a, *wide_b, *down_b, b_wide, b_down],
        [low, act, wide, wide, wide, part, part, block, block, block, block],
        [
            *[pltpu.VMEM(*v) for v in (act, act, act, wide, wide, wide, part, part, block, block, block, block)],
            pltpu.VMEM((WIDTH, FF), bf16),
            pltpu.VMEM((WIDTH, FF), bf16),
            pltpu.VMEM((WIDTH, FF), bf16),
            pltpu.SemaphoreType.DMA((44,)),
            pltpu.SemaphoreType.DMA((16,)),
        ],
        14 * LEN * WIDTH * FF,
        anywhere=21,
        outs_anywhere=10,
    )
    other = other_core(give)
    wide_out, stack = ((512, FF), bf16), ((4 * LEN, HEAD), bf16)
    work = 2 * LEN * WIDTH * FF
    both = (keep.astype(f32) + other.astype(f32)).astype(bf16)
    normed_grad = lax.psum_scatter(both, Z, scatter_dimension=0, tiled=True).astype(f32)
    dgate, dup, hid = lax.optimization_barrier((dgate, dup, hid, both))[:3]
    got_up = [x_out(up_2, *FLIPS[2]), x_out(up_3, *FLIPS[3])]
    got_gate = [shift(gate_1, Y, 1), shift(gate_3, Y, 3)]
    rest = call(
        weight_rest_body,
        "weight_rest",
        [at, a2, dy, dgate, dup, hid],
        [wide_out] * 4 + [((512, hf), bf16)] * 8,
        [],
        work * 2,
    )
    out_give, out_keep = call(
        ffn_out_body,
        "feed_forward_out",
        [at, after(hid, rest[0]), *down_a, *down_b, b_down],
        [stack, stack],
        [pltpu.VMEM((WIDTH, FF), bf16), pltpu.SemaphoreType.DMA((20,))],
        work,
        anywhere=9,
    )
    normed_grad, out_give, out_keep, *got = lax.optimization_barrier(
        (normed_grad, out_give, out_keep, *got_up, *got_gate, *rest)
    )
    got_up, got_gate, gate_b, up_b = [got[2 * i : 2 * i + 2] for i in range(4)]
    down_g = got[8:]

    gain_two = gain_rows[1:2]
    factor_own = lax.rsqrt(jnp.mean(hidden_own * hidden_own, axis=1, keepdims=True) + norm_epsilon)
    grad_gain_two = jnp.sum(normed_grad * hidden_own * factor_own, axis=0)
    scaled = normed_grad * gain_two
    grad_res = (
        lax.dynamic_slice_in_dim(dy, mine * OWN, OWN, 0).astype(f32)
        + factor_own * scaled
        - hidden_own * factor_own**3 * jnp.mean(scaled * hidden_own, axis=1, keepdims=True)
    )
    grad_low = grad_res.astype(bf16)
    db = team_gather(grad_low)
    got_gate = [gate_b[0], shift(gate_b[1], Y, 2)] + got_gate
    got_up = [x_out(up_b[0], 0, 0), x_out(up_b[1], *FLIPS[1])] + got_up
    out_both = (out_keep.astype(f32) + other_core(out_give).astype(f32)).astype(bf16)
    db, out_both, *got = lax.optimization_barrier((db, out_both, *got_gate, *got_up, *down_g))
    got_gate, got_up, down_g = got[:4], got[4:8], got[8:]
    got_down_a = [shift(down_g[1], Y, 1), shift(down_g[3], Y, 3)]
    got_down_b = [x_out(block, *flip) for block, flip in zip(down_g[6:], FLIPS[2:])]

    db_cols, dqkv, row_part, gain_part, part_give, part_keep = call(
        backward_body,
        "attention_backward",
        [at, db, cosine, sine, segment_row, segment_col, qr, kr, v, lse, a1, gain_rows, *first, *second],
        [low, ((LEN, 3 * HEAD), bf16), col, ((1, WIDTH), f32), stack, stack],
        [
            pltpu.VMEM((WIDTH, 3 * HEAD), bf16),
            pltpu.VMEM((WIDTH, HEAD), bf16),
            pltpu.VMEM((LEN, HEAD), bf16),
            pltpu.VMEM((LEN, HEAD), f32),
            pltpu.VMEM((LEN, HEAD), f32),
            pltpu.SemaphoreType.DMA((48,)),
        ],
        2 * LEN * WIDTH * 1024,
        anywhere=8,
    )
    part_give, part_keep, dqkv, down_y, down_0, down_1, *got = lax.optimization_barrier(
        (part_give, part_keep, dqkv, down_g[2], down_g[4], down_g[5], *got_down_a, *got_down_b)
    )
    got_down_a = [down_g[0], shift(down_y, Y, 2), *got[:2]]
    got_down_b = [x_out(down_0, 0, 0), x_out(down_1, *FLIPS[1]), *got[2:]]
    part_other = other_core(part_give)
    message = ((896, 512), bf16)
    blocks = call(
        attention_weight_body,
        "attention_weights",
        [at, a1, dqkv, db, o, *got_gate, *got_up, up_b[0]],
        [message] * 8,
        [
            *[pltpu.VMEM((512, 512), bf16)] * 8,
            *[pltpu.VMEM((256, 512), bf16)] * 8,
            *[pltpu.VMEM((512, FF), bf16)] * 9,
            pltpu.SemaphoreType.DMA((9,)),
            pltpu.SemaphoreType.DMA((16,)),
        ],
        2 * LEN * WIDTH * 1024,
        anywhere=9,
        outs_anywhere=8,
    )
    part_keep, part_other, *got = lax.optimization_barrier((part_keep, part_other, *blocks, *got_down_a, *got_down_b))
    blocks, got_down_a, got_down_b = got[:8], got[8:12], got[12:]
    blocks = call(
        functools.partial(ffn_sum_body, 768),
        "feed_forward_sums_down",
        [at, *got_down_a, *got_down_b, down_0, *blocks],
        [message] * 8,
        [pltpu.VMEM((128, 512), bf16)] * 8 + [pltpu.SemaphoreType.DMA((8,))],
        0,
        anywhere=8,
        outs_anywhere=8,
        alias=8,
    )
    part_both = (part_keep.astype(f32) + part_other.astype(f32)).astype(bf16)
    attn_grad = lax.psum_scatter(part_both, Z, scatter_dimension=0, tiled=True).astype(f32)
    got_attn_a = [shift(blocks[1], Y, 1), shift(blocks[3], Y, 3)]
    got_attn_b = [x_out(blocks[4 + i], *FLIPS[i]) for i in (2, 3)]
    row_part = after(row_part, part_both)

    block_at = jnp.stack([((r // 4 - y) % 4) * 4 + ((r // 2 % 2) ^ lo) * 2 + ((r % 2) ^ hi) for r in range(16)])
    pick = (block_at[:, None] == jnp.arange(16)[None, :]).astype(f32)
    gain_parts = jnp.concatenate([gain_part.reshape(16, 128), grad_gain_two.reshape(16, 128)], 1)
    gain_parts = jnp.dot(pick, gain_parts, precision=lax.Precision.HIGHEST)
    peaks = jnp.where((jnp.arange(QUERY_HEADS) == mine)[:, None], peak, 0.0)
    small = jnp.concatenate([row_part.reshape(6, 128), gain_parts[:, :128], gain_parts[:, 128:], peaks], 0)
    is_peak = (jnp.arange(46) >= 38)[:, None]

    def join(values):
        total, most = values[0], values[0]
        for value in values[1:]:
            total, most = total + value, jnp.maximum(most, value)
        return jnp.where(is_peak[-total.shape[0] :], most, total)

    small = join([small, other_core(small)])
    small = join([small, z_other(small, 1)])

    rest = lax.optimization_barrier((blocks[2], blocks[4], blocks[5], small, *got_attn_a, *got_attn_b))
    (block_y, block_0, block_1, small), got_attn_a, got_attn_b = rest[:4], rest[4:6], rest[6:]
    got_attn_a = [blocks[0], shift(block_y, Y, 2), *got_attn_a]
    got_attn_b = [x_out(block_0, 0, 0), x_out(block_1, *FLIPS[1]), *got_attn_b]
    out_late = after(out_both, part_both)
    small = join([small, z_other(small, 2)])
    row_sum = small[:6].reshape(LEN, 1)
    small = small[6:]
    small = join([small, y_other(small, 1)])
    got_attn_a, got_attn_b, small, attn_grad = lax.optimization_barrier((got_attn_a, got_attn_b, small, attn_grad))
    ffn_own = lax.psum_scatter(out_late, Z, scatter_dimension=0, tiled=True).astype(f32)

    gain_pair = jnp.dot(pick, gain_rows[0].reshape(16, 128), precision=lax.Precision.HIGHEST)
    gain_cols = lax.dynamic_slice(gain_pair, (mine * 2, 0), (2, 128)).reshape(1, HEAD)
    grad_inputs = (
        db_cols.astype(f32) + r1 * attn_grad * gain_cols - x_own.astype(f32) * r1**2 * (row_sum / WIDTH)
    )
    home = [(h_cols.astype(f32) + ffn_own).astype(bf16), grad_inputs.astype(bf16)]
    *sum_b, kv_give, kv_keep = call(
        join_body,
        "join_sums",
        [at, *got_attn_a, *got_attn_b, block_0],
        [((128, 512), bf16)] * 4 + [((512, HEAD), bf16), ((512, HEAD), f32)],
        [pltpu.VMEM((512, 512), bf16)] * 9 + [pltpu.SemaphoreType.DMA((9,))],
        0,
        anywhere=9,
    )
    home = swap(after(jnp.concatenate(home, 0), kv_give))
    kv_sum = (kv_keep + kv_partner(kv_give).astype(f32)).astype(bf16)
    sum_b = [sum_b[0]] + [shift(sum_b[i], Y, i) for i in (1, 2, 3)]
    first_y = sum_b[1]
    small = join([small, y_other(small, 2)])
    kv_sum, home, small, *sum_b = lax.optimization_barrier((kv_sum, home, small, *sum_b))
    high = lax.reduce_precision(small, 8, 7)
    rider = jnp.concatenate([high.astype(bf16), (small - high).astype(bf16)], 1)
    rider = jnp.pad(rider, ((0, 8), (0, 0)))
    rider = jnp.broadcast_to(rider[None], (4, 48, HEAD))
    last = jnp.concatenate([kv_sum.reshape(4, 128, HEAD), rider], 1).reshape(4 * 176, HEAD)
    sum_a = [x_out(last[i * 176 : (i + 1) * 176], *flip) for i, flip in enumerate(FLIPS)]
    grads = call(
        finish_body,
        "finish",
        [at, *got_attn_a, *got_attn_b, after(block_0, first_y)],
        [((128, FF), f32)] * 3,
        [pltpu.VMEM((384, 512), bf16)] * 9 + [pltpu.SemaphoreType.DMA((9,))],
        0,
        anywhere=9,
    )
    query, output, key, value, gain_one, gain_two, clipped_query, clipped_key = call(
        last_body,
        "last",
        [at, last[:176], *sum_a, *sum_b, w_query, w_key],
        [
            ((128, HEAD), f32),
            ((128, HEAD), f32),
            ((128, 128), f32),
            ((128, 128), f32),
            ((1, 128), f32),
            ((1, 128), f32),
            ((128, HEAD), bf16),
            ((128, 128), bf16),
        ],
        [pltpu.VMEM((48, 128), f32)],
        0,
    )
    return (
        home[:LEN],
        home[LEN:].astype(f32),
        gain_one.reshape(128),
        query,
        key,
        value,
        output,
        gain_two.reshape(128),
        grads[0],
        grads[1],
        grads[2],
        clipped_query,
        clipped_key,
    )


def solution(mesh):
    torus = Mesh(mesh.devices.reshape(4, 2, 2, 2, 4), (Y, XLO, CORE, XHI, Z))
    both, rows = P(TOK, MDL), P(TOK)
    return jax.shard_map(
        on_device,
        mesh=torus,
        in_specs=(both, P(TOK, None), rows, both, both, both, both, rows, both, both, both, both),
        out_specs=(both, both, rows, both, both, both, both, rows, both, both, both, both, both),
        check_vma=False,
    )
```
